32 devices in a mesh: grp: 8 (over z, y), tp: 4 (over x, core).
Axes of the slice: x: 2, y: 2, z: 4, core: 2. Of those that a mesh axis runs over, the one named last changes fastest.
Arguments:
- tokens: bfloat16 [512, 4, 8192], P('grp', None, 'tp'), may hold values from -6 to 6
- adapter_id: int32 [512], P('grp'), may hold values from 0 to 63, as said below
- pool_slot: int32 [64], replicated, may hold values from 0 to 63, as said below
- lengths: int32 [512], P('grp'), may hold values from 1 to 64, as said below
- w_query: bfloat16 [8192, 8192], P(None, 'tp'), may hold values from -0.0625 to 0.0625
- w_key: bfloat16 [8192, 1024], P(None, 'tp'), may hold values from -0.0625 to 0.0625
- w_value: bfloat16 [8192, 1024], P(None, 'tp'), may hold values from -0.0625 to 0.0625
- pooled_down_weights: bfloat16 [64, 8192, 64], P('grp', 'tp'), may hold values from -0.0625 to 0.0625
- pool_up: bfloat16 [64, 64, 8192], P('grp', None, 'tp'), may hold values from -0.75 to 0.75
- cache_key: bfloat16 [512, 64, 1024], P('grp', None, 'tp')
- cache_value: bfloat16 [512, 64, 1024], P('grp', None, 'tp'), may hold values from -6 to 6
Outputs:
- attended: bfloat16 [512, 4, 8192], P('grp', None, 'tp')
The draws below stay inside these ranges and needn't reach their ends.
Inputs may be any that keep to these rules, and one draw needn't show every extreme that they name: `adapter_id`: each aligned block of 64 rows (one group) uses adapters of exactly 8 owners (owner = pool_slot // 8), 8 rows each, and at most 2 distinct adapters of one owner, reached in every block; a single owner, the same for all blocks, serves 8 rows of every block. `pool_slot`: A permutation. `lengths`: each aligned block of 64 rows has a row of length 64.
All inputs are finite; a program needn't handle non-finite values.
Results may differ from the reference program's by a relative error of at most 0.012.
The reference program's roundings to bfloat16 on the way count: a program that leaves them out, or rounds other values in their place, can miss the bound.
Values may be sent and summed in bfloat16 or wider, within the bound.
No kernel may reach another device: no remote copies, remote signals or barrier semaphores. Data moves between devices by JAX's collectives and lax.ppermute only.
A program may use at most 128 MiB of HBM per device.

```python
import math
import jax
import jax.numpy as jnp
from jax import lax

D = 8192
QH = 64
KVH = 8
HD = 128
R = 64
ROWS_GRP = 64
LEN = 64
ADP_GRP = 8
STEPS = 4
CAP = 8
ROWS_ALL = 512
ADAPTERS = 64
N_GRP = 8


def routing(key):
    pool_order = jax.random.permutation(jax.random.fold_in(key, 11), ADAPTERS).astype(jnp.int32)
    inverse = jnp.zeros((ADAPTERS,), jnp.int32).at[pool_order].set(jnp.arange(ADAPTERS, dtype=jnp.int32))
    hot_owner = jax.random.randint(jax.random.fold_in(key, 12), (), 0, N_GRP).astype(jnp.int32)
    count_of_blocks = ROWS_GRP // CAP

    def one_group(group_key):
        keys = jax.random.split(group_key, 5)
        others = jax.random.permutation(keys[0], N_GRP - 1).astype(jnp.int32) + 1
        shifted = jnp.concatenate([jnp.zeros((1,), jnp.int32), others])
        owners = (hot_owner + shifted) % N_GRP
        first_slot = jax.random.randint(keys[1], (count_of_blocks,), 0, ADP_GRP).astype(jnp.int32)
        second_slot = (first_slot + jax.random.randint(keys[2], (count_of_blocks,), 1, ADP_GRP).astype(jnp.int32)) % ADP_GRP
        row_rank = jnp.arange(ROWS_GRP, dtype=jnp.int32) % CAP
        row_block = jnp.arange(ROWS_GRP, dtype=jnp.int32) // CAP
        coin_flip = jax.random.randint(keys[3], (ROWS_GRP,), 0, 2).astype(jnp.int32)
        chosen = jnp.where(row_rank == 0, 0, jnp.where(row_rank == 1, 1, coin_flip))
        slot_here = jnp.where(chosen == 0, first_slot[row_block], second_slot[row_block])
        pool_pos = owners[row_block] * ADP_GRP + slot_here
        shuffle = jax.random.permutation(keys[4], ROWS_GRP)
        return inverse[pool_pos[shuffle]]
    group_keys = jax.random.split(jax.random.fold_in(key, 13), N_GRP)
    identity = jax.vmap(one_group)(group_keys).reshape(-1).astype(jnp.int32)
    return (identity, pool_order)


def draw_adapter_id(key, part):
    return routing(key)[0]


def draw_pool_slot(key, part):
    return routing(key)[1]


def draw_lengths(key, part):
    base = jax.random.randint(jax.random.fold_in(key, 21), (N_GRP, ROWS_GRP), 1, LEN + 1).astype(jnp.int32)
    longest = jax.random.randint(jax.random.fold_in(key, 22), (N_GRP,), 0, ROWS_GRP).astype(jnp.int32)
    base = jnp.where(jnp.arange(ROWS_GRP, dtype=jnp.int32)[None, :] == longest[:, None], LEN, base)
    return base.reshape(-1).astype(jnp.int32)


def draw_cache_key(key, part):
    base = jax.random.normal(jax.random.fold_in(key, 31), (ROWS_ALL, LEN, KVH * HD), jnp.float32)
    return base.astype(jnp.bfloat16)


def shard_levels(key, shape, cuts, least, high):
    factor_of = 1.0
    for axis_at, blocks in cuts:
        heights = jax.random.uniform(jax.random.fold_in(jax.random.fold_in(key, 6), axis_at), (blocks,), jnp.float32, least / len(cuts), high / len(cuts))
        factor_of = factor_of * jnp.repeat(jnp.exp(heights), shape[axis_at] // blocks).reshape((-1,) + (1,) * (len(shape) - 1 - axis_at))
    return factor_of


def bell_draw(rng, shape, deviation, reach, cuts=(), kind=jnp.bfloat16):
    entries = jax.random.normal(rng, shape, jnp.float32) * deviation
    if len(cuts) > 0:
        entries = shard_levels(rng, shape, cuts, -0.22, 0.18) * entries
    return jnp.clip(entries, min=-reach, max=reach).astype(kind)


def setup_inputs(seed: int = 0) -> dict:
    splits = jax.random.split(jax.random.key(seed), 12)
    return {
        "tokens": bell_draw(splits[0], (ROWS_ALL, STEPS, D), 1.0, 6.0, ((0, 8), (2, 4))),
        "adapter_id": draw_adapter_id(jax.random.fold_in(splits[11], 71), 0),
        "pool_slot": draw_pool_slot(jax.random.fold_in(splits[11], 71), 0),
        "lengths": draw_lengths(jax.random.fold_in(splits[11], 71), 0),
        "w_query": bell_draw(splits[4], (D, QH * HD), D ** -0.5, 0.0625, ((1, 4),)),
        "w_key": bell_draw(splits[5], (D, KVH * HD), D ** -0.5, 0.0625, ((1, 4),)),
        "w_value": bell_draw(splits[6], (D, KVH * HD), D ** -0.5, 0.0625, ((1, 4),)),
        "pooled_down_weights": bell_draw(splits[7], (ADAPTERS, D, R), D ** -0.5, 0.0625, ((0, 8), (1, 4))),
        "pool_up": bell_draw(splits[8], (ADAPTERS, R, QH * HD), R ** -0.5, 0.75, ((0, 8), (2, 4))),
        "cache_key": draw_cache_key(jax.random.fold_in(splits[11], 71), 0),
        "cache_value": bell_draw(splits[10], (ROWS_ALL, LEN, KVH * HD), 1.0, 6.0, ((0, 8), (2, 4))),
    }


rope_base = 500000.0

def rotate(values, position):
    half_width = values.shape[-1] // 2
    inv_freq = jnp.exp(jnp.arange(half_width, dtype=jnp.float32) * (-2.0 * math.log(rope_base) / values.shape[-1]))
    angles = position.astype(jnp.float32)[:, :, None, None] * inv_freq
    cosine = jnp.cos(angles)
    sines = jnp.sin(angles)
    front_half = values[..., :half_width]
    back_half = values[..., half_width:]
    return jnp.concatenate([front_half * cosine - back_half * sines, back_half * cosine + front_half * sines], axis=-1)

def attend(queries, key_new, value_new, cache_key, cache_value, lengths):
    score_scale = 1.0 / math.sqrt(queries.shape[-1])
    cached = jnp.einsum('rskgd,rlkd->rskgl', queries.astype(jnp.float32), cache_key.astype(jnp.float32)) * score_scale
    fresh_scores = jnp.einsum('rskgd,rtkd->rskgt', queries.astype(jnp.float32), key_new.astype(jnp.float32)) * score_scale
    live_mask = jnp.arange(cache_key.shape[1], dtype=jnp.int32)[None, :] < lengths[:, None]
    cached = jnp.where(live_mask[:, None, None, None, :], cached, -1e+30)
    steps_here = key_new.shape[1]
    causal = jnp.arange(steps_here, dtype=jnp.int32)[:, None] >= jnp.arange(steps_here, dtype=jnp.int32)[None, :]
    fresh_scores = jnp.where(causal[None, :, None, None, :], fresh_scores, -1e+30)
    row_max = jnp.maximum(lax.optimization_barrier(jnp.max(cached, axis=-1)), lax.optimization_barrier(jnp.max(fresh_scores, axis=-1)))
    cache_exp = jnp.exp(cached - row_max[..., None])
    fresh_exp = jnp.exp(fresh_scores - row_max[..., None])
    weight_sum = lax.optimization_barrier(jnp.sum(cache_exp, axis=-1)) + lax.optimization_barrier(jnp.sum(fresh_exp, axis=-1))
    cache_weights = lax.optimization_barrier((cache_exp / weight_sum[..., None]).astype(jnp.bfloat16))
    fresh_weights = lax.optimization_barrier((fresh_exp / weight_sum[..., None]).astype(jnp.bfloat16))
    combined = jnp.einsum('rskgl,rlkd->rskgd', cache_weights.astype(jnp.float32), cache_value.astype(jnp.float32))
    combined = combined + jnp.einsum('rskgt,rtkd->rskgd', fresh_weights.astype(jnp.float32), value_new.astype(jnp.float32))
    return combined.astype(jnp.bfloat16)

def reference(tokens, adapter_id, pool_slot, lengths, w_query, w_key, w_value, pooled_down_weights, pool_up, cache_key, cache_value):
    group_size = QH // KVH

    def group_step(packed):
        tokens_per_group, group_ids, group_lengths, group_keys, group_values = packed
        pool_pos = pool_slot[group_ids]
        down_weight_panels = pooled_down_weights[pool_pos].astype(jnp.float32)
        up_weight_panels = pool_up[pool_pos].astype(jnp.float32)
        adapter_middle = lax.optimization_barrier(jnp.einsum('kjq,kqt->kjt', tokens_per_group.astype(jnp.float32), down_weight_panels).astype(jnp.bfloat16))
        adapter_output = lax.optimization_barrier(jnp.einsum('jzy,jya->jza', adapter_middle.astype(jnp.float32), up_weight_panels).astype(jnp.bfloat16))
        token_rows = tokens_per_group.reshape(ROWS_GRP * STEPS, D)
        base_query_rows = jnp.dot(token_rows, w_query, preferred_element_type=jnp.float32).reshape(ROWS_GRP, STEPS, QH * HD)
        base_query_rows = base_query_rows + adapter_output.astype(jnp.float32)
        key_base = jnp.dot(token_rows, w_key, preferred_element_type=jnp.float32)
        value_base = jnp.dot(token_rows, w_value, preferred_element_type=jnp.float32)
        position = group_lengths[:, None] + jnp.arange(STEPS, dtype=jnp.int32)[None, :]
        queries = rotate(base_query_rows.reshape(ROWS_GRP, STEPS, QH, HD), position)
        queries = lax.optimization_barrier(queries.astype(jnp.bfloat16)).reshape(ROWS_GRP, STEPS, KVH, group_size, HD)
        key_new = lax.optimization_barrier(rotate(key_base.reshape(ROWS_GRP, STEPS, KVH, HD), position).astype(jnp.bfloat16))
        value_new = lax.optimization_barrier(value_base.reshape(ROWS_GRP, STEPS, KVH, HD).astype(jnp.bfloat16))
        combined = attend(queries, key_new, value_new, group_keys, group_values, group_lengths)
        return combined.reshape(ROWS_GRP, STEPS, QH * HD)
    packed = (tokens.reshape(N_GRP, ROWS_GRP, STEPS, D), adapter_id.reshape(N_GRP, ROWS_GRP), lengths.reshape(N_GRP, ROWS_GRP), cache_key.reshape(N_GRP, ROWS_GRP, LEN, KVH, HD), cache_value.reshape(N_GRP, ROWS_GRP, LEN, KVH, HD))
    return lax.map(group_step, packed).reshape(ROWS_ALL, STEPS, QH * HD)
```

```python
import functools
import math

import jax
import jax.numpy as jnp
from jax import lax
from jax.experimental import pallas as pl
from jax.experimental.pallas import tpu as pltpu
from jax.sharding import PartitionSpec as P

HD = 128
CAP = 8
ROPE_BASE = 500000.0
NEG = -1e30
VMEM_LIMIT = 56 * 1024 * 1024
F32 = jnp.float32
BF16 = jnp.bfloat16


def params(**kw):
    return pltpu.CompilerParams(vmem_limit_bytes=VMEM_LIMIT, **kw)


VM = pl.BlockSpec(memory_space=pltpu.VMEM)
SM = pl.BlockSpec(memory_space=pltpu.SMEM)
ANY = pl.BlockSpec(memory_space=pl.ANY)


def dot(a, b):
    return jnp.dot(a, b, preferred_element_type=F32)


def dot_t(a, b):
    return lax.dot_general(a, b, (((1,), (1,)), ((), ())), preferred_element_type=F32)


def pack_kernel(adp_rows, n_grp, steps, ids_ref, lens_ref, slots_ref, tok_ref, *outs):
    sends = outs[:n_grp]
    sorted_ref, len_ref, row_ref = outs[n_grp : n_grp + 3]
    rows = ids_ref.shape[1]
    pool = slots_ref.shape[1]
    width = sorted_ref.shape[1]
    me = lax.axis_index("grp")
    sub = lax.broadcasted_iota(jnp.int32, (rows, rows), 0)
    lane = lax.broadcasted_iota(jnp.int32, (rows, rows), 1)
    eye = sub == lane

    def to_col(row):
        return jnp.sum(jnp.where(eye, row, 0.0), axis=1, keepdims=True)

    def to_row(col):
        return jnp.sum(jnp.where(eye, col, 0.0), axis=0, keepdims=True)

    ids_col = to_col(ids_ref[...].astype(F32))
    lens_col = to_col(lens_ref[...].astype(F32))
    span = lax.broadcasted_iota(jnp.int32, (rows, pool), 1).astype(F32)
    pos = jnp.sum(jnp.where(ids_col == span, slots_ref[...].astype(F32), 0.0), axis=1, keepdims=True)
    pos = pos.astype(jnp.int32)
    owner = lax.div(pos, adp_rows)
    slot = (pos - owner * adp_rows).astype(F32)
    key_col = lax.bitwise_xor(owner, me).astype(F32)
    key_row = to_row(key_col)
    same = key_row == key_col
    ahead = jnp.where((key_row < key_col) | (same & (lane < sub)), 1.0, 0.0)
    rank = jnp.sum(jnp.where(same & (lane < sub), 1.0, 0.0), axis=1, keepdims=True)
    dest_row = to_row(jnp.sum(ahead, axis=1, keepdims=True))
    perm = jnp.where(sub.astype(F32) == dest_row, 1.0, 0.0).astype(BF16)

    def wide(col):
        return jnp.broadcast_to(col, (rows, 128)).astype(BF16)

    len_ref[...] = dot(perm, wide(lens_col))
    row_ref[...] = dot(perm, wide(sub[:, :1].astype(F32))).astype(jnp.int32)
    dense = n_grp * CAP == rows
    if dense:
        perm_send = perm
    else:
        slot_row = to_row(key_col * CAP + rank)
        sub_s = lax.broadcasted_iota(jnp.int32, (n_grp * CAP, rows), 0).astype(F32)
        perm_send = jnp.where(sub_s == slot_row, 1.0, 0.0).astype(BF16)
    slot_s = dot(perm_send, wide(slot))
    for k in range(n_grp):
        tile = slot_s[k * CAP : (k + 1) * CAP]
        sends[k][steps * CAP * (width // 128) :, :] = jnp.concatenate([tile, tile], axis=0).astype(BF16)
    for j in range(0, width, 512):
        w = min(512, width - j)
        got = [dot(perm, tok_ref[s, :, j : j + w]) for s in range(steps)]
        for b in range(rows // CAP):
            blk = jnp.concatenate([t[b * CAP : (b + 1) * CAP] for t in got], axis=0).astype(BF16)
            sorted_ref[b * steps * CAP : (b + 1) * steps * CAP, j : j + w] = blk
        if not dense:
            got = [dot(perm_send, tok_ref[s, :, j : j + w]) for s in range(steps)]
        for k in range(n_grp):
            blk = jnp.concatenate([t[k * CAP : (k + 1) * CAP] for t in got], axis=0).astype(BF16)
            for c in range(w // 128):
                at = (j // 128 + c) * steps * CAP
                sends[k][at : at + steps * CAP, :] = blk[:, c * 128 : (c + 1) * 128]


def pack(n_grp, adp_rows, adapter_id, lengths, pool_slot, tok):
    steps, rows, width = tok.shape
    n_tok = steps * CAP
    out = (
        [jax.ShapeDtypeStruct((n_tok * (width // 128) + 16, 128), BF16)] * n_grp
        + [jax.ShapeDtypeStruct((rows * steps, width), BF16)]
        + [jax.ShapeDtypeStruct((rows, 128), F32), jax.ShapeDtypeStruct((rows, 128), jnp.int32)]
    )
    got = pl.pallas_call(
        functools.partial(pack_kernel, adp_rows, n_grp, steps),
        out_shape=out,
        in_specs=[VM] * 4,
        out_specs=[VM] * len(out),
        compiler_params=params(),
        name="pack",
    )(adapter_id[None, :], lengths[None, :], pool_slot[None, :], tok)
    return got[:n_grp], got[n_grp], got[n_grp + 1], got[n_grp + 2]


def qkv_kernel(n_x, has_acc, kblk, ids_ref, *refs):
    xs = refs[:n_x]
    w_refs = refs[n_x : n_x + 3]
    acc_refs = refs[n_x + 3 : n_x + 6] if has_acc else None
    outs = refs[-3:]
    p, kb = pl.program_id(0), pl.program_id(1)

    @pl.when((p == 0) & (kb == 0))
    def _():
        for i in range(3):
            outs[i][...] = acc_refs[i][...] if has_acc else jnp.zeros_like(outs[i])

    for j in range(n_x):

        @pl.when(p == j)
        def _():
            x = xs[j][:, pl.ds(pl.multiple_of(kb * kblk, kblk), kblk)]
            for w, o in zip(w_refs, outs):
                o[...] += dot(x, w[...])


def qkv(xs, shards, weights, acc):
    m, width = xs[0].shape
    kblk = min(512, width)
    nk = width // kblk
    n_x = len(xs)
    has_acc = acc is not None

    def whole(a):
        return pl.BlockSpec(a.shape, lambda p, kb, ids: (0,) * len(a.shape))

    def wspec(w):
        return pl.BlockSpec((kblk, w.shape[1]), lambda p, kb, ids: (ids[p] * nk + kb, 0))

    outs = [jax.ShapeDtypeStruct((m, w.shape[1]), F32) for w in weights]
    cols = sum(w.shape[1] for w in weights)
    extra = list(acc) if has_acc else []
    return pl.pallas_call(
        functools.partial(qkv_kernel, n_x, has_acc, kblk),
        out_shape=outs,
        grid_spec=pltpu.PrefetchScalarGridSpec(
            num_scalar_prefetch=1,
            grid=(n_x, nk),
            in_specs=[whole(x) for x in xs] + [wspec(w) for w in weights] + [whole(a) for a in extra],
            out_specs=[whole(o) for o in outs],
        ),
        compiler_params=params(),
        cost_estimate=pl.CostEstimate(
            flops=2 * n_x * m * width * cols, bytes_accessed=2 * n_x * width * cols, transcendentals=0
        ),
        name="qkv",
    )(shards, *xs, *weights, *extra)


def slot_mask(tile, n_tok, cols, rank):
    slots = jnp.concatenate([tile[:CAP].astype(F32)] * (n_tok // CAP), axis=0)
    slots = jnp.concatenate([slots] * (cols // 128), axis=1)
    col = lax.div(lax.broadcasted_iota(jnp.int32, (n_tok, cols), 1), rank).astype(F32)
    return slots == col


def mid_kernel(n_tok, rank, down_ref, *refs):
    ins, out_ref, x_ref = refs[:-2], refs[-2], refs[-1]
    width = x_ref.shape[1]
    cols = down_ref.shape[1]
    for k, r in enumerate(ins):
        for c in range(width // 128):
            x_ref[k * n_tok : (k + 1) * n_tok, c * 128 : (c + 1) * 128] = r[c * n_tok : (c + 1) * n_tok, :]
    half = len(ins) // 2
    prod = dot(x_ref[...], down_ref[...])
    lane = lax.broadcasted_iota(jnp.int32, (n_tok, 128), 1)
    folded = []
    for k, r in enumerate(ins):
        mask = slot_mask(r[n_tok * (width // 128) :, :], n_tok, cols, rank)
        part = jnp.where(mask, prod[k * n_tok : (k + 1) * n_tok], 0.0)
        tot = part[:, :128]
        for c in range(128, cols, 128):
            tot = tot + part[:, c : c + 128]
        folded.append(tot + pltpu.roll(tot, 64, 1))
    for k in range(half):
        out_ref[k * n_tok : (k + 1) * n_tok, :] = jnp.where(lane < 64, folded[k], folded[k + half])


def mid(recv, down, n_tok, rank):
    width = down.shape[0]
    n = len(recv)
    return pl.pallas_call(
        functools.partial(mid_kernel, n_tok, rank),
        out_shape=jax.ShapeDtypeStruct((n * n_tok // 2, 128), F32),
        in_specs=[VM] * (n + 1),
        out_specs=VM,
        scratch_shapes=[pltpu.VMEM((n * n_tok, width), BF16)],
        compiler_params=params(),
        name="mid",
    )(down, *recv)


def up_kernel(n_tok, rank, n_recv, up_ref, a_ref, b_ref, *refs):
    ins, outs = refs[:n_recv], refs[n_recv:]
    cols = up_ref.shape[0]
    half = n_recv // 2
    total = (a_ref[...] + b_ref[...]).astype(BF16).astype(F32)
    lane = lax.broadcasted_iota(jnp.int32, (n_tok, 128), 1)
    spread = []
    for k in range(n_recv):
        at = (k % half) * n_tok
        mine = total[at : at + n_tok]
        other = pltpu.roll(mine, 64, 1)
        both = jnp.where((lane < 64) == (k < half), mine, other)
        both = jnp.concatenate([both] * (cols // 128), axis=1)
        mask = slot_mask(ins[k][ins[k].shape[0] - 16 :, :], n_tok, cols, rank)
        spread.append(jnp.where(mask, both, 0.0).astype(BF16))
    rows = jnp.concatenate(spread, axis=0)
    for j in range(0, up_ref.shape[1], 512):
        got = dot(rows, up_ref[:, j : j + 512]).astype(BF16)
        for k in range(n_recv):
            outs[k][:, j : j + 512] = got[k * n_tok : (k + 1) * n_tok]


def up(a, b, recv, up_rows, n_tok, rank):
    n = len(recv)
    return pl.pallas_call(
        functools.partial(up_kernel, n_tok, rank, n),
        out_shape=[jax.ShapeDtypeStruct((n_tok, up_rows.shape[1]), BF16)] * n,
        in_specs=[VM] * (n + 3),
        out_specs=[VM] * n,
        compiler_params=params(),
        name="up",
    )(up_rows, a, b, *recv)


def make_attn_kernel(first, nb, steps, group, has_prev):
    def kernel(*refs):
        rows_ref, q_ref, k_ref, v_ref, cos_ref, sin_ref, len_ref, ck_ref, cv_ref = refs[:9]
        loras = refs[9 : 9 + nb]
        at = 9 + nb + (1 if has_prev else 0)
        out_ref, kbuf, vbuf, obuf, ksem, vsem, osem = refs[at:]
        n_tok = steps * CAP
        kv_local = k_ref.shape[1] // HD
        span = ck_ref.shape[1]
        scale = 1.0 / math.sqrt(HD)

        def copies(b, i):
            r = rows_ref[(first + b) * CAP + i, 0]
            return (
                pltpu.make_async_copy(ck_ref.at[r], kbuf.at[b, i], ksem.at[b]),
                pltpu.make_async_copy(cv_ref.at[r], vbuf.at[b, i], vsem.at[b]),
            )

        for b in range(nb):
            for i in range(CAP):
                for c in copies(b, i):
                    c.start()

        n_q = group * n_tok
        tok_q = lax.broadcasted_iota(jnp.int32, (n_tok, n_tok), 0)
        tok_k = lax.broadcasted_iota(jnp.int32, (n_tok, n_tok), 1)
        new_ok = (lax.rem(tok_q, CAP) == lax.rem(tok_k, CAP)) & (lax.div(tok_q, CAP) >= lax.div(tok_k, CAP))
        new_ok = jnp.concatenate([new_ok.astype(F32)] * group, axis=0) > 0.5
        col = lax.broadcasted_iota(jnp.int32, (CAP, CAP * span), 1)
        sub = lax.broadcasted_iota(jnp.int32, (CAP, CAP * span), 0)
        own = lax.div(col, span) == sub
        at_pos = lax.rem(col, span).astype(F32)
        turn = (
            (lax.rem(tok_q, steps) * CAP + lax.div(tok_q, steps)) == tok_k
        ).astype(F32).astype(BF16)

        for b in range(nb):
            for i in range(CAP):
                for c in copies(b, i):
                    c.wait()
            rows = slice(b * n_tok, (b + 1) * n_tok)
            cos, sin = cos_ref[rows], sin_ref[rows]
            lens = len_ref[b * CAP : (b + 1) * CAP][:, :1]
            ok = own & (at_pos < lens)
            bias = jnp.where(ok, 0.0, NEG)
            bias = jnp.concatenate([bias] * (n_q // CAP), axis=0)

            def rope(v):
                return v * cos + pltpu.roll(v, HD // 2, 1) * sin

            for h in range(kv_local):
                hs = slice(h * HD, (h + 1) * HD)
                heads = []
                for g in range(group):
                    cs = slice((h * group + g) * HD, (h * group + g + 1) * HD)
                    heads.append(rope(q_ref[rows, cs] + loras[b][:, cs].astype(F32)))
                q = jnp.concatenate(heads, axis=0).astype(BF16)
                kn = rope(k_ref[rows, hs]).astype(BF16)
                vn = v_ref[rows, hs].astype(BF16)
                kc = kbuf[b, :, :, hs].reshape(CAP * span, HD)
                vc = vbuf[b, :, :, hs].reshape(CAP * span, HD)
                s1 = dot_t(q, kc) * scale + bias
                s2 = jnp.where(new_ok, dot_t(q, kn) * scale, NEG)
                top = jnp.maximum(jnp.max(s1, axis=1, keepdims=True), jnp.max(s2, axis=1, keepdims=True))
                e1 = jnp.exp(s1 - top)
                e2 = jnp.exp(s2 - top)
                den = jnp.sum(e1, axis=1, keepdims=True) + jnp.sum(e2, axis=1, keepdims=True)
                inv = 1.0 / den
                o = dot((e1 * inv).astype(BF16), vc) + dot((e2 * inv).astype(BF16), vn)
                o = o.astype(BF16)
                for g in range(group):
                    cs = slice((h * group + g) * HD, (h * group + g + 1) * HD)
                    mixed = dot(turn, o[g * n_tok : (g + 1) * n_tok])
                    for i in range(CAP):
                        obuf[b, i, :, cs] = mixed[i * steps : (i + 1) * steps].astype(BF16)
            for i in range(CAP):
                r = rows_ref[(first + b) * CAP + i, 0]
                pltpu.make_async_copy(obuf.at[b, i], out_ref.at[r], osem).start()
        for b in range(nb):
            for i in range(CAP):
                r = rows_ref[(first + b) * CAP + i, 0]
                pltpu.make_async_copy(obuf.at[b, i], out_ref.at[r], osem).wait()

    return kernel


def attention(first, nb, steps, rows, q, k, v, cos, sin, lens, ck, cv, loras, prev):
    n_tok = steps * CAP
    group = q.shape[1] // k.shape[1]
    n_rows = ck.shape[0]
    out = jax.ShapeDtypeStruct((n_rows, steps, q.shape[1]), BF16)
    at = first // nb

    def part(a, n):
        return pl.BlockSpec((n, a.shape[1]), lambda i: (at, 0))

    ins = [rows, q, k, v, cos, sin, lens, ck, cv, *loras]
    specs = [SM] + [part(a, nb * n_tok) for a in (q, k, v, cos, sin)] + [part(lens, nb * CAP), ANY, ANY]
    specs += [VM] * nb
    alias = {}
    if prev is not None:
        alias = {len(ins): 0}
        ins.append(prev)
        specs.append(ANY)
    buf = (nb, CAP) + ck.shape[1:]
    return pl.pallas_call(
        make_attn_kernel(first, nb, steps, group, prev is not None),
        out_shape=out,
        grid=(1,),
        in_specs=specs,
        out_specs=ANY,
        scratch_shapes=[
            pltpu.VMEM(buf, BF16),
            pltpu.VMEM(buf, BF16),
            pltpu.VMEM((nb, CAP, steps, q.shape[1]), BF16),
            pltpu.SemaphoreType.DMA((nb,)),
            pltpu.SemaphoreType.DMA((nb,)),
            pltpu.SemaphoreType.DMA,
        ],
        input_output_aliases=alias,
        compiler_params=params(),
        name="attn",
    )(*ins)


def swap(x, axis, n, bit):
    return lax.ppermute(x, axis, [(i, i ^ bit) for i in range(n)])


def body(
    tokens,
    adapter_id,
    pool_slot,
    lengths,
    w_query,
    w_key,
    w_value,
    pooled_down_weights,
    pool_up,
    cache_key,
    cache_value,
):
    n_grp = lax.axis_size("grp")
    n_tp = lax.axis_size("tp")
    row_count, steps, width = tokens.shape
    adp_rows, _, rank = pooled_down_weights.shape
    n_tok = steps * CAP
    n_blocks = row_count // CAP

    tok = jnp.transpose(tokens, (1, 0, 2))
    sends, mine, lens, rows = pack(n_grp, adp_rows, adapter_id, lengths, pool_slot, tok)

    recv = [sends[0]] + [swap(sends[k], "grp", n_grp, k) for k in range(1, n_grp)]

    pieces = {0: mine}
    bit = n_tp // 2
    while bit:
        pieces.update({off ^ bit: swap(p, "tp", n_tp, bit) for off, p in list(pieces.items())})
        bit //= 2
    me = lax.axis_index("tp")
    weights = (w_query, w_key, w_value)
    early = [o for o in pieces if o < 2]
    late = [o for o in pieces if o >= 2]

    def shards(offs):
        return jnp.stack([lax.bitwise_xor(me, o) for o in offs]).astype(jnp.int32)

    acc = qkv([pieces[o] for o in early], shards(early), weights, None)
    q, k, v = qkv([pieces[o] for o in late], shards(late), weights, acc)

    half = HD // 2
    inv_freq = jnp.exp(jnp.arange(half, dtype=F32) * (-2.0 * math.log(ROPE_BASE) / HD))
    inv_freq = jnp.concatenate([inv_freq, inv_freq])
    position = lens.reshape(n_blocks, 1, CAP, 128) + jnp.arange(steps, dtype=F32)[None, :, None, None]
    angles = (position * inv_freq).reshape(row_count * steps, HD)
    sign = jnp.where(jnp.arange(HD) < half, -1.0, 1.0).astype(F32)
    cos, sin = jnp.cos(angles), jnp.sin(angles) * sign

    down = jnp.transpose(pooled_down_weights, (1, 0, 2)).reshape(width, adp_rows * rank)
    part = mid(recv, down, n_tok, rank)
    bit = 1
    while bit < n_tp // 2:
        part = part + swap(part, "tp", n_tp, bit)
        bit *= 2
    other = swap(part, "tp", n_tp, bit)
    up_rows = pool_up.reshape(adp_rows * rank, pool_up.shape[2])
    back = up(part, other, recv, up_rows, n_tok, rank)
    loras = [back[0]] + [swap(back[k], "grp", n_grp, k) for k in range(1, n_grp)]
    rows = rows[:, :1]
    if n_grp != n_blocks:
        group = lax.axis_index("grp")
        span = jnp.arange(pool_slot.shape[0], dtype=jnp.int32)
        pos = jnp.sum(jnp.where(adapter_id[:, None] == span[None, :], pool_slot[None, :], 0), axis=1)
        keys = lax.bitwise_xor(lax.div(pos, adp_rows), group)
        used = jnp.any(keys[:, None] == jnp.arange(n_grp)[None, :], axis=0)
        at = jnp.cumsum(used.astype(jnp.int32)) - 1
        pick = (at[None, :] == jnp.arange(n_blocks)[:, None]) & used[None, :]
        chosen = jnp.sum(jnp.where(pick, jnp.arange(n_grp)[None, :], 0), axis=1)
        stacked = jnp.stack(loras)
        loras = [stacked[chosen[b]] for b in range(n_blocks)]
    out = None
    chunk = n_blocks // 2
    for first in range(0, n_blocks, chunk):
        out = attention(
            first, chunk, steps, rows, q, k, v, cos, sin, lens, cache_key, cache_value, loras[first : first + chunk], out
        )
    return out


def solution(mesh):
    in_specs = (
        P("grp", None, "tp"),
        P("grp"),
        P(),
        P("grp"),
        P(None, "tp"),
        P(None, "tp"),
        P(None, "tp"),
        P("grp", "tp", None),
        P("grp", None, "tp"),
        P("grp", None, "tp"),
        P("grp", None, "tp"),
    )
    out_specs = P("grp", None, "tp")
    return jax.shard_map(body, mesh=mesh, in_specs=in_specs, out_specs=out_specs, check_vma=False)
```

```python
import functools
import math

import jax
import jax.numpy as jnp
from jax import lax
from jax.experimental import pallas as pl
from jax.experimental.pallas import tpu as pltpu
from jax.sharding import PartitionSpec as P

HD = 128
CAP = 8
SUB = 4
ROPE_BASE = 500000.0
NEG = -1e30
MIB = 1024 * 1024
F32 = jnp.float32
BF16 = jnp.bfloat16
I32 = jnp.int32
N_CHUNKS = 1

VM = pl.BlockSpec(memory_space=pltpu.VMEM)
SM = pl.BlockSpec(memory_space=pltpu.SMEM)
HBM = pl.BlockSpec(memory_space=pltpu.HBM)


def params(mib):
    return pltpu.CompilerParams(vmem_limit_bytes=mib * MIB)


def dot(a, b):
    return jnp.dot(a, b, preferred_element_type=F32)


def dot_t(a, b):
    return lax.dot_general(a, b, (((1,), (1,)), ((), ())), preferred_element_type=F32)


def iota(shape, dim):
    return lax.broadcasted_iota(I32, shape, dim)


def one_hot(cond):
    return jnp.where(cond, 1.0, 0.0).astype(BF16)


def token_place(p, steps):
    n_sub = SUB * steps
    half = lax.rem(lax.div(p, n_sub), CAP // SUB)
    return half * SUB + lax.rem(p, SUB), lax.rem(lax.div(p, SUB), steps)


def route_kernel(adp_rows, seq, steps, ids_ref, lens_ref, slots_ref, *outs):
    perm_ref, send_ref, slot_ref, len_ref, row_ref = outs
    rows = ids_ref.shape[1]
    pool = slots_ref.shape[1]
    toks = rows * steps
    me = lax.axis_index("grp")
    core = lax.rem(lax.axis_index("tp"), 2)
    sub, lane = iota((rows, rows), 0), iota((rows, rows), 1)
    eye = sub == lane

    def to_col(row):
        return jnp.sum(jnp.where(eye, row, 0.0), axis=1, keepdims=True)

    def to_row(col):
        return jnp.sum(jnp.where(eye, col, 0.0), axis=0, keepdims=True)

    ids_col = to_col(ids_ref[...].astype(F32))
    lens_col = to_col(lens_ref[...].astype(F32))
    span = iota((rows, pool), 1).astype(F32)
    pos = jnp.sum(jnp.where(ids_col == span, slots_ref[...].astype(F32), 0.0), axis=1, keepdims=True)
    pos = pos.astype(I32)
    owner = lax.div(pos, adp_rows)
    slot = (pos - owner * adp_rows).astype(F32)
    key = lax.bitwise_xor(owner, me)
    pair = lax.div(key, 2)
    place = jnp.zeros_like(pair)
    for at, j in enumerate(seq):
        place = jnp.where(pair == j, at, place)
    place = (place * 2 + lax.rem(key, 2)).astype(F32)
    key = key.astype(F32)
    place_row = to_row(place)
    same = place_row == place
    before = same & (lane < sub)
    rank = jnp.sum(jnp.where(before, 1.0, 0.0), axis=1, keepdims=True)
    dest = jnp.sum(jnp.where((place_row < place) | before, 1.0, 0.0), axis=1, keepdims=True)
    dest_row, key_row, rank_row = to_row(dest), to_row(key), to_row(rank)

    def wide(col):
        return jnp.broadcast_to(col, (rows, 128)).astype(BF16)

    row_perm = one_hot(sub.astype(F32) == dest_row)
    row_ref[...] = dot(row_perm, wide(sub[:, :1].astype(F32))).astype(I32)
    row_of, _ = token_place(iota((toks, rows), 0), steps)
    row_of = (row_of + lax.div(iota((toks, rows), 0), CAP * steps) * CAP).astype(F32)
    len_ref[...] = dot(one_hot(row_of == dest_row), wide(lens_col))
    n_pairs = len(seq)
    y = iota((n_pairs * 2 * CAP, rows), 0)
    y_key = (lax.div(y, 2 * CAP) * 2 + core).astype(F32)
    y_rank = (lax.rem(lax.div(y, CAP), 2) * SUB + lax.rem(y, SUB)).astype(F32)
    slot_ref[...] = dot(one_hot((y_key == key_row) & (y_rank == rank_row)), wide(slot)).astype(BF16)

    spread = one_hot(lax.div(iota((rows, toks), 1), steps) == iota((rows, toks), 0))
    info = jnp.concatenate([dest_row, key_row, rank_row] + [dest_row] * 5, axis=0).astype(BF16)
    info = dot(info, spread)
    dest_tok, key_tok, rank_tok = info[0:1], info[1:2], info[2:3]
    p, step_tok = iota((toks, toks), 0), lax.rem(iota((toks, toks), 1), steps)
    p_row, p_step = token_place(p, steps)
    p_row = (p_row + lax.div(p, CAP * steps) * CAP).astype(F32)
    perm = one_hot((p_row == dest_tok) & (p_step == step_tok))
    perm_ref[...] = perm
    n_send = n_pairs * CAP * steps
    p, step_tok = iota((n_send, toks), 0), lax.rem(iota((n_send, toks), 1), steps)
    p_row, p_step = token_place(p, steps)
    p_key = (lax.div(p, CAP * steps) * 2 + core).astype(F32)
    send_ref[...] = one_hot((p_key == key_tok) & (p_row.astype(F32) == rank_tok) & (p_step == step_tok))


def route(adp_rows, seq, steps, adapter_id, lengths, pool_slot):
    rows = adapter_id.shape[0]
    toks = rows * steps
    out = [
        jax.ShapeDtypeStruct((toks, toks), BF16),
        jax.ShapeDtypeStruct((len(seq) * CAP * steps, toks), BF16),
        jax.ShapeDtypeStruct((len(seq) * 2 * CAP, 128), BF16),
        jax.ShapeDtypeStruct((toks, 128), F32),
        jax.ShapeDtypeStruct((rows, 128), I32),
    ]
    return pl.pallas_call(
        functools.partial(route_kernel, adp_rows, seq, steps),
        out_shape=out,
        in_specs=[VM] * 3,
        out_specs=[VM] * len(out),
        compiler_params=params(8),
        name="route",
    )(adapter_id[None, :], lengths[None, :], pool_slot[None, :])


def pack_kernel(n_tok, send_ref, slot_ref, tok_ref, oth_ref, *sends):
    rows, steps, width = tok_ref.shape
    for j in range(0, width, 512):
        for half, ref in enumerate((tok_ref, oth_ref)):
            part = ref[:, :, j : j + 512].reshape(rows * steps, 512)
            got = dot(send_ref[...], part).astype(BF16)
            for k, out in enumerate(sends):
                for c in range(4):
                    at = ((j // 128 + c) * 2 + half) * n_tok
                    out[at : at + n_tok, :] = got[k * n_tok : (k + 1) * n_tok, c * 128 : (c + 1) * 128]
    for k, out in enumerate(sends):
        out[width // 128 * 2 * n_tok :, :] = slot_ref[k * 2 * CAP : (k + 1) * 2 * CAP, :]


def pack(n_pairs, send, slot, tokens, other):
    _, steps, width = tokens.shape
    n_tok = steps * CAP
    out = [jax.ShapeDtypeStruct((width // 128 * 2 * n_tok + 2 * CAP, 128), BF16)] * n_pairs
    return pl.pallas_call(
        functools.partial(pack_kernel, n_tok),
        out_shape=out,
        in_specs=[VM] * 4,
        out_specs=[VM] * len(out),
        compiler_params=params(16),
        name="pack",
    )(send, slot, tokens, other)


def qkv_kernel(n_x, has_acc, chunk, ids_ref, perm_ref, *refs):
    xs, ws = refs[:n_x], refs[n_x : n_x + 3]
    at = n_x + 3
    accs = refs[at : at + 3] if has_acc else (None,) * 3
    at += 3 if has_acc else 0
    outs, raw, xbuf = refs[at : at + 3], refs[at + 3], refs[at + 4]
    bufs, xsem, wsem = refs[at + 5 : at + 8], refs[at + 8], refs[at + 9]
    rows, n_steps, width = xs[0].shape
    per = width // chunk
    n_chunks = n_x * per

    def x_copy(p):
        return pltpu.make_async_copy(xs[p], raw.at[p], xsem.at[p])

    def w_copy(c, i):
        row = pl.multiple_of(ids_ref[c // per] * width + (c % per) * chunk, chunk)
        return pltpu.make_async_copy(
            ws[i].at[pl.ds(row, chunk)], bufs[i].at[c * chunk : (c + 1) * chunk], wsem.at[c, i]
        )

    def begin(c):
        if c < n_chunks:
            if c % per == 0:
                x_copy(c // per).start()
            for i in range(3):
                w_copy(c, i).start()

    ahead = 4
    for c in range(ahead):
        begin(c)
    steps = [(0, 1), (1, 2)] + [(c, min(c + 2, n_chunks)) for c in range(2, n_chunks, 2)]
    for lo, hi in steps:
        for c in range(lo, hi):
            p = c // per
            if c % per == 0:
                x_copy(p).wait()
                for j in range(0, width, chunk):
                    part = raw[p, :, :, j : j + chunk].reshape(rows * n_steps, chunk)
                    xbuf[:, p * width + j : p * width + j + chunk] = dot(perm_ref[...], part).astype(BF16)
            for i in range(3):
                w_copy(c, i).wait()
            begin(c + ahead)
        x = xbuf[:, lo * chunk : hi * chunk]
        for i in range(3):
            got = dot(x, bufs[i][lo * chunk : hi * chunk, :])
            if lo:
                outs[i][...] += got
            else:
                outs[i][...] = accs[i][...] + got if has_acc else got


def qkv(xs, perm, shards, weights, acc):
    rows, steps, width = xs[0].shape
    m = rows * steps
    chunk = min(512, width)
    n_x = len(xs)
    has_acc = acc is not None
    outs = [jax.ShapeDtypeStruct((m, w.shape[1]), F32) for w in weights]
    cols = sum(w.shape[1] for w in weights)
    extra = list(acc) if has_acc else []
    depth = n_x * width
    return pl.pallas_call(
        functools.partial(qkv_kernel, n_x, has_acc, chunk),
        out_shape=outs,
        in_specs=[SM, VM] + [HBM] * (n_x + 3) + [VM] * len(extra),
        out_specs=[VM] * 3,
        scratch_shapes=[pltpu.VMEM((n_x, rows, steps, width), BF16), pltpu.VMEM((m, depth), BF16)]
        + [pltpu.VMEM((depth, w.shape[1]), BF16) for w in weights]
        + [pltpu.SemaphoreType.DMA((n_x,)), pltpu.SemaphoreType.DMA((depth // chunk, 3))],
        compiler_params=params(62),
        cost_estimate=pl.CostEstimate(
            flops=2 * m * depth * cols, bytes_accessed=2 * depth * cols, transcendentals=0
        ),
        name="qkv",
    )(shards, perm, *xs, *weights, *extra)


def slot_mask(tiles, n_tok, cols, rank):
    tiles = tiles.astype(F32)
    rep = n_tok // (2 * CAP)
    slots = jnp.concatenate([tiles[:CAP]] * rep + [tiles[CAP:]] * rep, axis=0)
    slots = jnp.concatenate([slots] * (cols // 128), axis=1)
    return slots == lax.div(iota((n_tok, cols), 1), rank).astype(F32)


def mid_kernel(n_tok, rank, down_ref, oth_ref, *refs):
    ins, out_ref, x_ref, d_ref, sem = refs[:-4], refs[-4], refs[-3], refs[-2], refs[-1]
    loads = [pltpu.make_async_copy(r, d_ref.at[i], sem.at[i]) for i, r in enumerate((down_ref, oth_ref))]
    for c in loads:
        c.start()
    _, cols, width = d_ref.shape
    for k, r in enumerate(ins):
        rows = slice(k * n_tok, (k + 1) * n_tok)
        for c in range(width // 128):
            for half in range(2):
                at = (c * 2 + half) * n_tok
                x_ref[half, rows, c * 128 : (c + 1) * 128] = r[at : at + n_tok, :]
    prod = 0.0
    for half in range(2):
        loads[half].wait()
        prod = prod + dot_t(x_ref[half], d_ref[half])
    for k, r in enumerate(ins):
        mask = slot_mask(r[r.shape[0] - 2 * CAP :, :], n_tok, cols, rank)
        part = jnp.where(mask, prod[k * n_tok : (k + 1) * n_tok], 0.0)
        tot = part[:, :128]
        for c in range(128, cols, 128):
            tot = tot + part[:, c : c + 128]
        out_ref[k * n_tok : (k + 1) * n_tok, :] = tot + pltpu.roll(tot, rank, 1)


def mid(recv, down, other, n_tok, rank):
    n = len(recv)
    cols, width = down.shape
    return pl.pallas_call(
        functools.partial(mid_kernel, n_tok, rank),
        out_shape=jax.ShapeDtypeStruct((n * n_tok, 128), F32),
        in_specs=[HBM] * 2 + [VM] * n,
        out_specs=VM,
        scratch_shapes=[
            pltpu.VMEM((2, n * n_tok, width), BF16),
            pltpu.VMEM((2, cols, width), BF16),
            pltpu.SemaphoreType.DMA((2,)),
        ],
        compiler_params=params(24),
        cost_estimate=pl.CostEstimate(
            flops=4 * n * n_tok * width * cols, bytes_accessed=4 * width * cols, transcendentals=0
        ),
        name="mid",
    )(down, other, *recv)


def up_kernel(n_tok, rank, n_recv, up_ref, oth_ref, a_ref, b_ref, *refs):
    ins, outs, u_ref, sem = refs[:n_recv], refs[n_recv : 2 * n_recv], refs[-2], refs[-1]
    loads = [pltpu.make_async_copy(r, u_ref.at[i], sem.at[i]) for i, r in enumerate((up_ref, oth_ref))]
    for c in loads:
        c.start()
    _, cols, width = u_ref.shape
    total = (a_ref[...] + b_ref[...]).astype(BF16).astype(F32)
    spread = []
    for k in range(n_recv):
        both = jnp.concatenate([total[k * n_tok : (k + 1) * n_tok]] * (cols // 128), axis=1)
        mask = slot_mask(ins[k][...], n_tok, cols, rank)
        spread.append(jnp.where(mask, both, 0.0).astype(BF16))
    rows = jnp.concatenate(spread, axis=0)
    for half in range(2):
        loads[half].wait()
        for j in range(0, width, 512):
            got = dot(rows, u_ref[half, :, j : j + 512]).astype(BF16)
            for k in range(n_recv):
                outs[k][half * n_tok : (half + 1) * n_tok, j : j + 512] = got[k * n_tok : (k + 1) * n_tok]


def up(a, b, recv, up_rows, other, n_tok, rank):
    n = len(recv)
    cols, width = up_rows.shape
    last = recv[0].shape[0] // (2 * CAP) - 1
    tail = pl.BlockSpec((2 * CAP, 128), lambda i: (last, 0))

    def whole(x):
        return pl.BlockSpec(x.shape, lambda i: (0, 0))

    out = jax.ShapeDtypeStruct((2 * n_tok, width), BF16)
    return pl.pallas_call(
        functools.partial(up_kernel, n_tok, rank, n),
        out_shape=[out] * n,
        grid=(1,),
        in_specs=[HBM] * 2 + [whole(a), whole(b)] + [tail] * n,
        out_specs=[whole(out)] * n,
        scratch_shapes=[pltpu.VMEM((2, cols, width), BF16), pltpu.SemaphoreType.DMA((2,))],
        compiler_params=params(20),
        cost_estimate=pl.CostEstimate(
            flops=4 * n * n_tok * width * cols, bytes_accessed=4 * width * cols, transcendentals=0
        ),
        name="up",
    )(up_rows, other, a, b, *recv)


def make_attn_kernel(nb, steps, group):
    halves = CAP // SUB
    n_tok = steps * CAP
    n_sub = steps * SUB
    n_q = group * n_sub

    def kernel(*refs):
        core_ref, rows_ref, q_hbm, k_hbm, v_hbm, tab_hbm, ck_ref, cv_ref = refs[:8]
        lora_refs = refs[8 : 8 + nb]
        out_ref, kbuf, vbuf, obuf, q_ref, k_ref, v_ref, tab_ref, loras, sem, osem = refs[8 + nb :]
        kv_local = k_ref.shape[1] // HD
        span = ck_ref.shape[1]
        scale = 1.0 / math.sqrt(HD)
        is_even = core_ref[0] == 0

        def copies(b):
            at = pl.ds(b * n_tok, n_tok)
            got = [
                pltpu.make_async_copy(src.at[at], dst.at[at], sem.at[b, n])
                for n, (src, dst) in enumerate(
                    ((q_hbm, q_ref), (k_hbm, k_ref), (v_hbm, v_ref), (tab_hbm, tab_ref))
                )
            ]
            got.append(pltpu.make_async_copy(lora_refs[b], loras.at[b], sem.at[b, 4]))
            return got

        for b in range(0, nb, 2):
            for n in (b, b + 1):
                for i in range(CAP):
                    r = rows_ref[n * CAP + i, 0]
                    pltpu.make_async_copy(ck_ref.at[r], kbuf.at[n, i], sem.at[n, 5]).start()
                    pltpu.make_async_copy(cv_ref.at[r], vbuf.at[n, i], sem.at[n, 6]).start()
                for c in copies(n):
                    c.start()

        qi, ki = iota((n_sub, n_sub), 0), iota((n_sub, n_sub), 1)
        new_ok = (lax.rem(qi, SUB) == lax.rem(ki, SUB)) & (lax.div(qi, SUB) >= lax.div(ki, SUB))
        new_bias = jnp.concatenate([jnp.where(new_ok, 0.0, NEG)] * group, axis=0)
        col, sub = iota((CAP, SUB * span), 1), iota((CAP, SUB * span), 0)
        own = lax.div(col, span) == lax.rem(sub, SUB)
        at_pos = lax.rem(col, span).astype(F32)
        y, x = iota((n_tok, n_tok), 0), iota((n_tok, n_tok), 1)
        x_row, x_step = token_place(x, steps)
        turn = one_hot((lax.div(y, steps) == x_row) & (lax.rem(y, steps) == x_step))

        for b in range(nb):
            if b % 2 == 0:
                for n in (b, b + 1):
                    for c in copies(n):
                        c.wait()
                    pltpu.make_async_copy(ck_ref.at[pl.ds(0, CAP)], kbuf.at[n], sem.at[n, 5]).wait()
                    pltpu.make_async_copy(cv_ref.at[pl.ds(0, CAP)], vbuf.at[n], sem.at[n, 6]).wait()
            rows = slice(b * n_tok, (b + 1) * n_tok)
            cos, sin = tab_ref[rows, :HD], tab_ref[rows, HD : 2 * HD]
            mine, theirs = loras.at[2 * (b // 2)], loras.at[2 * (b // 2) + 1]
            biases = []
            for t in range(halves):
                at = b * n_tok + t * n_sub
                lens = tab_ref[at : at + CAP, 2 * HD :][:, :1]
                bias = jnp.where(own & (at_pos < lens), 0.0, NEG)
                biases.append(jnp.concatenate([bias] * (n_q // CAP), axis=0))

            def rope(v):
                return v * cos + pltpu.roll(v, HD // 2, 1) * sin

            work = [(h, t) for h in range(kv_local) for t in range(halves)]
            qs, kns, vns = {}, {}, {}
            for h in range(kv_local):
                hs = slice(h * HD, (h + 1) * HD)
                heads = []
                for g in range(group):
                    cs = slice((h * group + g) * HD, (h * group + g + 1) * HD)
                    if b % 2 == 0:
                        lora = jnp.where(is_even, mine[:n_tok, cs], theirs[n_tok:, cs])
                    else:
                        lora = jnp.where(is_even, theirs[n_tok:, cs], mine[:n_tok, cs])
                    heads.append(rope(q_ref[rows, cs] + lora.astype(F32)).astype(BF16))
                kn = rope(k_ref[rows, hs]).astype(BF16)
                vn = v_ref[rows, hs].astype(BF16)
                for t in range(halves):
                    ts = slice(t * n_sub, (t + 1) * n_sub)
                    qs[h, t] = jnp.concatenate([v[ts] for v in heads], axis=0)
                    kns[h, t], vns[h, t] = kn[ts], vn[ts]
            s1, s2 = {}, {}
            for h, t in work:
                kc = kbuf[b, t * SUB : (t + 1) * SUB, :, h * HD : (h + 1) * HD].reshape(SUB * span, HD)
                s1[h, t] = dot_t(qs[h, t], kc) * scale + biases[t]
                s2[h, t] = dot_t(qs[h, t], kns[h, t]) * scale + new_bias
            p1, p2 = {}, {}
            for w in work:
                top = jnp.maximum(jnp.max(s1[w], axis=1, keepdims=True), jnp.max(s2[w], axis=1, keepdims=True))
                e1 = jnp.exp(s1[w] - top)
                e2 = jnp.exp(s2[w] - top)
                den = jnp.sum(e1, axis=1, keepdims=True) + jnp.sum(e2, axis=1, keepdims=True)
                inv = 1.0 / den
                p1[w], p2[w] = (e1 * inv).astype(BF16), (e2 * inv).astype(BF16)
            parts = {}
            for h, t in work:
                vc = vbuf[b, t * SUB : (t + 1) * SUB, :, h * HD : (h + 1) * HD].reshape(SUB * span, HD)
                o = dot(p1[h, t], vc) + dot(p2[h, t], vns[h, t])
                o = o.astype(BF16)
                parts[h, t] = jnp.concatenate([o[g * n_sub : (g + 1) * n_sub] for g in range(group)], axis=1)
            wide = group * HD
            for h in range(kv_local):
                both = jnp.concatenate([parts[h, t] for t in range(halves)], axis=0)
                mixed = dot(turn, both).astype(BF16)
                obuf[b, :, :, h * wide : (h + 1) * wide] = mixed.reshape(CAP, steps, wide)
            for i in range(CAP):
                r = rows_ref[b * CAP + i, 0]
                pltpu.make_async_copy(obuf.at[b, i], out_ref.at[r], osem).start()
        for b in range(nb):
            pltpu.make_async_copy(obuf.at[b], out_ref.at[pl.ds(0, CAP)], osem).wait()

    return kernel


def attention(steps, core, rows, q, k, v, table, ck, cv, loras):
    n_rows = ck.shape[0]
    nb = n_rows // CAP
    group = q.shape[1] // k.shape[1]
    buf = (nb, CAP) + ck.shape[1:]
    return pl.pallas_call(
        make_attn_kernel(nb, steps, group),
        out_shape=jax.ShapeDtypeStruct((n_rows, steps, q.shape[1]), BF16),
        in_specs=[SM, SM] + [HBM] * (6 + nb),
        out_specs=HBM,
        scratch_shapes=[
            pltpu.VMEM(buf, BF16),
            pltpu.VMEM(buf, BF16),
            pltpu.VMEM((nb, CAP, steps, q.shape[1]), BF16),
            pltpu.VMEM(q.shape, F32),
            pltpu.VMEM(k.shape, F32),
            pltpu.VMEM(v.shape, F32),
            pltpu.VMEM(table.shape, F32),
            pltpu.VMEM((nb,) + loras[0].shape, BF16),
            pltpu.SemaphoreType.DMA((nb, 7)),
            pltpu.SemaphoreType.DMA,
        ],
        compiler_params=params(62),
        name="attn",
    )(core, rows, q, k, v, table, ck, cv, *loras)


def swap(x, n, bit):
    return lax.ppermute(x, "tp", [(i, i ^ bit) for i in range(n)])


def after(x, *deps):
    return lax.optimization_barrier((x, *deps))[0]


def body(
    tokens,
    adapter_id,
    pool_slot,
    lengths,
    w_query,
    w_key,
    w_value,
    pooled_down_weights,
    pool_up,
    cache_key,
    cache_value,
):
    n_grp = lax.axis_size("grp")
    n_tp = lax.axis_size("tp")
    row_count, steps, width = tokens.shape
    adp_rows, _, rank = pooled_down_weights.shape
    n_tok = steps * CAP
    n_blocks = row_count // CAP
    n_pairs = n_grp // 2
    seq = [j for a in range(n_pairs // 2) for j in (n_pairs // 2 + a, a)]
    me = lax.axis_index("tp")
    core = lax.rem(me, 2)

    def cross(x, j):
        perm = [
            (g * n_tp + t, (g ^ (2 * j + t % 2)) * n_tp + t)
            for g in range(n_grp)
            for t in range(n_tp)
        ]
        return lax.ppermute(x, ("grp", "tp"), perm)

    other_tokens = swap(tokens, n_tp, 1)
    perm, send, slot, lens, rows = route(adp_rows, seq, steps, adapter_id, lengths, pool_slot)
    sends = pack(n_pairs, send, slot, tokens, other_tokens)
    recv = {j: cross(sends[j], j) for j in seq}

    first = recv[0]
    up_rows = after(pool_up, sends[0]).reshape(adp_rows * rank, pool_up.shape[2])
    up_other = swap(up_rows, n_tp, 1)
    down = jnp.swapaxes(after(pooled_down_weights, sends[0]), 1, 2).reshape(adp_rows * rank, width)
    down_other = swap(down, n_tp, 1)

    pieces = {0: after(tokens, sends[0])}
    bit = n_tp // 2
    while bit > 1:
        pieces.update({off ^ bit: swap(p, n_tp, bit) for off, p in list(pieces.items())})
        bit //= 2
    far = [o for o in sorted(pieces) if o]
    weights = (w_query, w_key, w_value)

    def shards(offs):
        return jnp.stack([lax.bitwise_xor(me, o) for o in offs]).astype(I32)

    ids = after(shards([0, 1]), first, up_other, down_other)
    acc = qkv([tokens, other_tokens], perm, ids, weights, None)

    half = HD // 2
    inv_freq = jnp.exp(jnp.arange(half, dtype=F32) * (-2.0 * math.log(ROPE_BASE) / HD))
    inv_freq = jnp.concatenate([inv_freq, inv_freq])
    step_of = jnp.tile(jnp.repeat(jnp.arange(steps, dtype=F32), SUB), row_count // SUB)
    lens = after(lens, first)
    angles = (lens + step_of[:, None]) * inv_freq
    sign = jnp.where(jnp.arange(HD) < half, -1.0, 1.0).astype(F32)
    table = jnp.concatenate([jnp.cos(angles), jnp.sin(angles) * sign, lens], axis=1)

    chunk = n_pairs // N_CHUNKS
    groups = [seq[i : i + chunk] for i in range(0, n_pairs, chunk)]
    mids = []
    for i, js in enumerate(groups):
        got = [recv[j] for j in js]
        if i == 0:
            got, acc, table = lax.optimization_barrier((got, acc, table))
        part = mid(got, down, down_other, n_tok, rank)
        bit = 2
        while bit < n_tp // 2:
            part = part + swap(part, n_tp, bit)
            bit *= 2
        mids.append((got, part, swap(part, n_tp, bit)))
    back = {}
    for js, (got, part, other) in zip(groups, mids):
        for j, x in zip(js, up(part, other, got, up_rows, up_other, n_tok, rank)):
            back[j] = cross(x, j)
    late = {}
    for o in far:
        x = after(pieces[o], mids[-1][1])
        late[o] = x
        late[o ^ 1] = swap(x, n_tp, 1)
    ids = after(shards(sorted(late)), back[0])
    q, k, v = qkv([late[o] for o in sorted(late)], perm, ids, weights, acc)
    loras = {}
    for j in seq:
        own = after(back[j], q)
        loras[j] = (own, swap(own, n_tp, 1))
    core_id = core.astype(I32).reshape(1)
    lora_list = [a for j in seq for a in loras[j]]
    if n_grp != n_blocks:
        mine_all = jnp.stack([a[:n_tok] for a in lora_list[0::2]])
        other_all = jnp.stack([a[n_tok:] for a in lora_list[1::2]])
        even = jnp.where(core == 0, mine_all, other_all)
        odd = jnp.where(core == 0, other_all, mine_all)
        full = jnp.stack([even, odd], axis=1).reshape(n_grp, n_tok, even.shape[2])
        span = jnp.arange(pool_slot.shape[0], dtype=I32)
        pos = jnp.sum(jnp.where(adapter_id[:, None] == span[None, :], pool_slot[None, :], 0), axis=1)
        key = lax.bitwise_xor(lax.div(pos, adp_rows), lax.axis_index("grp"))
        order = jnp.array([2 * j + c for j in seq for c in (0, 1)], I32)
        used = jnp.any(key[:, None] == order[None, :], axis=0)
        at = jnp.cumsum(used.astype(I32)) - 1
        pick = (at[None, :] == jnp.arange(n_blocks)[:, None]) & used[None, :]
        chosen = full[jnp.sum(jnp.where(pick, jnp.arange(n_grp)[None, :], 0), axis=1)]
        core_id = jnp.zeros((1,), I32)
        twice = jnp.concatenate([chosen, chosen], axis=1)
        lora_list = [twice[b] for b in range(n_blocks)]
    return attention(steps, core_id, rows[:, :1], q, k, v, table, cache_key, cache_value, lora_list)


def solution(mesh):
    in_specs = (
        P("grp", None, "tp"),
        P("grp"),
        P(),
        P("grp"),
        P(None, "tp"),
        P(None, "tp"),
        P(None, "tp"),
        P("grp", "tp", None),
        P("grp", None, "tp"),
        P("grp", None, "tp"),
        P("grp", None, "tp"),
    )
    out_specs = P("grp", None, "tp")
    return jax.shard_map(body, mesh=mesh, in_specs=in_specs, out_specs=out_specs, check_vma=False)
```

```python
import functools
import math

import jax
import jax.numpy as jnp
from jax import lax
from jax.experimental import pallas as pl
from jax.experimental.pallas import tpu as pltpu
from jax.sharding import PartitionSpec as P

HD = 128
CAP = 8
SUB = 4
ROPE_BASE = 500000.0
NEG = -1e30
MIB = 1024 * 1024
F32 = jnp.float32
BF16 = jnp.bfloat16
I32 = jnp.int32
FIRST_STEPS = (256, 256)
STEP = 512
PARTS = 4
AHEAD = 4
TOGETHER = 2

TINY = pl.CostEstimate(flops=1, bytes_accessed=1, transcendentals=0)
COST = pl.CostEstimate(flops=10**10, bytes_accessed=3 * 10**7, transcendentals=0)
VM = pl.BlockSpec(memory_space=pltpu.VMEM)
SM = pl.BlockSpec(memory_space=pltpu.SMEM)
HBM = pl.BlockSpec(memory_space=pltpu.HBM)


def params(mib):
    return pltpu.CompilerParams(vmem_limit_bytes=int(mib * MIB))


def dot(a, b):
    return jnp.dot(a, b, preferred_element_type=F32)


def dot_t(a, b):
    return lax.dot_general(a, b, (((1,), (1,)), ((), ())), preferred_element_type=F32)


def iota(shape, dim):
    return lax.broadcasted_iota(I32, shape, dim)


def one_hot(cond):
    return jnp.where(cond, 1.0, 0.0).astype(BF16)


def token_place(p, steps):
    n_sub = SUB * steps
    half = lax.rem(lax.div(p, n_sub), CAP // SUB)
    return half * SUB + lax.rem(p, SUB), lax.rem(lax.div(p, SUB), steps)


def route_kernel(adp_rows, seq, steps, ids_ref, lens_ref, slots_ref, *outs):
    perm_ref, send_ref, slot_ref, len_ref, row_ref = outs
    rows = ids_ref.shape[1]
    pool = slots_ref.shape[1]
    toks = rows * steps
    me = lax.axis_index("grp")
    core = lax.rem(lax.axis_index("tp"), 2)
    sub, lane = iota((rows, rows), 0), iota((rows, rows), 1)
    eye = sub == lane

    def to_col(row):
        return jnp.sum(jnp.where(eye, row, 0.0), axis=1, keepdims=True)

    def to_row(col):
        return jnp.sum(jnp.where(eye, col, 0.0), axis=0, keepdims=True)

    ids_col = to_col(ids_ref[...].astype(F32))
    lens_col = to_col(lens_ref[...].astype(F32))
    span = iota((rows, pool), 1).astype(F32)
    pos = jnp.sum(jnp.where(ids_col == span, slots_ref[...].astype(F32), 0.0), axis=1, keepdims=True)
    pos = pos.astype(I32)
    owner = lax.div(pos, adp_rows)
    slot = (pos - owner * adp_rows).astype(F32)
    key = lax.bitwise_xor(owner, me)
    pair = lax.div(key, 2)
    place = jnp.zeros_like(pair)
    for at, j in enumerate(seq):
        place = jnp.where(pair == j, at, place)
    place = (place * 2 + lax.rem(key, 2)).astype(F32)
    key = key.astype(F32)
    place_row = to_row(place)
    same = place_row == place
    before = same & (lane < sub)
    rank = jnp.sum(jnp.where(before, 1.0, 0.0), axis=1, keepdims=True)
    dest = jnp.sum(jnp.where((place_row < place) | before, 1.0, 0.0), axis=1, keepdims=True)
    dest_row, key_row, rank_row = to_row(dest), to_row(key), to_row(rank)

    def wide(col):
        return jnp.broadcast_to(col, (rows, 128)).astype(BF16)

    row_perm = one_hot(sub.astype(F32) == dest_row)
    ids = jnp.broadcast_to(lane[:1].astype(F32), (8, rows)).astype(BF16)
    row_ref[...] = dot_t(ids, row_perm).astype(I32)
    row_of, _ = token_place(iota((toks, rows), 0), steps)
    row_of = (row_of + lax.div(iota((toks, rows), 0), CAP * steps) * CAP).astype(F32)
    len_ref[...] = dot(one_hot(row_of == dest_row), wide(lens_col))
    n_pairs = len(seq)
    y = iota((n_pairs * 2 * CAP, rows), 0)
    y_key = (lax.div(y, 2 * CAP) * 2 + core).astype(F32)
    y_rank = (lax.rem(lax.div(y, CAP), 2) * SUB + lax.rem(y, SUB)).astype(F32)
    slot_ref[...] = dot(one_hot((y_key == key_row) & (y_rank == rank_row)), wide(slot)).astype(BF16)

    spread = one_hot(lax.div(iota((rows, toks), 1), steps) == iota((rows, toks), 0))
    info = jnp.concatenate([dest_row, key_row, rank_row] + [dest_row] * 5, axis=0).astype(BF16)
    info = dot(info, spread)
    dest_tok, key_tok, rank_tok = info[0:1], info[1:2], info[2:3]
    p, step_tok = iota((toks, toks), 0), lax.rem(iota((toks, toks), 1), steps)
    p_row, p_step = token_place(p, steps)
    p_row = (p_row + lax.div(p, CAP * steps) * CAP).astype(F32)
    perm = one_hot((p_row == dest_tok) & (p_step == step_tok))
    perm_ref[...] = perm
    n_send = n_pairs * CAP * steps
    p, step_tok = iota((n_send, toks), 0), lax.rem(iota((n_send, toks), 1), steps)
    p_row, p_step = token_place(p, steps)
    p_key = (lax.div(p, CAP * steps) * 2 + core).astype(F32)
    send_ref[...] = one_hot((p_key == key_tok) & (p_row.astype(F32) == rank_tok) & (p_step == step_tok))


def route(adp_rows, seq, steps, adapter_id, lengths, pool_slot):
    rows = adapter_id.shape[0]
    toks = rows * steps
    out = [
        jax.ShapeDtypeStruct((toks, toks), BF16),
        jax.ShapeDtypeStruct((len(seq) * CAP * steps, toks), BF16),
        jax.ShapeDtypeStruct((len(seq) * 2 * CAP, 128), BF16),
        jax.ShapeDtypeStruct((toks, 128), F32),
        jax.ShapeDtypeStruct((8, rows), I32),
    ]
    return pl.pallas_call(
        functools.partial(route_kernel, adp_rows, seq, steps),
        out_shape=out,
        in_specs=[VM] * 3,
        out_specs=[VM] * len(out),
        compiler_params=params(62),
        name="route",
    )(adapter_id[None, :], lengths[None, :], pool_slot[None, :])


def pack_kernel(n_tok, send_ref, slot_ref, tok_ref, oth_ref, *sends):
    rows, steps, width = tok_ref.shape
    for j in range(0, width, 512):
        for half, ref in enumerate((tok_ref, oth_ref)):
            part = ref[:, :, j : j + 512].reshape(rows * steps, 512)
            got = dot(send_ref[...], part).astype(BF16)
            for k, out in enumerate(sends):
                for c in range(4):
                    at = ((j // 128 + c) * 2 + half) * n_tok
                    out[at : at + n_tok, :] = got[k * n_tok : (k + 1) * n_tok, c * 128 : (c + 1) * 128]
    for k, out in enumerate(sends):
        out[width // 128 * 2 * n_tok :, :] = slot_ref[k * 2 * CAP : (k + 1) * 2 * CAP, :]


def pack(n_pairs, send, slot, tokens, other):
    _, steps, width = tokens.shape
    n_tok = steps * CAP
    out = [jax.ShapeDtypeStruct((width // 128 * 2 * n_tok + 2 * CAP, 128), BF16)] * n_pairs
    return pl.pallas_call(
        functools.partial(pack_kernel, n_tok),
        out_shape=out,
        in_specs=[VM] * 4,
        out_specs=[VM] * len(out),
        compiler_params=params(62),
        name="pack",
    )(send, slot, tokens, other)


def qkv_kernel(n_x, has_acc, steps, ids_ref, perm_ref, *refs):
    xs, ws = refs[:n_x], refs[n_x : n_x + 3]
    at = n_x + 3
    accs = refs[at : at + 3] if has_acc else (None,) * 3
    at += 3 if has_acc else 0
    outs, raw, xbuf = refs[at : at + 3], refs[at + 3], refs[at + 4]
    bufs, xsem, wsem = refs[at + 5 : at + 8], refs[at + 8], refs[at + 9]
    rows, n_steps, width = xs[0].shape

    def x_copy(p):
        return pltpu.make_async_copy(xs[p], raw.at[p], xsem.at[p])

    def w_copy(n, i):
        lo, size = steps[n]
        row = pl.multiple_of(ids_ref[lo // width] * width + lo % width, 256)
        return pltpu.make_async_copy(ws[i].at[pl.ds(row, size)], bufs[i].at[lo : lo + size], wsem.at[n, i])

    def begin(n):
        if n < len(steps):
            if steps[n][0] % width == 0:
                x_copy(steps[n][0] // width).start()
            for i in range(3):
                w_copy(n, i).start()

    begin(0)
    begin(1)
    for n, (lo, size) in enumerate(steps):
        begin(n + 2)
        if lo % width == 0:
            p = lo // width
            x_copy(p).wait()
            for j in range(0, width, 512):
                part = raw[p, :, :, j : j + 512].reshape(rows * n_steps, 512)
                xbuf[:, lo + j : lo + j + 512] = dot(perm_ref[...], part).astype(BF16)
        for i in range(3):
            w_copy(n, i).wait()
        x = xbuf[:, lo : lo + size]
        for i in range(3):
            got = dot(x, bufs[i][lo : lo + size, :])
            if lo:
                outs[i][...] += got
            else:
                outs[i][...] = accs[i][...] + got if has_acc else got


def qkv(xs, perm, shards, weights, acc):
    rows, steps, width = xs[0].shape
    m = rows * steps
    n_x = len(xs)
    has_acc = acc is not None
    outs = [jax.ShapeDtypeStruct((m, w.shape[1]), F32) for w in weights]
    cols = sum(w.shape[1] for w in weights)
    extra = list(acc) if has_acc else []
    depth = n_x * width
    plan, at = [], 0
    for size in FIRST_STEPS:
        plan.append((at, size))
        at += size
    while at < depth:
        plan.append((at, min(STEP, width - at % width)))
        at += plan[-1][1]
    return pl.pallas_call(
        functools.partial(qkv_kernel, n_x, has_acc, plan),
        out_shape=outs,
        in_specs=[SM, VM] + [HBM] * (n_x + 3) + [VM] * len(extra),
        out_specs=[VM] * 3,
        scratch_shapes=[pltpu.VMEM((n_x, rows, steps, width), BF16), pltpu.VMEM((m, depth), BF16)]
        + [pltpu.VMEM((depth, w.shape[1]), BF16) for w in weights]
        + [pltpu.SemaphoreType.DMA((n_x,)), pltpu.SemaphoreType.DMA((len(plan), 3))],
        compiler_params=params(60.5),
        cost_estimate=COST,
        name="qkv",
    )(shards, perm, *xs, *weights, *extra)


def panel_loads(srcs, dst, sem):
    size = dst.shape[1] // PARTS
    loads = []
    for i, src in enumerate(srcs):
        at = [pl.ds(p * size, size) for p in range(PARTS)]
        loads.append([pltpu.make_async_copy(src.at[a], dst.at[i, a], sem.at[i, p]) for p, a in enumerate(at)])
        for c in loads[-1]:
            c.start()
    return loads


def slot_mask(tiles, n_tok, cols, rank):
    tiles = tiles.astype(F32)
    rep = n_tok // (2 * CAP)
    slots = jnp.concatenate([tiles[:CAP]] * rep + [tiles[CAP:]] * rep, axis=0)
    slots = jnp.concatenate([slots] * (cols // 128), axis=1)
    return slots == lax.div(iota((n_tok, cols), 1), rank).astype(F32)


def mid_kernel(n_tok, rank, down_ref, oth_ref, *refs):
    ins, out_ref, x_ref, d_ref, sem = refs[:-4], refs[-4], refs[-3], refs[-2], refs[-1]
    _, cols, width = d_ref.shape
    loads = panel_loads((down_ref, oth_ref), d_ref, sem)
    for k, r in enumerate(ins):
        rows = slice(k * n_tok, (k + 1) * n_tok)
        for c in range(width // 128):
            for half in range(2):
                at = (c * 2 + half) * n_tok
                x_ref[half, rows, c * 128 : (c + 1) * 128] = r[at : at + n_tok, :]
    prod = 0.0
    for half in range(2):
        for c in loads[half]:
            c.wait()
        prod = prod + dot_t(x_ref[half], d_ref[half])
    for k, r in enumerate(ins):
        mask = slot_mask(r[r.shape[0] - 2 * CAP :, :], n_tok, cols, rank)
        part = jnp.where(mask, prod[k * n_tok : (k + 1) * n_tok], 0.0)
        tot = part[:, :128]
        for c in range(128, cols, 128):
            tot = tot + part[:, c : c + 128]
        out_ref[k * n_tok : (k + 1) * n_tok, :] = tot + pltpu.roll(tot, rank, 1)


def mid(recv, down, other, n_tok, rank):
    n = len(recv)
    cols, width = down.shape
    return pl.pallas_call(
        functools.partial(mid_kernel, n_tok, rank),
        out_shape=jax.ShapeDtypeStruct((n * n_tok, 128), F32),
        in_specs=[HBM] * 2 + [VM] * n,
        out_specs=VM,
        scratch_shapes=[
            pltpu.VMEM((2, n * n_tok, width), BF16),
            pltpu.VMEM((2, cols, width), BF16),
            pltpu.SemaphoreType.DMA((2, PARTS)),
        ],
        compiler_params=params(24),
        cost_estimate=COST,
        name="mid",
    )(down, other, *recv)


def up_kernel(n_tok, rank, n_recv, up_ref, oth_ref, a_ref, b_ref, *refs):
    ins, outs, u_ref, sem = refs[:n_recv], refs[n_recv : 2 * n_recv], refs[-2], refs[-1]
    _, cols, width = u_ref.shape
    loads = panel_loads((up_ref, oth_ref), u_ref, sem)
    total = (a_ref[...] + b_ref[...]).astype(BF16).astype(F32)
    spread = []
    for k in range(n_recv):
        both = jnp.concatenate([total[k * n_tok : (k + 1) * n_tok]] * (cols // 128), axis=1)
        mask = slot_mask(ins[k][...], n_tok, cols, rank)
        spread.append(jnp.where(mask, both, 0.0).astype(BF16))
    rows = jnp.concatenate(spread, axis=0)
    for half in range(2):
        for c in loads[half]:
            c.wait()
        for j in range(0, width, 512):
            got = dot(rows, u_ref[half, :, j : j + 512]).astype(BF16)
            for k in range(n_recv):
                outs[k][half * n_tok : (half + 1) * n_tok, j : j + 512] = got[k * n_tok : (k + 1) * n_tok]


def up(a, b, recv, up_rows, other, n_tok, rank):
    n = len(recv)
    cols, width = up_rows.shape
    last = recv[0].shape[0] // (2 * CAP) - 1
    tail = pl.BlockSpec((2 * CAP, 128), lambda i: (last, 0))

    def whole(x):
        return pl.BlockSpec(x.shape, lambda i: (0, 0))

    out = jax.ShapeDtypeStruct((2 * n_tok, width), BF16)
    return pl.pallas_call(
        functools.partial(up_kernel, n_tok, rank, n),
        out_shape=[out] * n,
        grid=(1,),
        in_specs=[HBM] * 2 + [whole(a), whole(b)] + [tail] * n,
        out_specs=[whole(out)] * n,
        scratch_shapes=[pltpu.VMEM((2, cols, width), BF16), pltpu.SemaphoreType.DMA((2, PARTS))],
        compiler_params=params(20),
        cost_estimate=COST,
        name="up",
    )(up_rows, other, a, b, *recv)


def make_attn_kernel(plan, steps, group, has_prev):
    nb = len(plan)
    halves = CAP // SUB
    n_tok = steps * CAP
    n_sub = steps * SUB
    n_q = group * n_sub

    def kernel(*refs):
        core_ref, rows_ref, q_hbm, k_hbm, v_hbm, tab_hbm, ck_ref, cv_ref = refs[:8]
        lora_refs = refs[8 : 8 + nb]
        at = 8 + nb + int(has_prev)
        out_ref, kbuf, vbuf, obuf, q_ref, k_ref, v_ref, tab_ref, loras, sem, osem = refs[at:]
        kv_local = k_ref.shape[1] // HD
        span = ck_ref.shape[1]
        scale = 1.0 / math.sqrt(HD)
        core = core_ref[0]
        blocks = [2 * j + (1 - core if other else core) for j, other in plan]

        def copies(b):
            at, to = pl.ds(pl.multiple_of(blocks[b] * n_tok, n_tok), n_tok), pl.ds(b * n_tok, n_tok)
            got = [
                pltpu.make_async_copy(src.at[at], dst.at[to], sem.at[b, n])
                for n, (src, dst) in enumerate(
                    ((q_hbm, q_ref), (k_hbm, k_ref), (v_hbm, v_ref), (tab_hbm, tab_ref))
                )
            ]
            part = pl.ds(n_tok if plan[b][1] else 0, n_tok)
            got.append(pltpu.make_async_copy(lora_refs[b].at[part], loras.at[b], sem.at[b, 4]))
            return got

        def begin(b):
            for i in range(CAP):
                r = rows_ref[blocks[b] * CAP + i]
                pltpu.make_async_copy(ck_ref.at[r], kbuf.at[b, i], sem.at[b, 5]).start()
                pltpu.make_async_copy(cv_ref.at[r], vbuf.at[b, i], sem.at[b, 6]).start()
            for c in copies(b):
                c.start()

        for b in range(min(AHEAD, nb)):
            begin(b)

        qi, ki = iota((n_sub, n_sub), 0), iota((n_sub, n_sub), 1)
        new_ok = (lax.rem(qi, SUB) == lax.rem(ki, SUB)) & (lax.div(qi, SUB) >= lax.div(ki, SUB))
        new_bias = jnp.concatenate([jnp.where(new_ok, 0.0, NEG)] * group, axis=0)
        col, sub = iota((CAP, SUB * span), 1), iota((CAP, SUB * span), 0)
        own = lax.div(col, span) == lax.rem(sub, SUB)
        at_pos = lax.rem(col, span).astype(F32)
        y, x = iota((n_tok, n_tok), 0), iota((n_tok, n_tok), 1)
        x_row, x_step = token_place(x, steps)
        turn = one_hot((lax.div(y, steps) == x_row) & (lax.rem(y, steps) == x_step))

        wide = group * HD
        for start in range(0, nb, TOGETHER):
            these = range(start, min(start + TOGETHER, nb))
            for b in these:
                if b + AHEAD < nb:
                    begin(b + AHEAD)
            for b in these:
                for c in copies(b):
                    c.wait()
                pltpu.make_async_copy(ck_ref.at[pl.ds(0, CAP)], kbuf.at[b], sem.at[b, 5]).wait()
                pltpu.make_async_copy(cv_ref.at[pl.ds(0, CAP)], vbuf.at[b], sem.at[b, 6]).wait()
            work = [(b, h, t) for b in these for h in range(kv_local) for t in range(halves)]
            biases, qs, kns, vns = {}, {}, {}, {}
            for b in these:
                rows = slice(b * n_tok, (b + 1) * n_tok)
                cos, sin = tab_ref[rows, :HD], tab_ref[rows, HD : 2 * HD]

                def rope(v):
                    return v * cos + pltpu.roll(v, HD // 2, 1) * sin

                for t in range(halves):
                    at = b * n_tok + t * n_sub
                    lens = tab_ref[at : at + CAP, 2 * HD :][:, :1]
                    bias = jnp.where(own & (at_pos < lens), 0.0, NEG)
                    biases[b, t] = jnp.concatenate([bias] * (n_q // CAP), axis=0)
                for h in range(kv_local):
                    hs = slice(h * HD, (h + 1) * HD)
                    heads = []
                    for g in range(group):
                        cs = slice((h * group + g) * HD, (h * group + g + 1) * HD)
                        heads.append(rope(q_ref[rows, cs] + loras[b, :, cs].astype(F32)).astype(BF16))
                    kn = rope(k_ref[rows, hs]).astype(BF16)
                    vn = v_ref[rows, hs].astype(BF16)
                    for t in range(halves):
                        ts = slice(t * n_sub, (t + 1) * n_sub)
                        qs[b, h, t] = jnp.concatenate([v[ts] for v in heads], axis=0)
                        kns[b, h, t], vns[b, h, t] = kn[ts], vn[ts]
            s1, s2 = {}, {}
            for w in work:
                b, h, t = w
                kc = kbuf[b, t * SUB : (t + 1) * SUB, :, h * HD : (h + 1) * HD].reshape(SUB * span, HD)
                s1[w] = dot_t(qs[w], kc) * scale + biases[b, t]
                s2[w] = dot_t(qs[w], kns[w]) * scale + new_bias
            p1, p2 = {}, {}
            for w in work:
                top = jnp.maximum(jnp.max(s1[w], axis=1, keepdims=True), jnp.max(s2[w], axis=1, keepdims=True))
                e1 = jnp.exp(s1[w] - top)
                e2 = jnp.exp(s2[w] - top)
                den = jnp.sum(e1, axis=1, keepdims=True) + jnp.sum(e2, axis=1, keepdims=True)
                inv = 1.0 / den
                p1[w], p2[w] = (e1 * inv).astype(BF16), (e2 * inv).astype(BF16)
            parts = {}
            for w in work:
                b, h, t = w
                vc = vbuf[b, t * SUB : (t + 1) * SUB, :, h * HD : (h + 1) * HD].reshape(SUB * span, HD)
                o = dot(p1[w], vc) + dot(p2[w], vns[w])
                o = o.astype(BF16)
                parts[w] = jnp.concatenate([o[g * n_sub : (g + 1) * n_sub] for g in range(group)], axis=1)
            for b in these:
                for h in range(kv_local):
                    both = jnp.concatenate([parts[b, h, t] for t in range(halves)], axis=0)
                    mixed = dot(turn, both).astype(BF16)
                    obuf[b, :, :, h * wide : (h + 1) * wide] = mixed.reshape(CAP, steps, wide)
                for i in range(CAP):
                    r = rows_ref[blocks[b] * CAP + i]
                    pltpu.make_async_copy(obuf.at[b, i], out_ref.at[r], osem).start()
        for b in range(nb):
            pltpu.make_async_copy(obuf.at[b], out_ref.at[pl.ds(0, CAP)], osem).wait()

    return kernel


def attention(plan, steps, core, rows, q, k, v, table, ck, cv, loras, prev):
    n_rows = ck.shape[0]
    nb = len(plan)
    n = nb * CAP * steps
    group = q.shape[1] // k.shape[1]
    buf = (nb, CAP) + ck.shape[1:]
    extra = [] if prev is None else [prev]
    return pl.pallas_call(
        make_attn_kernel(plan, steps, group, bool(extra)),
        out_shape=jax.ShapeDtypeStruct((n_rows, steps, q.shape[1]), BF16),
        in_specs=[SM, SM] + [HBM] * (6 + nb + len(extra)),
        out_specs=HBM,
        scratch_shapes=[
            pltpu.VMEM(buf, BF16),
            pltpu.VMEM(buf, BF16),
            pltpu.VMEM((nb, CAP, steps, q.shape[1]), BF16),
            pltpu.VMEM((n, q.shape[1]), F32),
            pltpu.VMEM((n, k.shape[1]), F32),
            pltpu.VMEM((n, v.shape[1]), F32),
            pltpu.VMEM((n, table.shape[1]), F32),
            pltpu.VMEM((nb, CAP * steps, q.shape[1]), BF16),
            pltpu.SemaphoreType.DMA((nb, 7)),
            pltpu.SemaphoreType.DMA,
        ],
        input_output_aliases={8 + nb: 0} if extra else {},
        compiler_params=params(62),
        cost_estimate=TINY,
        name="attn",
    )(core, rows, q, k, v, table, ck, cv, *loras, *extra)


def swap(x, n, bit):
    return lax.ppermute(x, "tp", [(i, i ^ bit) for i in range(n)])


def after(x, *deps):
    return lax.optimization_barrier((x, *deps))[0]


def body(
    tokens,
    adapter_id,
    pool_slot,
    lengths,
    w_query,
    w_key,
    w_value,
    pooled_down_weights,
    pool_up,
    cache_key,
    cache_value,
):
    n_grp = lax.axis_size("grp")
    n_tp = lax.axis_size("tp")
    row_count, steps, width = tokens.shape
    adp_rows, _, rank = pooled_down_weights.shape
    n_tok = steps * CAP
    n_blocks = row_count // CAP
    n_pairs = n_grp // 2
    seq = [*range(n_pairs // 2, n_pairs), *range(n_pairs // 2)]
    me = lax.axis_index("tp")
    core = lax.rem(me, 2)

    def cross(x, j):
        perm = [
            (g * n_tp + t, (g ^ (2 * j + t % 2)) * n_tp + t)
            for g in range(n_grp)
            for t in range(n_tp)
        ]
        return lax.ppermute(x, ("grp", "tp"), perm)

    other_tokens = swap(tokens, n_tp, 1)
    perm, send, slot, lens, rows = route(adp_rows, seq, steps, adapter_id, lengths, pool_slot)
    rows = rows[0]
    sends = pack(n_pairs, send, slot, tokens, other_tokens)
    recv = {j: cross(sends[j], j) for j in seq}

    first = recv[0]
    up_rows = after(pool_up, sends[0]).reshape(adp_rows * rank, pool_up.shape[2])
    up_other = swap(up_rows, n_tp, 1)
    down = jnp.swapaxes(after(pooled_down_weights, sends[0]), 1, 2).reshape(adp_rows * rank, width)
    down_other = swap(down, n_tp, 1)

    weights = (w_query, w_key, w_value)

    def shards(offs):
        return jnp.stack([lax.bitwise_xor(me, o) for o in offs]).astype(I32)

    ids = after(shards([0, 1]), up_other, down_other)
    acc = qkv([tokens, other_tokens], perm, ids, weights, None)
    pieces = {0: tokens}
    bit = n_tp // 2
    while bit > 1:
        pieces.update({off ^ bit: swap(p, n_tp, bit) for off, p in list(pieces.items())})
        bit //= 2
    far = [o for o in sorted(pieces) if o]

    half = HD // 2
    inv_freq = jnp.exp(jnp.arange(half, dtype=F32) * (-2.0 * math.log(ROPE_BASE) / HD))
    inv_freq = jnp.concatenate([inv_freq, inv_freq])
    step_of = jnp.tile(jnp.repeat(jnp.arange(steps, dtype=F32), SUB), row_count // SUB)
    lens = after(lens, first)
    angles = (lens + step_of[:, None]) * inv_freq
    sign = jnp.where(jnp.arange(HD) < half, -1.0, 1.0).astype(F32)
    table = jnp.concatenate([jnp.cos(angles), jnp.sin(angles) * sign, lens], axis=1)

    got = [recv[j] for j in seq]
    got, acc, table = lax.optimization_barrier((got, acc, table))
    part = mid(got, down, down_other, n_tok, rank)
    bit = 2
    while bit < n_tp // 2:
        part = part + swap(part, n_tp, bit)
        bit *= 2
    sent = up(part, swap(part, n_tp, bit), got, up_rows, up_other, n_tok, rank)
    back = {j: cross(x, j) for j, x in zip(seq, sent)}
    late = {}
    for o in far:
        x = after(pieces[o], sent[0])
        late[o] = x
        late[o ^ 1] = swap(x, n_tp, 1)
    ids = after(shards(sorted(late)), back[0])
    q, k, v = qkv([late[o] for o in sorted(late)], perm, ids, weights, acc)

    def attend(plan, loras, core_id, prev):
        return attention(
            plan, steps, core_id, rows, q, k, v, table, cache_key, cache_value, loras, prev
        )

    if n_grp == n_blocks:
        core_id = core.astype(I32).reshape(1)
        own = {j: after(back[j], q) for j in seq}
        other = {j: swap(own[j], n_tp, 1) for j in seq}
        plan = [(j, o) for j in seq for o in (False, True)]
        placed = [(seq.index(j), o) for j, o in plan]
        return attend(placed, [(other if o else own)[j] for j, o in plan], core_id, None)

    pairs = [(back[j], swap(back[j], n_tp, 1)) for j in seq]
    mine_all = jnp.stack([a[:n_tok] for a, _ in pairs])
    other_all = jnp.stack([a[n_tok:] for _, a in pairs])
    even = jnp.where(core == 0, mine_all, other_all)
    odd = jnp.where(core == 0, other_all, mine_all)
    full = jnp.stack([even, odd], axis=1).reshape(n_grp, n_tok, even.shape[2])
    span = jnp.arange(pool_slot.shape[0], dtype=I32)
    pos = jnp.sum(jnp.where(adapter_id[:, None] == span[None, :], pool_slot[None, :], 0), axis=1)
    key = lax.bitwise_xor(lax.div(pos, adp_rows), lax.axis_index("grp"))
    order = jnp.array([2 * j + c for j in seq for c in (0, 1)], I32)
    used = jnp.any(key[:, None] == order[None, :], axis=0)
    at = jnp.cumsum(used.astype(I32)) - 1
    pick = (at[None, :] == jnp.arange(n_blocks)[:, None]) & used[None, :]
    chosen = full[jnp.sum(jnp.where(pick, jnp.arange(n_grp)[None, :], 0), axis=1)]
    twice = jnp.concatenate([chosen, chosen], axis=1)
    plan = [(b // 2, b % 2 == 1) for b in range(n_blocks)]
    return attend(plan, [twice[b] for b in range(n_blocks)], jnp.zeros((1,), I32), None)


def solution(mesh):
    in_specs = (
        P("grp", None, "tp"),
        P("grp"),
        P(),
        P("grp"),
        P(None, "tp"),
        P(None, "tp"),
        P(None, "tp"),
        P("grp", "tp", None),
        P("grp", None, "tp"),
        P("grp", None, "tp"),
        P("grp", None, "tp"),
    )
    out_specs = P("grp", None, "tp")
    return jax.shard_map(body, mesh=mesh, in_specs=in_specs, out_specs=out_specs, check_vma=False)
```

```python
import functools
import math

import jax
import jax.numpy as jnp
from jax import lax
from jax.experimental import pallas as pl
from jax.experimental.pallas import tpu as pltpu
from jax.sharding import PartitionSpec as P

HD = 128
CAP = 8
SUB = 4
ROPE_BASE = 500000.0
NEG = -1e30
MIB = 1024 * 1024
F32 = jnp.float32
BF16 = jnp.bfloat16
I32 = jnp.int32
FIRST_STEPS = (256, 256)
STEP = 512
PARTS = 4
AHEAD = 4
TOGETHER = 2

TINY = pl.CostEstimate(flops=1, bytes_accessed=1, transcendentals=0)
QKV_COST = pl.CostEstimate(flops=10**11, bytes_accessed=3 * 10**8, transcendentals=0)
COST = pl.CostEstimate(flops=10**10, bytes_accessed=3 * 10**7, transcendentals=0)
VM = pl.BlockSpec(memory_space=pltpu.VMEM)
SM = pl.BlockSpec(memory_space=pltpu.SMEM)
HBM = pl.BlockSpec(memory_space=pltpu.HBM)


def params(mib):
    return pltpu.CompilerParams(vmem_limit_bytes=int(mib * MIB))


def dot(a, b):
    return jnp.dot(a, b, preferred_element_type=F32)


def dot_t(a, b):
    return lax.dot_general(a, b, (((1,), (1,)), ((), ())), preferred_element_type=F32)


def iota(shape, dim):
    return lax.broadcasted_iota(I32, shape, dim)


def one_hot(cond):
    return jnp.where(cond, 1.0, 0.0).astype(BF16)


def token_place(p, steps):
    n_sub = SUB * steps
    half = lax.rem(lax.div(p, n_sub), CAP // SUB)
    return half * SUB + lax.rem(p, SUB), lax.rem(lax.div(p, SUB), steps)


def route_kernel(adp_rows, seq, steps, ids_ref, lens_ref, slots_ref, *outs):
    perm_ref, send_ref, slot_ref, len_ref, row_ref = outs
    rows = ids_ref.shape[1]
    pool = slots_ref.shape[1]
    toks = rows * steps
    me = lax.axis_index("grp")
    core = lax.rem(lax.axis_index("tp"), 2)
    sub, lane = iota((rows, rows), 0), iota((rows, rows), 1)
    eye = sub == lane

    def to_col(row):
        return jnp.sum(jnp.where(eye, row, 0.0), axis=1, keepdims=True)

    def to_row(col):
        return jnp.sum(jnp.where(eye, col, 0.0), axis=0, keepdims=True)

    ids_col = to_col(ids_ref[...].astype(F32))
    lens_col = to_col(lens_ref[...].astype(F32))
    span = iota((rows, pool), 1).astype(F32)
    pos = jnp.sum(jnp.where(ids_col == span, slots_ref[...].astype(F32), 0.0), axis=1, keepdims=True)
    pos = pos.astype(I32)
    owner = lax.div(pos, adp_rows)
    slot = (pos - owner * adp_rows).astype(F32)
    key = lax.bitwise_xor(owner, me)
    pair = lax.div(key, 2)
    place = jnp.zeros_like(pair)
    for at, j in enumerate(seq):
        place = jnp.where(pair == j, at, place)
    place = (place * 2 + lax.rem(key, 2)).astype(F32)
    key = key.astype(F32)
    place_row = to_row(place)
    same = place_row == place
    before = same & (lane < sub)
    rank = jnp.sum(jnp.where(before, 1.0, 0.0), axis=1, keepdims=True)
    dest = jnp.sum(jnp.where((place_row < place) | before, 1.0, 0.0), axis=1, keepdims=True)
    dest_row, key_row, rank_row = to_row(dest), to_row(key), to_row(rank)

    def wide(col):
        return jnp.broadcast_to(col, (rows, 128)).astype(BF16)

    row_perm = one_hot(sub.astype(F32) == dest_row)
    ids = jnp.broadcast_to(lane[:1].astype(F32), (8, rows)).astype(BF16)
    row_ref[...] = dot_t(ids, row_perm)[:1].astype(I32)
    row_of, _ = token_place(iota((toks, rows), 0), steps)
    row_of = (row_of + lax.div(iota((toks, rows), 0), CAP * steps) * CAP).astype(F32)
    len_ref[...] = dot(one_hot(row_of == dest_row), wide(lens_col))
    n_pairs = len(seq)
    y = iota((n_pairs * 2 * CAP, rows), 0)
    y_key = (lax.div(y, 2 * CAP) * 2 + core).astype(F32)
    y_rank = (lax.rem(lax.div(y, CAP), 2) * SUB + lax.rem(y, SUB)).astype(F32)
    slot_ref[...] = dot(one_hot((y_key == key_row) & (y_rank == rank_row)), wide(slot)).astype(BF16)

    spread = one_hot(lax.div(iota((rows, toks), 1), steps) == iota((rows, toks), 0))
    info = jnp.concatenate([dest_row, key_row, rank_row] + [dest_row] * 5, axis=0).astype(BF16)
    info = dot(info, spread)
    dest_tok, key_tok, rank_tok = info[0:1], info[1:2], info[2:3]
    p, step_tok = iota((toks, toks), 0), lax.rem(iota((toks, toks), 1), steps)
    p_row, p_step = token_place(p, steps)
    p_row = (p_row + lax.div(p, CAP * steps) * CAP).astype(F32)
    perm = one_hot((p_row == dest_tok) & (p_step == step_tok))
    perm_ref[...] = perm
    n_send = n_pairs * CAP * steps
    p, step_tok = iota((n_send, toks), 0), lax.rem(iota((n_send, toks), 1), steps)
    p_row, p_step = token_place(p, steps)
    p_key = (lax.div(p, CAP * steps) * 2 + core).astype(F32)
    send_ref[...] = one_hot((p_key == key_tok) & (p_row.astype(F32) == rank_tok) & (p_step == step_tok))


def route(adp_rows, seq, steps, adapter_id, lengths, pool_slot):
    rows = adapter_id.shape[0]
    toks = rows * steps
    out = [
        jax.ShapeDtypeStruct((toks, toks), BF16),
        jax.ShapeDtypeStruct((len(seq) * CAP * steps, toks), BF16),
        jax.ShapeDtypeStruct((len(seq) * 2 * CAP, 128), BF16),
        jax.ShapeDtypeStruct((toks, 128), F32),
        jax.ShapeDtypeStruct((1, rows), I32),
    ]
    return pl.pallas_call(
        functools.partial(route_kernel, adp_rows, seq, steps),
        out_shape=out,
        in_specs=[VM] * 3,
        out_specs=[VM] * len(out),
        compiler_params=params(62),
        name="route",
    )(adapter_id[None, :], lengths[None, :], pool_slot[None, :])


def pack_kernel(n_tok, send_ref, slot_ref, tok_ref, oth_ref, *sends):
    rows, steps, width = tok_ref.shape
    for j in range(0, width, 512):
        for half, ref in enumerate((tok_ref, oth_ref)):
            part = ref[:, :, j : j + 512].reshape(rows * steps, 512)
            got = dot(send_ref[...], part).astype(BF16)
            for k, out in enumerate(sends):
                for c in range(4):
                    at = ((j // 128 + c) * 2 + half) * n_tok
                    out[at : at + n_tok, :] = got[k * n_tok : (k + 1) * n_tok, c * 128 : (c + 1) * 128]
    for k, out in enumerate(sends):
        out[width // 128 * 2 * n_tok :, :] = slot_ref[k * 2 * CAP : (k + 1) * 2 * CAP, :]


def pack(n_pairs, send, slot, tokens, other):
    _, steps, width = tokens.shape
    n_tok = steps * CAP
    out = [jax.ShapeDtypeStruct((width // 128 * 2 * n_tok + 2 * CAP, 128), BF16)] * n_pairs
    return pl.pallas_call(
        functools.partial(pack_kernel, n_tok),
        out_shape=out,
        in_specs=[VM] * 4,
        out_specs=[VM] * len(out),
        compiler_params=params(62),
        name="pack",
    )(send, slot, tokens, other)


def qkv_kernel(n_x, has_acc, steps, ids_ref, perm_ref, *refs):
    xs, ws = refs[:n_x], refs[n_x : n_x + 3]
    at = n_x + 3
    accs = refs[at : at + 3] if has_acc else (None,) * 3
    at += 3 if has_acc else 0
    outs, raw, xbuf = refs[at : at + 3], refs[at + 3], refs[at + 4]
    bufs, xsem, wsem = refs[at + 5 : at + 8], refs[at + 8], refs[at + 9]
    rows, n_steps, width = xs[0].shape

    def x_copy(p):
        return pltpu.make_async_copy(xs[p], raw.at[p], xsem.at[p])

    def w_copy(n, i):
        lo, size = steps[n]
        row = pl.multiple_of(ids_ref[lo // width] * width + lo % width, 256)
        return pltpu.make_async_copy(ws[i].at[pl.ds(row, size)], bufs[i].at[lo : lo + size], wsem.at[n, i])

    def begin(n):
        if n < len(steps):
            if steps[n][0] % width == 0:
                x_copy(steps[n][0] // width).start()
            for i in range(3):
                w_copy(n, i).start()

    begin(0)
    begin(1)
    for n, (lo, size) in enumerate(steps):
        begin(n + 2)
        if lo % width == 0:
            p = lo // width
            x_copy(p).wait()
            for j in range(0, width, 512):
                part = raw[p, :, :, j : j + 512].reshape(rows * n_steps, 512)
                xbuf[:, lo + j : lo + j + 512] = dot(perm_ref[...], part).astype(BF16)
        for i in range(3):
            w_copy(n, i).wait()
        x = xbuf[:, lo : lo + size]
        for i in range(3):
            got = dot(x, bufs[i][lo : lo + size, :])
            if lo:
                outs[i][...] += got
            else:
                outs[i][...] = accs[i][...] + got if has_acc else got


def qkv(xs, perm, shards, weights, acc):
    rows, steps, width = xs[0].shape
    m = rows * steps
    n_x = len(xs)
    has_acc = acc is not None
    outs = [jax.ShapeDtypeStruct((m, w.shape[1]), F32) for w in weights]
    cols = sum(w.shape[1] for w in weights)
    extra = list(acc) if has_acc else []
    depth = n_x * width
    plan, at = [], 0
    for size in FIRST_STEPS:
        plan.append((at, size))
        at += size
    while at < depth:
        plan.append((at, min(STEP, width - at % width)))
        at += plan[-1][1]
    return pl.pallas_call(
        functools.partial(qkv_kernel, n_x, has_acc, plan),
        out_shape=outs,
        in_specs=[SM, VM] + [HBM] * (n_x + 3) + [VM] * len(extra),
        out_specs=[VM] * 3,
        scratch_shapes=[pltpu.VMEM((n_x, rows, steps, width), BF16), pltpu.VMEM((m, depth), BF16)]
        + [pltpu.VMEM((depth, w.shape[1]), BF16) for w in weights]
        + [pltpu.SemaphoreType.DMA((n_x,)), pltpu.SemaphoreType.DMA((len(plan), 3))],
        compiler_params=params(60.5),
        cost_estimate=QKV_COST,
        name="qkv",
    )(shards, perm, *xs, *weights, *extra)


def panel_loads(srcs, dst, sem):
    size = dst.shape[1] // PARTS
    loads = []
    for i, src in enumerate(srcs):
        at = [pl.ds(p * size, size) for p in range(PARTS)]
        loads.append([pltpu.make_async_copy(src.at[a], dst.at[i, a], sem.at[i, p]) for p, a in enumerate(at)])
        for c in loads[-1]:
            c.start()
    return loads


def slot_mask(tiles, n_tok, cols, rank):
    tiles = tiles.astype(F32)
    rep = n_tok // (2 * CAP)
    slots = jnp.concatenate([tiles[:CAP]] * rep + [tiles[CAP:]] * rep, axis=0)
    slots = jnp.concatenate([slots] * (cols // 128), axis=1)
    return slots == lax.div(iota((n_tok, cols), 1), rank).astype(F32)


def mid_kernel(n_tok, rank, down_ref, oth_ref, *refs):
    ins, out_ref, x_ref, d_ref, sem = refs[:-4], refs[-4], refs[-3], refs[-2], refs[-1]
    _, cols, width = d_ref.shape
    loads = panel_loads((down_ref, oth_ref), d_ref, sem)
    for k, r in enumerate(ins):
        rows = slice(k * n_tok, (k + 1) * n_tok)
        for c in range(width // 128):
            for half in range(2):
                at = (c * 2 + half) * n_tok
                x_ref[half, rows, c * 128 : (c + 1) * 128] = r[at : at + n_tok, :]
    prod = 0.0
    for half in range(2):
        for c in loads[half]:
            c.wait()
        prod = prod + dot_t(x_ref[half], d_ref[half])
    for k, r in enumerate(ins):
        mask = slot_mask(r[r.shape[0] - 2 * CAP :, :], n_tok, cols, rank)
        part = jnp.where(mask, prod[k * n_tok : (k + 1) * n_tok], 0.0)
        tot = part[:, :128]
        for c in range(128, cols, 128):
            tot = tot + part[:, c : c + 128]
        out_ref[k * n_tok : (k + 1) * n_tok, :] = tot + pltpu.roll(tot, rank, 1)


def mid(recv, down, other, n_tok, rank):
    n = len(recv)
    cols, width = down.shape
    return pl.pallas_call(
        functools.partial(mid_kernel, n_tok, rank),
        out_shape=jax.ShapeDtypeStruct((n * n_tok, 128), F32),
        in_specs=[HBM] * 2 + [VM] * n,
        out_specs=VM,
        scratch_shapes=[
            pltpu.VMEM((2, n * n_tok, width), BF16),
            pltpu.VMEM((2, cols, width), BF16),
            pltpu.SemaphoreType.DMA((2, PARTS)),
        ],
        compiler_params=params(24),
        cost_estimate=COST,
        name="mid",
    )(down, other, *recv)


def up_kernel(n_tok, rank, n_recv, up_ref, oth_ref, a_ref, b_ref, *refs):
    ins, outs, u_ref, sem = refs[:n_recv], refs[n_recv : 2 * n_recv], refs[-2], refs[-1]
    _, cols, width = u_ref.shape
    loads = panel_loads((up_ref, oth_ref), u_ref, sem)
    total = (a_ref[...] + b_ref[...]).astype(BF16).astype(F32)
    spread = []
    for k in range(n_recv):
        both = jnp.concatenate([total[k * n_tok : (k + 1) * n_tok]] * (cols // 128), axis=1)
        mask = slot_mask(ins[k][...], n_tok, cols, rank)
        spread.append(jnp.where(mask, both, 0.0).astype(BF16))
    rows = jnp.concatenate(spread, axis=0)
    for half in range(2):
        for c in loads[half]:
            c.wait()
        for j in range(0, width, 512):
            got = dot(rows, u_ref[half, :, j : j + 512]).astype(BF16)
            for k in range(n_recv):
                outs[k][half * n_tok : (half + 1) * n_tok, j : j + 512] = got[k * n_tok : (k + 1) * n_tok]


def up(a, b, recv, up_rows, other, n_tok, rank):
    n = len(recv)
    cols, width = up_rows.shape
    last = recv[0].shape[0] // (2 * CAP) - 1
    tail = pl.BlockSpec((2 * CAP, 128), lambda i: (last, 0))

    def whole(x):
        return pl.BlockSpec(x.shape, lambda i: (0, 0))

    out = jax.ShapeDtypeStruct((2 * n_tok, width), BF16)
    return pl.pallas_call(
        functools.partial(up_kernel, n_tok, rank, n),
        out_shape=[out] * n,
        grid=(1,),
        in_specs=[HBM] * 2 + [whole(a), whole(b)] + [tail] * n,
        out_specs=[whole(out)] * n,
        scratch_shapes=[pltpu.VMEM((2, cols, width), BF16), pltpu.SemaphoreType.DMA((2, PARTS))],
        compiler_params=params(20),
        cost_estimate=COST,
        name="up",
    )(up_rows, other, a, b, *recv)


def make_attn_kernel(plan, steps, group, has_prev):
    nb = len(plan)
    halves = CAP // SUB
    n_tok = steps * CAP
    n_sub = steps * SUB
    n_q = group * n_sub

    def kernel(*refs):
        core_ref, rows_ref, q_hbm, k_hbm, v_hbm, tab_hbm, ck_ref, cv_ref = refs[:8]
        lora_refs = refs[8 : 8 + nb]
        at = 8 + nb + int(has_prev)
        out_ref, kbuf, vbuf, obuf, q_ref, k_ref, v_ref, tab_ref, loras, sem, osem = refs[at:]
        kv_local = k_ref.shape[1] // HD
        span = ck_ref.shape[1]
        scale = 1.0 / math.sqrt(HD)
        core = core_ref[0]
        blocks = [2 * j + (1 - core if other else core) for j, other in plan]

        def copies(b):
            at, to = pl.ds(pl.multiple_of(blocks[b] * n_tok, n_tok), n_tok), pl.ds(b * n_tok, n_tok)
            got = [
                pltpu.make_async_copy(src.at[at], dst.at[to], sem.at[b, n])
                for n, (src, dst) in enumerate(
                    ((q_hbm, q_ref), (k_hbm, k_ref), (v_hbm, v_ref), (tab_hbm, tab_ref))
                )
            ]
            part = pl.ds(n_tok if plan[b][1] else 0, n_tok)
            got.append(pltpu.make_async_copy(lora_refs[b].at[part], loras.at[b], sem.at[b, 4]))
            return got

        def begin(b):
            for i in range(CAP):
                r = rows_ref[0, blocks[b] * CAP + i]
                pltpu.make_async_copy(ck_ref.at[r], kbuf.at[b, i], sem.at[b, 5]).start()
                pltpu.make_async_copy(cv_ref.at[r], vbuf.at[b, i], sem.at[b, 6]).start()
            for c in copies(b):
                c.start()

        for b in range(min(AHEAD, nb)):
            begin(b)

        qi, ki = iota((n_sub, n_sub), 0), iota((n_sub, n_sub), 1)
        new_ok = (lax.rem(qi, SUB) == lax.rem(ki, SUB)) & (lax.div(qi, SUB) >= lax.div(ki, SUB))
        new_bias = jnp.concatenate([jnp.where(new_ok, 0.0, NEG)] * group, axis=0)
        col, sub = iota((CAP, SUB * span), 1), iota((CAP, SUB * span), 0)
        own = lax.div(col, span) == lax.rem(sub, SUB)
        at_pos = lax.rem(col, span).astype(F32)
        y, x = iota((n_tok, n_tok), 0), iota((n_tok, n_tok), 1)
        x_row, x_step = token_place(x, steps)
        turn = one_hot((lax.div(y, steps) == x_row) & (lax.rem(y, steps) == x_step))

        wide = group * HD
        for start in range(0, nb, TOGETHER):
            these = range(start, min(start + TOGETHER, nb))
            for b in these:
                if b + AHEAD < nb:
                    begin(b + AHEAD)
            for b in these:
                for c in copies(b):
                    c.wait()
                pltpu.make_async_copy(ck_ref.at[pl.ds(0, CAP)], kbuf.at[b], sem.at[b, 5]).wait()
                pltpu.make_async_copy(cv_ref.at[pl.ds(0, CAP)], vbuf.at[b], sem.at[b, 6]).wait()
            work = [(b, h, t) for b in these for h in range(kv_local) for t in range(halves)]
            biases, qs, kns, vns = {}, {}, {}, {}
            for b in these:
                rows = slice(b * n_tok, (b + 1) * n_tok)
                cos, sin = tab_ref[rows, :HD], tab_ref[rows, HD : 2 * HD]

                def rope(v):
                    return v * cos + pltpu.roll(v, HD // 2, 1) * sin

                for t in range(halves):
                    at = b * n_tok + t * n_sub
                    lens = tab_ref[at : at + CAP, 2 * HD :][:, :1]
                    bias = jnp.where(own & (at_pos < lens), 0.0, NEG)
                    biases[b, t] = jnp.concatenate([bias] * (n_q // CAP), axis=0)
                for h in range(kv_local):
                    hs = slice(h * HD, (h + 1) * HD)
                    heads = []
                    for g in range(group):
                        cs = slice((h * group + g) * HD, (h * group + g + 1) * HD)
                        heads.append(rope(q_ref[rows, cs] + loras[b, :, cs].astype(F32)).astype(BF16))
                    kn = rope(k_ref[rows, hs]).astype(BF16)
                    vn = v_ref[rows, hs].astype(BF16)
                    for t in range(halves):
                        ts = slice(t * n_sub, (t + 1) * n_sub)
                        qs[b, h, t] = jnp.concatenate([v[ts] for v in heads], axis=0)
                        kns[b, h, t], vns[b, h, t] = kn[ts], vn[ts]
            s1, s2 = {}, {}
            for w in work:
                b, h, t = w
                kc = kbuf[b, t * SUB : (t + 1) * SUB, :, h * HD : (h + 1) * HD].reshape(SUB * span, HD)
                s1[w] = dot_t(qs[w], kc) * scale + biases[b, t]
                s2[w] = dot_t(qs[w], kns[w]) * scale + new_bias
            p1, p2 = {}, {}
            for w in work:
                top = jnp.maximum(jnp.max(s1[w], axis=1, keepdims=True), jnp.max(s2[w], axis=1, keepdims=True))
                e1 = jnp.exp(s1[w] - top)
                e2 = jnp.exp(s2[w] - top)
                den = jnp.sum(e1, axis=1, keepdims=True) + jnp.sum(e2, axis=1, keepdims=True)
                inv = 1.0 / den
                p1[w], p2[w] = (e1 * inv).astype(BF16), (e2 * inv).astype(BF16)
            parts = {}
            for w in work:
                b, h, t = w
                vc = vbuf[b, t * SUB : (t + 1) * SUB, :, h * HD : (h + 1) * HD].reshape(SUB * span, HD)
                o = dot(p1[w], vc) + dot(p2[w], vns[w])
                o = o.astype(BF16)
                parts[w] = jnp.concatenate([o[g * n_sub : (g + 1) * n_sub] for g in range(group)], axis=1)
            for b in these:
                for h in range(kv_local):
                    both = jnp.concatenate([parts[b, h, t] for t in range(halves)], axis=0)
                    mixed = dot(turn, both).astype(BF16)
                    obuf[b, :, :, h * wide : (h + 1) * wide] = mixed.reshape(CAP, steps, wide)
                for i in range(CAP):
                    r = rows_ref[0, blocks[b] * CAP + i]
                    pltpu.make_async_copy(obuf.at[b, i], out_ref.at[r], osem).start()
        for b in range(nb):
            pltpu.make_async_copy(obuf.at[b], out_ref.at[pl.ds(0, CAP)], osem).wait()

    return kernel


def attention(plan, steps, core, rows, q, k, v, table, ck, cv, loras, prev):
    n_rows = ck.shape[0]
    nb = len(plan)
    n = nb * CAP * steps
    group = q.shape[1] // k.shape[1]
    buf = (nb, CAP) + ck.shape[1:]
    extra = [] if prev is None else [prev]
    return pl.pallas_call(
        make_attn_kernel(plan, steps, group, bool(extra)),
        out_shape=jax.ShapeDtypeStruct((n_rows, steps, q.shape[1]), BF16),
        in_specs=[SM, SM] + [HBM] * (6 + nb + len(extra)),
        out_specs=HBM,
        scratch_shapes=[
            pltpu.VMEM(buf, BF16),
            pltpu.VMEM(buf, BF16),
            pltpu.VMEM((nb, CAP, steps, q.shape[1]), BF16),
            pltpu.VMEM((n, q.shape[1]), F32),
            pltpu.VMEM((n, k.shape[1]), F32),
            pltpu.VMEM((n, v.shape[1]), F32),
            pltpu.VMEM((n, table.shape[1]), F32),
            pltpu.VMEM((nb, CAP * steps, q.shape[1]), BF16),
            pltpu.SemaphoreType.DMA((nb, 7)),
            pltpu.SemaphoreType.DMA,
        ],
        input_output_aliases={8 + nb: 0} if extra else {},
        compiler_params=params(62),
        cost_estimate=TINY,
        name="attn",
    )(core, rows, q, k, v, table, ck, cv, *loras, *extra)


def swap(x, n, bit):
    return lax.ppermute(x, "tp", [(i, i ^ bit) for i in range(n)])


def after(x, *deps):
    return lax.optimization_barrier((x, *deps))[0]


def body(
    tokens,
    adapter_id,
    pool_slot,
    lengths,
    w_query,
    w_key,
    w_value,
    pooled_down_weights,
    pool_up,
    cache_key,
    cache_value,
):
    n_grp = lax.axis_size("grp")
    n_tp = lax.axis_size("tp")
    row_count, steps, width = tokens.shape
    adp_rows, _, rank = pooled_down_weights.shape
    n_tok = steps * CAP
    n_blocks = row_count // CAP
    n_pairs = n_grp // 2
    seq = [*range(n_pairs // 2, n_pairs), *range(n_pairs // 2)]
    me = lax.axis_index("tp")
    core = lax.rem(me, 2)

    def cross(x, j):
        perm = [
            (g * n_tp + t, (g ^ (2 * j + t % 2)) * n_tp + t)
            for g in range(n_grp)
            for t in range(n_tp)
        ]
        return lax.ppermute(x, ("grp", "tp"), perm)

    other_tokens = swap(tokens, n_tp, 1)
    perm, send, slot, lens, rows = route(adp_rows, seq, steps, adapter_id, lengths, pool_slot)
    sends = pack(n_pairs, send, slot, tokens, other_tokens)
    recv = {j: cross(sends[j], j) for j in seq}

    first = recv[0]
    up_rows = after(pool_up, sends[0]).reshape(adp_rows * rank, pool_up.shape[2])
    up_other = swap(up_rows, n_tp, 1)
    down = jnp.swapaxes(after(pooled_down_weights, sends[0]), 1, 2).reshape(adp_rows * rank, width)
    down_other = swap(down, n_tp, 1)

    weights = (w_query, w_key, w_value)

    def shards(offs):
        return jnp.stack([lax.bitwise_xor(me, o) for o in offs]).astype(I32)

    ids = after(shards([0, 1]), up_other, down_other)
    acc = qkv([tokens, other_tokens], perm, ids, weights, None)
    pieces = {0: after(tokens, sends[0])}
    bit = n_tp // 2
    while bit > 1:
        pieces.update({off ^ bit: swap(p, n_tp, bit) for off, p in list(pieces.items())})
        bit //= 2
    far = [o for o in sorted(pieces) if o]

    half = HD // 2
    inv_freq = jnp.exp(jnp.arange(half, dtype=F32) * (-2.0 * math.log(ROPE_BASE) / HD))
    inv_freq = jnp.concatenate([inv_freq, inv_freq])
    step_of = jnp.tile(jnp.repeat(jnp.arange(steps, dtype=F32), SUB), row_count // SUB)
    lens = after(lens, first)
    angles = (lens + step_of[:, None]) * inv_freq
    sign = jnp.where(jnp.arange(HD) < half, -1.0, 1.0).astype(F32)
    table = jnp.concatenate([jnp.cos(angles), jnp.sin(angles) * sign, lens], axis=1)

    got = [recv[j] for j in seq]
    got, acc, table = lax.optimization_barrier((got, acc, table))
    part = mid(got, down, down_other, n_tok, rank)
    bit = 2
    while bit < n_tp // 2:
        part = part + swap(part, n_tp, bit)
        bit *= 2
    sent = up(part, swap(part, n_tp, bit), got, up_rows, up_other, n_tok, rank)
    back = {j: cross(x, j) for j, x in zip(seq, sent)}
    late = {}
    for o in far:
        x = after(pieces[o], sent[0])
        late[o] = x
        late[o ^ 1] = swap(x, n_tp, 1)
    ids = after(shards(sorted(late)), back[0])
    q, k, v = qkv([late[o] for o in sorted(late)], perm, ids, weights, acc)

    def attend(plan, loras, core_id, prev):
        return attention(
            plan, steps, core_id, rows, q, k, v, table, cache_key, cache_value, loras, prev
        )

    if n_grp == n_blocks:
        core_id = core.astype(I32).reshape(1)
        own = {j: after(back[j], q) for j in seq}
        other = {j: swap(own[j], n_tp, 1) for j in seq}
        plan = [(j, o) for j in seq for o in (False, True)]
        placed = [(seq.index(j), o) for j, o in plan]
        return attend(placed, [(other if o else own)[j] for j, o in plan], core_id, None)

    pairs = [(back[j], swap(back[j], n_tp, 1)) for j in seq]
    mine_all = jnp.stack([a[:n_tok] for a, _ in pairs])
    other_all = jnp.stack([a[n_tok:] for _, a in pairs])
    even = jnp.where(core == 0, mine_all, other_all)
    odd = jnp.where(core == 0, other_all, mine_all)
    full = jnp.stack([even, odd], axis=1).reshape(n_grp, n_tok, even.shape[2])
    span = jnp.arange(pool_slot.shape[0], dtype=I32)
    pos = jnp.sum(jnp.where(adapter_id[:, None] == span[None, :], pool_slot[None, :], 0), axis=1)
    key = lax.bitwise_xor(lax.div(pos, adp_rows), lax.axis_index("grp"))
    order = jnp.array([2 * j + c for j in seq for c in (0, 1)], I32)
    used = jnp.any(key[:, None] == order[None, :], axis=0)
    at = jnp.cumsum(used.astype(I32)) - 1
    pick = (at[None, :] == jnp.arange(n_blocks)[:, None]) & used[None, :]
    chosen = full[jnp.sum(jnp.where(pick, jnp.arange(n_grp)[None, :], 0), axis=1)]
    twice = jnp.concatenate([chosen, chosen], axis=1)
    plan = [(b // 2, b % 2 == 1) for b in range(n_blocks)]
    return attend(plan, [twice[b] for b in range(n_blocks)], jnp.zeros((1,), I32), None)


def solution(mesh):
    in_specs = (
        P("grp", None, "tp"),
        P("grp"),
        P(),
        P("grp"),
        P(None, "tp"),
        P(None, "tp"),
        P(None, "tp"),
        P("grp", "tp", None),
        P("grp", None, "tp"),
        P("grp", None, "tp"),
        P("grp", None, "tp"),
    )
    out_specs = P("grp", None, "tp")
    return jax.shard_map(body, mesh=mesh, in_specs=in_specs, out_specs=out_specs, check_vma=False)
```

```python
import functools
import math

import jax
import jax.numpy as jnp
from jax import lax
from jax.experimental import pallas as pl
from jax.experimental.pallas import tpu as pltpu
from jax.sharding import PartitionSpec as P

HD = 128
CAP = 8
SUB = 4
ROPE_BASE = 500000.0
NEG = -1e30
MIB = 1024 * 1024
F32 = jnp.float32
BF16 = jnp.bfloat16
I32 = jnp.int32
FIRST_STEPS = (256, 256)
STEP = 512
PARTS = 4
AHEAD = 4
TOGETHER = 2

TINY = pl.CostEstimate(flops=1, bytes_accessed=1, transcendentals=0)
QKV_COST = pl.CostEstimate(flops=10**11, bytes_accessed=3 * 10**8, transcendentals=0)
COST = pl.CostEstimate(flops=10**10, bytes_accessed=3 * 10**7, transcendentals=0)
VM = pl.BlockSpec(memory_space=pltpu.VMEM)
SM = pl.BlockSpec(memory_space=pltpu.SMEM)
HBM = pl.BlockSpec(memory_space=pltpu.HBM)


def params(mib):
    return pltpu.CompilerParams(vmem_limit_bytes=int(mib * MIB))


def dot(a, b):
    return jnp.dot(a, b, preferred_element_type=F32)


def dot_t(a, b):
    return lax.dot_general(a, b, (((1,), (1,)), ((), ())), preferred_element_type=F32)


def iota(shape, dim):
    return lax.broadcasted_iota(I32, shape, dim)


def one_hot(cond):
    return jnp.where(cond, 1.0, 0.0).astype(BF16)


def token_place(p, steps):
    n_sub = SUB * steps
    half = lax.rem(lax.div(p, n_sub), CAP // SUB)
    return half * SUB + lax.rem(p, SUB), lax.rem(lax.div(p, SUB), steps)


def route_kernel(adp_rows, seq, steps, ids_ref, lens_ref, slots_ref, *outs):
    perm_ref, send_ref, slot_ref, len_ref, row_ref = outs
    rows = ids_ref.shape[1]
    pool = slots_ref.shape[1]
    toks = rows * steps
    me = lax.axis_index("grp")
    core = lax.rem(lax.axis_index("tp"), 2)
    sub, lane = iota((rows, rows), 0), iota((rows, rows), 1)
    eye = sub == lane

    def to_col(row):
        return jnp.sum(jnp.where(eye, row, 0.0), axis=1, keepdims=True)

    def to_row(col):
        return jnp.sum(jnp.where(eye, col, 0.0), axis=0, keepdims=True)

    ids_col = to_col(ids_ref[...].astype(F32))
    lens_col = to_col(lens_ref[...].astype(F32))
    span = iota((rows, pool), 1).astype(F32)
    pos = jnp.sum(jnp.where(ids_col == span, slots_ref[...].astype(F32), 0.0), axis=1, keepdims=True)
    pos = pos.astype(I32)
    owner = lax.div(pos, adp_rows)
    slot = (pos - owner * adp_rows).astype(F32)
    key = lax.bitwise_xor(owner, me)
    pair = lax.div(key, 2)
    place = jnp.zeros_like(pair)
    for at, j in enumerate(seq):
        place = jnp.where(pair == j, at, place)
    place = (place * 2 + lax.rem(key, 2)).astype(F32)
    key = key.astype(F32)
    place_row = to_row(place)
    same = place_row == place
    before = same & (lane < sub)
    rank = jnp.sum(jnp.where(before, 1.0, 0.0), axis=1, keepdims=True)
    dest = jnp.sum(jnp.where((place_row < place) | before, 1.0, 0.0), axis=1, keepdims=True)
    dest_row, key_row, rank_row = to_row(dest), to_row(key), to_row(rank)

    def wide(col):
        return jnp.broadcast_to(col, (rows, 128)).astype(BF16)

    row_perm = one_hot(sub.astype(F32) == dest_row)
    ids = jnp.broadcast_to(lane[:1].astype(F32), (8, rows)).astype(BF16)
    row_ref[...] = dot_t(ids, row_perm)[:1].astype(I32)
    row_of, _ = token_place(iota((toks, rows), 0), steps)
    row_of = (row_of + lax.div(iota((toks, rows), 0), CAP * steps) * CAP).astype(F32)
    len_ref[...] = dot(one_hot(row_of == dest_row), wide(lens_col))
    n_pairs = len(seq)
    y = iota((n_pairs * 2 * CAP, rows), 0)
    y_key = (lax.div(y, 2 * CAP) * 2 + core).astype(F32)
    y_rank = (lax.rem(lax.div(y, CAP), 2) * SUB + lax.rem(y, SUB)).astype(F32)
    slot_ref[...] = dot(one_hot((y_key == key_row) & (y_rank == rank_row)), wide(slot)).astype(BF16)

    spread = one_hot(lax.div(iota((rows, toks), 1), steps) == iota((rows, toks), 0))
    info = jnp.concatenate([dest_row, key_row, rank_row] + [dest_row] * 5, axis=0).astype(BF16)
    info = dot(info, spread)
    dest_tok, key_tok, rank_tok = info[0:1], info[1:2], info[2:3]
    p, step_tok = iota((toks, toks), 0), lax.rem(iota((toks, toks), 1), steps)
    p_row, p_step = token_place(p, steps)
    p_row = (p_row + lax.div(p, CAP * steps) * CAP).astype(F32)
    perm = one_hot((p_row == dest_tok) & (p_step == step_tok))
    perm_ref[...] = perm
    n_send = n_pairs * CAP * steps
    p, step_tok = iota((n_send, toks), 0), lax.rem(iota((n_send, toks), 1), steps)
    p_row, p_step = token_place(p, steps)
    p_key = (lax.div(p, CAP * steps) * 2 + core).astype(F32)
    send_ref[...] = one_hot((p_key == key_tok) & (p_row.astype(F32) == rank_tok) & (p_step == step_tok))


def route(adp_rows, seq, steps, adapter_id, lengths, pool_slot):
    rows = adapter_id.shape[0]
    toks = rows * steps
    out = [
        jax.ShapeDtypeStruct((toks, toks), BF16),
        jax.ShapeDtypeStruct((len(seq) * CAP * steps, toks), BF16),
        jax.ShapeDtypeStruct((len(seq) * 2 * CAP, 128), BF16),
        jax.ShapeDtypeStruct((toks, 128), F32),
        jax.ShapeDtypeStruct((1, rows), I32),
    ]
    return pl.pallas_call(
        functools.partial(route_kernel, adp_rows, seq, steps),
        out_shape=out,
        in_specs=[VM] * 3,
        out_specs=[VM] * len(out),
        compiler_params=params(62),
        name="route",
    )(adapter_id[None, :], lengths[None, :], pool_slot[None, :])


def pack_kernel(n_tok, send_ref, slot_ref, tok_ref, oth_ref, *sends):
    rows, steps, width = tok_ref.shape
    for j in range(0, width, 512):
        for half, ref in enumerate((tok_ref, oth_ref)):
            part = ref[:, :, j : j + 512].reshape(rows * steps, 512)
            got = dot(send_ref[...], part).astype(BF16)
            for k, out in enumerate(sends):
                for c in range(4):
                    at = ((j // 128 + c) * 2 + half) * n_tok
                    out[at : at + n_tok, :] = got[k * n_tok : (k + 1) * n_tok, c * 128 : (c + 1) * 128]
    for k, out in enumerate(sends):
        out[width // 128 * 2 * n_tok :, :] = slot_ref[k * 2 * CAP : (k + 1) * 2 * CAP, :]


def pack(n_pairs, send, slot, tokens, other):
    _, steps, width = tokens.shape
    n_tok = steps * CAP
    out = [jax.ShapeDtypeStruct((width // 128 * 2 * n_tok + 2 * CAP, 128), BF16)] * n_pairs
    return pl.pallas_call(
        functools.partial(pack_kernel, n_tok),
        out_shape=out,
        in_specs=[VM] * 4,
        out_specs=[VM] * len(out),
        compiler_params=params(62),
        name="pack",
    )(send, slot, tokens, other)


def qkv_kernel(offsets, has_acc, steps, perm_ref, *refs):
    n_x = len(offsets)
    me = lax.axis_index("tp")
    xs, ws = refs[:n_x], refs[n_x : n_x + 3]
    at = n_x + 3
    accs = refs[at : at + 3] if has_acc else (None,) * 3
    at += 3 if has_acc else 0
    outs, raw, xbuf = refs[at : at + 3], refs[at + 3], refs[at + 4]
    bufs, xsem, wsem = refs[at + 5 : at + 8], refs[at + 8], refs[at + 9]
    rows, n_steps, width = xs[0].shape

    def x_copy(p):
        return pltpu.make_async_copy(xs[p], raw.at[p], xsem.at[p])

    def w_copy(n, i):
        lo, size = steps[n]
        shard = lax.bitwise_xor(me, offsets[lo // width])
        row = pl.multiple_of(shard * width + lo % width, 256)
        return pltpu.make_async_copy(ws[i].at[pl.ds(row, size)], bufs[i].at[lo : lo + size], wsem.at[n, i])

    def begin(n):
        if n < len(steps):
            if steps[n][0] % width == 0:
                x_copy(steps[n][0] // width).start()
            for i in range(3):
                w_copy(n, i).start()

    begin(0)
    begin(1)
    for n, (lo, size) in enumerate(steps):
        begin(n + 2)
        if lo % width == 0:
            p = lo // width
            x_copy(p).wait()
            for j in range(0, width, 512):
                part = raw[p, :, :, j : j + 512].reshape(rows * n_steps, 512)
                xbuf[:, lo + j : lo + j + 512] = dot(perm_ref[...], part).astype(BF16)
        for i in range(3):
            w_copy(n, i).wait()
        x = xbuf[:, lo : lo + size]
        for i in range(3):
            got = dot(x, bufs[i][lo : lo + size, :])
            if lo:
                outs[i][...] += got
            else:
                outs[i][...] = accs[i][...] + got if has_acc else got


def qkv(xs, perm, offsets, weights, acc):
    rows, steps, width = xs[0].shape
    m = rows * steps
    n_x = len(xs)
    has_acc = acc is not None
    outs = [jax.ShapeDtypeStruct((m, w.shape[1]), F32) for w in weights]
    cols = sum(w.shape[1] for w in weights)
    extra = list(acc) if has_acc else []
    depth = n_x * width
    plan, at = [], 0
    for size in FIRST_STEPS:
        plan.append((at, size))
        at += size
    while at < depth:
        plan.append((at, min(STEP, width - at % width)))
        at += plan[-1][1]
    return pl.pallas_call(
        functools.partial(qkv_kernel, tuple(offsets), has_acc, plan),
        out_shape=outs,
        in_specs=[VM] + [HBM] * (n_x + 3) + [VM] * len(extra),
        out_specs=[VM] * 3,
        scratch_shapes=[pltpu.VMEM((n_x, rows, steps, width), BF16), pltpu.VMEM((m, depth), BF16)]
        + [pltpu.VMEM((depth, w.shape[1]), BF16) for w in weights]
        + [pltpu.SemaphoreType.DMA((n_x,)), pltpu.SemaphoreType.DMA((len(plan), 3))],
        compiler_params=params(60.5),
        cost_estimate=QKV_COST,
        name="qkv",
    )(perm, *xs, *weights, *extra)


def panel_loads(srcs, dst, sem):
    size = dst.shape[1] // PARTS
    loads = []
    for i, src in enumerate(srcs):
        at = [pl.ds(p * size, size) for p in range(PARTS)]
        loads.append([pltpu.make_async_copy(src.at[a], dst.at[i, a], sem.at[i, p]) for p, a in enumerate(at)])
        for c in loads[-1]:
            c.start()
    return loads


def slot_mask(tiles, n_tok, cols, rank):
    tiles = tiles.astype(F32)
    rep = n_tok // (2 * CAP)
    slots = jnp.concatenate([tiles[:CAP]] * rep + [tiles[CAP:]] * rep, axis=0)
    slots = jnp.concatenate([slots] * (cols // 128), axis=1)
    return slots == lax.div(iota((n_tok, cols), 1), rank).astype(F32)


def mid_kernel(n_tok, rank, down_ref, oth_ref, *refs):
    ins, out_ref, x_ref, d_ref, sem = refs[:-4], refs[-4], refs[-3], refs[-2], refs[-1]
    _, cols, width = d_ref.shape
    loads = panel_loads((down_ref, oth_ref), d_ref, sem)
    for k, r in enumerate(ins):
        rows = slice(k * n_tok, (k + 1) * n_tok)
        for c in range(width // 128):
            for half in range(2):
                at = (c * 2 + half) * n_tok
                x_ref[half, rows, c * 128 : (c + 1) * 128] = r[at : at + n_tok, :]
    prod = 0.0
    for half in range(2):
        for c in loads[half]:
            c.wait()
        prod = prod + dot_t(x_ref[half], d_ref[half])
    for k, r in enumerate(ins):
        mask = slot_mask(r[r.shape[0] - 2 * CAP :, :], n_tok, cols, rank)
        part = jnp.where(mask, prod[k * n_tok : (k + 1) * n_tok], 0.0)
        tot = part[:, :128]
        for c in range(128, cols, 128):
            tot = tot + part[:, c : c + 128]
        out_ref[k * n_tok : (k + 1) * n_tok, :] = tot + pltpu.roll(tot, rank, 1)


def mid(recv, down, other, n_tok, rank):
    n = len(recv)
    cols, width = down.shape
    return pl.pallas_call(
        functools.partial(mid_kernel, n_tok, rank),
        out_shape=jax.ShapeDtypeStruct((n * n_tok, 128), F32),
        in_specs=[HBM] * 2 + [VM] * n,
        out_specs=VM,
        scratch_shapes=[
            pltpu.VMEM((2, n * n_tok, width), BF16),
            pltpu.VMEM((2, cols, width), BF16),
            pltpu.SemaphoreType.DMA((2, PARTS)),
        ],
        compiler_params=params(24),
        cost_estimate=COST,
        name="mid",
    )(down, other, *recv)


def up_kernel(n_tok, rank, n_recv, up_ref, oth_ref, a_ref, b_ref, *refs):
    ins, outs, u_ref, sem = refs[:n_recv], refs[n_recv : 2 * n_recv], refs[-2], refs[-1]
    _, cols, width = u_ref.shape
    loads = panel_loads((up_ref, oth_ref), u_ref, sem)
    total = (a_ref[...] + b_ref[...]).astype(BF16).astype(F32)
    spread = []
    for k in range(n_recv):
        both = jnp.concatenate([total[k * n_tok : (k + 1) * n_tok]] * (cols // 128), axis=1)
        mask = slot_mask(ins[k][...], n_tok, cols, rank)
        spread.append(jnp.where(mask, both, 0.0).astype(BF16))
    rows = jnp.concatenate(spread, axis=0)
    for half in range(2):
        for c in loads[half]:
            c.wait()
        for j in range(0, width, 512):
            got = dot(rows, u_ref[half, :, j : j + 512]).astype(BF16)
            for k in range(n_recv):
                outs[k][half * n_tok : (half + 1) * n_tok, j : j + 512] = got[k * n_tok : (k + 1) * n_tok]


def up(a, b, recv, up_rows, other, n_tok, rank):
    n = len(recv)
    cols, width = up_rows.shape
    last = recv[0].shape[0] // (2 * CAP) - 1
    tail = pl.BlockSpec((2 * CAP, 128), lambda i: (last, 0))

    def whole(x):
        return pl.BlockSpec(x.shape, lambda i: (0, 0))

    out = jax.ShapeDtypeStruct((2 * n_tok, width), BF16)
    return pl.pallas_call(
        functools.partial(up_kernel, n_tok, rank, n),
        out_shape=[out] * n,
        grid=(1,),
        in_specs=[HBM] * 2 + [whole(a), whole(b)] + [tail] * n,
        out_specs=[whole(out)] * n,
        scratch_shapes=[pltpu.VMEM((2, cols, width), BF16), pltpu.SemaphoreType.DMA((2, PARTS))],
        compiler_params=params(20),
        cost_estimate=COST,
        name="up",
    )(up_rows, other, a, b, *recv)


def make_attn_kernel(plan, steps, group, has_prev):
    nb = len(plan)
    halves = CAP // SUB
    n_tok = steps * CAP
    n_sub = steps * SUB
    n_q = group * n_sub

    def kernel(*refs):
        core_ref, rows_ref, q_hbm, k_hbm, v_hbm, tab_hbm, ck_ref, cv_ref = refs[:8]
        lora_refs = refs[8 : 8 + nb]
        at = 8 + nb + int(has_prev)
        out_ref, kbuf, vbuf, obuf, q_ref, k_ref, v_ref, tab_ref, loras, sem, osem = refs[at:]
        kv_local = k_ref.shape[1] // HD
        span = ck_ref.shape[1]
        scale = 1.0 / math.sqrt(HD)
        core = core_ref[0]
        blocks = [2 * j + (1 - core if other else core) for j, other in plan]

        def copies(b):
            at, to = pl.ds(pl.multiple_of(blocks[b] * n_tok, n_tok), n_tok), pl.ds(b * n_tok, n_tok)
            got = [
                pltpu.make_async_copy(src.at[at], dst.at[to], sem.at[b, n])
                for n, (src, dst) in enumerate(
                    ((q_hbm, q_ref), (k_hbm, k_ref), (v_hbm, v_ref), (tab_hbm, tab_ref))
                )
            ]
            part = pl.ds(n_tok if plan[b][1] else 0, n_tok)
            got.append(pltpu.make_async_copy(lora_refs[b].at[part], loras.at[b], sem.at[b, 4]))
            return got

        def begin(b):
            for i in range(CAP):
                r = rows_ref[0, blocks[b] * CAP + i]
                pltpu.make_async_copy(ck_ref.at[r], kbuf.at[b, i], sem.at[b, 5]).start()
                pltpu.make_async_copy(cv_ref.at[r], vbuf.at[b, i], sem.at[b, 6]).start()
            for c in copies(b):
                c.start()

        for b in range(min(AHEAD, nb)):
            begin(b)

        qi, ki = iota((n_sub, n_sub), 0), iota((n_sub, n_sub), 1)
        new_ok = (lax.rem(qi, SUB) == lax.rem(ki, SUB)) & (lax.div(qi, SUB) >= lax.div(ki, SUB))
        new_bias = jnp.concatenate([jnp.where(new_ok, 0.0, NEG)] * group, axis=0)
        col, sub = iota((CAP, SUB * span), 1), iota((CAP, SUB * span), 0)
        own = lax.div(col, span) == lax.rem(sub, SUB)
        at_pos = lax.rem(col, span).astype(F32)
        y, x = iota((n_tok, n_tok), 0), iota((n_tok, n_tok), 1)
        x_row, x_step = token_place(x, steps)
        turn = one_hot((lax.div(y, steps) == x_row) & (lax.rem(y, steps) == x_step))

        wide = group * HD
        for start in range(0, nb, TOGETHER):
            these = range(start, min(start + TOGETHER, nb))
            for b in these:
                if b + AHEAD < nb:
                    begin(b + AHEAD)
            for b in these:
                for c in copies(b):
                    c.wait()
                pltpu.make_async_copy(ck_ref.at[pl.ds(0, CAP)], kbuf.at[b], sem.at[b, 5]).wait()
                pltpu.make_async_copy(cv_ref.at[pl.ds(0, CAP)], vbuf.at[b], sem.at[b, 6]).wait()
            work = [(b, h, t) for b in these for h in range(kv_local) for t in range(halves)]
            biases, qs, kns, vns = {}, {}, {}, {}
            for b in these:
                rows = slice(b * n_tok, (b + 1) * n_tok)
                cos, sin = tab_ref[rows, :HD], tab_ref[rows, HD : 2 * HD]

                def rope(v):
                    return v * cos + pltpu.roll(v, HD // 2, 1) * sin

                for t in range(halves):
                    at = b * n_tok + t * n_sub
                    lens = tab_ref[at : at + CAP, 2 * HD :][:, :1]
                    bias = jnp.where(own & (at_pos < lens), 0.0, NEG)
                    biases[b, t] = jnp.concatenate([bias] * (n_q // CAP), axis=0)
                for h in range(kv_local):
                    hs = slice(h * HD, (h + 1) * HD)
                    heads = []
                    for g in range(group):
                        cs = slice((h * group + g) * HD, (h * group + g + 1) * HD)
                        heads.append(rope(q_ref[rows, cs] + loras[b, :, cs].astype(F32)).astype(BF16))
                    kn = rope(k_ref[rows, hs]).astype(BF16)
                    vn = v_ref[rows, hs].astype(BF16)
                    for t in range(halves):
                        ts = slice(t * n_sub, (t + 1) * n_sub)
                        qs[b, h, t] = jnp.concatenate([v[ts] for v in heads], axis=0)
                        kns[b, h, t], vns[b, h, t] = kn[ts], vn[ts]
            s1, s2 = {}, {}
            for w in work:
                b, h, t = w
                kc = kbuf[b, t * SUB : (t + 1) * SUB, :, h * HD : (h + 1) * HD].reshape(SUB * span, HD)
                s1[w] = dot_t(qs[w], kc) * scale + biases[b, t]
                s2[w] = dot_t(qs[w], kns[w]) * scale + new_bias
            p1, p2 = {}, {}
            for w in work:
                top = jnp.maximum(jnp.max(s1[w], axis=1, keepdims=True), jnp.max(s2[w], axis=1, keepdims=True))
                e1 = jnp.exp(s1[w] - top)
                e2 = jnp.exp(s2[w] - top)
                den = jnp.sum(e1, axis=1, keepdims=True) + jnp.sum(e2, axis=1, keepdims=True)
                inv = 1.0 / den
                p1[w], p2[w] = (e1 * inv).astype(BF16), (e2 * inv).astype(BF16)
            parts = {}
            for w in work:
                b, h, t = w
                vc = vbuf[b, t * SUB : (t + 1) * SUB, :, h * HD : (h + 1) * HD].reshape(SUB * span, HD)
                o = dot(p1[w], vc) + dot(p2[w], vns[w])
                o = o.astype(BF16)
                parts[w] = jnp.concatenate([o[g * n_sub : (g + 1) * n_sub] for g in range(group)], axis=1)
            for b in these:
                for h in range(kv_local):
                    both = jnp.concatenate([parts[b, h, t] for t in range(halves)], axis=0)
                    mixed = dot(turn, both).astype(BF16)
                    obuf[b, :, :, h * wide : (h + 1) * wide] = mixed.reshape(CAP, steps, wide)
                for i in range(CAP):
                    r = rows_ref[0, blocks[b] * CAP + i]
                    pltpu.make_async_copy(obuf.at[b, i], out_ref.at[r], osem).start()
        for b in range(nb):
            pltpu.make_async_copy(obuf.at[b], out_ref.at[pl.ds(0, CAP)], osem).wait()

    return kernel


def attention(plan, steps, core, rows, q, k, v, table, ck, cv, loras, prev):
    n_rows = ck.shape[0]
    nb = len(plan)
    n = nb * CAP * steps
    group = q.shape[1] // k.shape[1]
    buf = (nb, CAP) + ck.shape[1:]
    extra = [] if prev is None else [prev]
    return pl.pallas_call(
        make_attn_kernel(plan, steps, group, bool(extra)),
        out_shape=jax.ShapeDtypeStruct((n_rows, steps, q.shape[1]), BF16),
        in_specs=[SM, SM] + [HBM] * (6 + nb + len(extra)),
        out_specs=HBM,
        scratch_shapes=[
            pltpu.VMEM(buf, BF16),
            pltpu.VMEM(buf, BF16),
            pltpu.VMEM((nb, CAP, steps, q.shape[1]), BF16),
            pltpu.VMEM((n, q.shape[1]), F32),
            pltpu.VMEM((n, k.shape[1]), F32),
            pltpu.VMEM((n, v.shape[1]), F32),
            pltpu.VMEM((n, table.shape[1]), F32),
            pltpu.VMEM((nb, CAP * steps, q.shape[1]), BF16),
            pltpu.SemaphoreType.DMA((nb, 7)),
            pltpu.SemaphoreType.DMA,
        ],
        input_output_aliases={8 + nb: 0} if extra else {},
        compiler_params=params(62),
        cost_estimate=TINY,
        name="attn",
    )(core, rows, q, k, v, table, ck, cv, *loras, *extra)


def swap(x, n, bit):
    return lax.ppermute(x, "tp", [(i, i ^ bit) for i in range(n)])


def after(x, *deps):
    return lax.optimization_barrier((x, *deps))[0]


def body(
    tokens,
    adapter_id,
    pool_slot,
    lengths,
    w_query,
    w_key,
    w_value,
    pooled_down_weights,
    pool_up,
    cache_key,
    cache_value,
):
    n_grp = lax.axis_size("grp")
    n_tp = lax.axis_size("tp")
    row_count, steps, width = tokens.shape
    adp_rows, _, rank = pooled_down_weights.shape
    n_tok = steps * CAP
    n_blocks = row_count // CAP
    n_pairs = n_grp // 2
    seq = [*range(n_pairs // 2, n_pairs), *range(n_pairs // 2)]
    me = lax.axis_index("tp")
    core = lax.rem(me, 2)

    def cross(x, j):
        perm = [
            (g * n_tp + t, (g ^ (2 * j + t % 2)) * n_tp + t)
            for g in range(n_grp)
            for t in range(n_tp)
        ]
        return lax.ppermute(x, ("grp", "tp"), perm)

    other_tokens = swap(tokens, n_tp, 1)
    perm, send, slot, lens, rows = route(adp_rows, seq, steps, adapter_id, lengths, pool_slot)
    sends = pack(n_pairs, send, slot, tokens, other_tokens)
    recv = {j: cross(sends[j], j) for j in seq}

    first = recv[0]
    up_rows = after(pool_up, sends[0]).reshape(adp_rows * rank, pool_up.shape[2])
    up_other = swap(up_rows, n_tp, 1)
    down = jnp.swapaxes(after(pooled_down_weights, sends[0]), 1, 2).reshape(adp_rows * rank, width)
    down_other = swap(down, n_tp, 1)

    weights = (w_query, w_key, w_value)

    ready = after(perm, up_other, down_other)
    acc = qkv([tokens, other_tokens], ready, [0, 1], weights, None)
    pieces = {0: after(tokens, sends[0])}
    bit = n_tp // 2
    while bit > 1:
        pieces.update({off ^ bit: swap(p, n_tp, bit) for off, p in list(pieces.items())})
        bit //= 2
    far = [o for o in sorted(pieces) if o]

    half = HD // 2
    inv_freq = jnp.exp(jnp.arange(half, dtype=F32) * (-2.0 * math.log(ROPE_BASE) / HD))
    inv_freq = jnp.concatenate([inv_freq, inv_freq])
    step_of = jnp.tile(jnp.repeat(jnp.arange(steps, dtype=F32), SUB), row_count // SUB)
    lens = after(lens, first)
    angles = (lens + step_of[:, None]) * inv_freq
    sign = jnp.where(jnp.arange(HD) < half, -1.0, 1.0).astype(F32)
    table = jnp.concatenate([jnp.cos(angles), jnp.sin(angles) * sign, lens], axis=1)

    got = [recv[j] for j in seq]
    got, acc, table = lax.optimization_barrier((got, acc, table))
    part = mid(got, down, down_other, n_tok, rank)
    bit = 2
    while bit < n_tp // 2:
        part = part + swap(part, n_tp, bit)
        bit *= 2
    sent = up(part, swap(part, n_tp, bit), got, up_rows, up_other, n_tok, rank)
    back = {j: cross(x, j) for j, x in zip(seq, sent)}
    late = {}
    for o in far:
        x = after(pieces[o], sent[0])
        late[o] = x
        late[o ^ 1] = swap(x, n_tp, 1)
    offsets = sorted(late)
    ready = after(perm, back[0])
    q, k, v = qkv([late[o] for o in offsets], ready, offsets, weights, acc)

    def attend(plan, loras, core_id, prev):
        return attention(
            plan, steps, core_id, rows, q, k, v, table, cache_key, cache_value, loras, prev
        )

    if n_grp == n_blocks:
        core_id = core.astype(I32).reshape(1)
        own = {j: after(back[j], q) for j in seq}
        other = {j: swap(own[j], n_tp, 1) for j in seq}
        plan = [(j, o) for j in seq for o in (False, True)]
        placed = [(seq.index(j), o) for j, o in plan]
        return attend(placed, [(other if o else own)[j] for j, o in plan], core_id, None)

    pairs = [(back[j], swap(back[j], n_tp, 1)) for j in seq]
    mine_all = jnp.stack([a[:n_tok] for a, _ in pairs])
    other_all = jnp.stack([a[n_tok:] for _, a in pairs])
    even = jnp.where(core == 0, mine_all, other_all)
    odd = jnp.where(core == 0, other_all, mine_all)
    full = jnp.stack([even, odd], axis=1).reshape(n_grp, n_tok, even.shape[2])
    span = jnp.arange(pool_slot.shape[0], dtype=I32)
    pos = jnp.sum(jnp.where(adapter_id[:, None] == span[None, :], pool_slot[None, :], 0), axis=1)
    key = lax.bitwise_xor(lax.div(pos, adp_rows), lax.axis_index("grp"))
    order = jnp.array([2 * j + c for j in seq for c in (0, 1)], I32)
    used = jnp.any(key[:, None] == order[None, :], axis=0)
    at = jnp.cumsum(used.astype(I32)) - 1
    pick = (at[None, :] == jnp.arange(n_blocks)[:, None]) & used[None, :]
    chosen = full[jnp.sum(jnp.where(pick, jnp.arange(n_grp)[None, :], 0), axis=1)]
    twice = jnp.concatenate([chosen, chosen], axis=1)
    plan = [(b // 2, b % 2 == 1) for b in range(n_blocks)]
    return attend(plan, [twice[b] for b in range(n_blocks)], jnp.zeros((1,), I32), None)


def solution(mesh):
    in_specs = (
        P("grp", None, "tp"),
        P("grp"),
        P(),
        P("grp"),
        P(None, "tp"),
        P(None, "tp"),
        P(None, "tp"),
        P("grp", "tp", None),
        P("grp", None, "tp"),
        P("grp", None, "tp"),
        P("grp", None, "tp"),
    )
    out_specs = P("grp", None, "tp")
    return jax.shard_map(body, mesh=mesh, in_specs=in_specs, out_specs=out_specs, check_vma=False)
```

```python
import functools
import math

import jax
import jax.numpy as jnp
from jax import lax
from jax.experimental import pallas as pl
from jax.experimental.pallas import tpu as pltpu
from jax.sharding import PartitionSpec as P

HD = 128
CAP = 8
SUB = 4
ROPE_BASE = 500000.0
NEG = -1e30
MIB = 1024 * 1024
F32 = jnp.float32
BF16 = jnp.bfloat16
I32 = jnp.int32
FIRST_STEPS = (256, 256)
STEP = 512
PARTS = 4
AHEAD = 4
TOGETHER = 2

TINY = pl.CostEstimate(flops=1, bytes_accessed=1, transcendentals=0)
QKV_COST = pl.CostEstimate(flops=10**11, bytes_accessed=3 * 10**8, transcendentals=0)
COST = pl.CostEstimate(flops=10**10, bytes_accessed=3 * 10**7, transcendentals=0)
VM = pl.BlockSpec(memory_space=pltpu.VMEM)
SM = pl.BlockSpec(memory_space=pltpu.SMEM)
HBM = pl.BlockSpec(memory_space=pltpu.HBM)


def params(mib):
    return pltpu.CompilerParams(vmem_limit_bytes=int(mib * MIB))


def dot(a, b):
    return jnp.dot(a, b, preferred_element_type=F32)


def dot_t(a, b):
    return lax.dot_general(a, b, (((1,), (1,)), ((), ())), preferred_element_type=F32)


def iota(shape, dim):
    return lax.broadcasted_iota(I32, shape, dim)


def one_hot(cond):
    return jnp.where(cond, 1.0, 0.0).astype(BF16)


def token_place(p, steps):
    n_sub = SUB * steps
    half = lax.rem(lax.div(p, n_sub), CAP // SUB)
    return half * SUB + lax.rem(p, SUB), lax.rem(lax.div(p, SUB), steps)


def route_kernel(adp_rows, seq, steps, ids_ref, lens_ref, slots_ref, *outs):
    perm_ref, send_ref, slot_ref, len_ref, row_ref = outs
    rows = ids_ref.shape[1]
    pool = slots_ref.shape[1]
    toks = rows * steps
    me = lax.axis_index("grp")
    core = lax.rem(lax.axis_index("tp"), 2)
    sub, lane = iota((rows, rows), 0), iota((rows, rows), 1)
    eye = sub == lane

    def to_col(row):
        return jnp.sum(jnp.where(eye, row, 0.0), axis=1, keepdims=True)

    def to_row(col):
        return jnp.sum(jnp.where(eye, col, 0.0), axis=0, keepdims=True)

    ids_col = to_col(ids_ref[...].astype(F32))
    lens_col = to_col(lens_ref[...].astype(F32))
    span = iota((rows, pool), 1).astype(F32)
    pos = jnp.sum(jnp.where(ids_col == span, slots_ref[...].astype(F32), 0.0), axis=1, keepdims=True)
    pos = pos.astype(I32)
    owner = lax.div(pos, adp_rows)
    slot = (pos - owner * adp_rows).astype(F32)
    key = lax.bitwise_xor(owner, me)
    pair = lax.div(key, 2)
    place = jnp.zeros_like(pair)
    for at, j in enumerate(seq):
        place = jnp.where(pair == j, at, place)
    place = (place * 2 + lax.rem(key, 2)).astype(F32)
    key = key.astype(F32)
    place_row = to_row(place)
    same = place_row == place
    before = same & (lane < sub)
    rank = jnp.sum(jnp.where(before, 1.0, 0.0), axis=1, keepdims=True)
    dest = jnp.sum(jnp.where((place_row < place) | before, 1.0, 0.0), axis=1, keepdims=True)
    dest_row, key_row, rank_row = to_row(dest), to_row(key), to_row(rank)

    def wide(col):
        return jnp.broadcast_to(col, (rows, 128)).astype(BF16)

    row_perm = one_hot(sub.astype(F32) == dest_row)
    ids = jnp.broadcast_to(lane[:1].astype(F32), (8, rows)).astype(BF16)
    row_ref[...] = dot_t(ids, row_perm)[:1].astype(I32)
    row_of, _ = token_place(iota((toks, rows), 0), steps)
    row_of = (row_of + lax.div(iota((toks, rows), 0), CAP * steps) * CAP).astype(F32)
    len_ref[...] = dot(one_hot(row_of == dest_row), wide(lens_col))
    n_pairs = len(seq)
    y = iota((n_pairs * 2 * CAP, rows), 0)
    y_key = (lax.div(y, 2 * CAP) * 2 + core).astype(F32)
    y_rank = (lax.rem(lax.div(y, CAP), 2) * SUB + lax.rem(y, SUB)).astype(F32)
    slot_ref[...] = dot(one_hot((y_key == key_row) & (y_rank == rank_row)), wide(slot)).astype(BF16)

    spread = one_hot(lax.div(iota((rows, toks), 1), steps) == iota((rows, toks), 0))
    info = jnp.concatenate([dest_row, key_row, rank_row] + [dest_row] * 5, axis=0).astype(BF16)
    info = dot(info, spread)
    dest_tok, key_tok, rank_tok = info[0:1], info[1:2], info[2:3]
    p, step_tok = iota((toks, toks), 0), lax.rem(iota((toks, toks), 1), steps)
    p_row, p_step = token_place(p, steps)
    p_row = (p_row + lax.div(p, CAP * steps) * CAP).astype(F32)
    perm = one_hot((p_row == dest_tok) & (p_step == step_tok))
    perm_ref[...] = perm
    n_send = n_pairs * CAP * steps
    p, step_tok = iota((n_send, toks), 0), lax.rem(iota((n_send, toks), 1), steps)
    p_row, p_step = token_place(p, steps)
    p_key = (lax.div(p, CAP * steps) * 2 + core).astype(F32)
    send_ref[...] = one_hot((p_key == key_tok) & (p_row.astype(F32) == rank_tok) & (p_step == step_tok))


def route(adp_rows, seq, steps, adapter_id, lengths, pool_slot):
    rows = adapter_id.shape[0]
    toks = rows * steps
    out = [
        jax.ShapeDtypeStruct((toks, toks), BF16),
        jax.ShapeDtypeStruct((len(seq) * CAP * steps, toks), BF16),
        jax.ShapeDtypeStruct((len(seq) * 2 * CAP, 128), BF16),
        jax.ShapeDtypeStruct((toks, 128), F32),
        jax.ShapeDtypeStruct((1, rows), I32),
    ]
    return pl.pallas_call(
        functools.partial(route_kernel, adp_rows, seq, steps),
        out_shape=out,
        in_specs=[VM] * 3,
        out_specs=[VM] * len(out),
        compiler_params=params(62),
        name="route",
    )(adapter_id[None, :], lengths[None, :], pool_slot[None, :])


def pack_kernel(n_tok, send_ref, slot_ref, tok_ref, oth_ref, *sends):
    rows, steps, width = tok_ref.shape
    for j in range(0, width, 512):
        for half, ref in enumerate((tok_ref, oth_ref)):
            part = ref[:, :, j : j + 512].reshape(rows * steps, 512)
            got = dot(send_ref[...], part).astype(BF16)
            for k, out in enumerate(sends):
                for c in range(4):
                    at = ((j // 128 + c) * 2 + half) * n_tok
                    out[at : at + n_tok, :] = got[k * n_tok : (k + 1) * n_tok, c * 128 : (c + 1) * 128]
    for k, out in enumerate(sends):
        out[width // 128 * 2 * n_tok :, :] = slot_ref[k * 2 * CAP : (k + 1) * 2 * CAP, :]


def pack(n_pairs, send, slot, tokens, other):
    _, steps, width = tokens.shape
    n_tok = steps * CAP
    out = [jax.ShapeDtypeStruct((width // 128 * 2 * n_tok + 2 * CAP, 128), BF16)] * n_pairs
    return pl.pallas_call(
        functools.partial(pack_kernel, n_tok),
        out_shape=out,
        in_specs=[VM] * 4,
        out_specs=[VM] * len(out),
        compiler_params=params(62),
        name="pack",
    )(send, slot, tokens, other)


def qkv_kernel(offsets, has_acc, steps, perm_ref, *refs):
    n_x = len(offsets)
    me = lax.axis_index("tp")
    xs, ws = refs[:n_x], refs[n_x : n_x + 3]
    at = n_x + 3
    accs = refs[at : at + 3] if has_acc else (None,) * 3
    at += 3 if has_acc else 0
    outs, raw, xbuf = refs[at : at + 3], refs[at + 3], refs[at + 4]
    bufs, xsem, wsem = refs[at + 5 : at + 8], refs[at + 8], refs[at + 9]
    rows, n_steps, width = xs[0].shape

    def x_copy(p):
        return pltpu.make_async_copy(xs[p], raw.at[p], xsem.at[p])

    def w_copy(n, i):
        lo, size = steps[n]
        shard = lax.bitwise_xor(me, offsets[lo // width])
        row = pl.multiple_of(shard * width + lo % width, 256)
        return pltpu.make_async_copy(ws[i].at[pl.ds(row, size)], bufs[i].at[lo : lo + size], wsem.at[n, i])

    def begin(n):
        if n < len(steps):
            if steps[n][0] % width == 0:
                x_copy(steps[n][0] // width).start()
            for i in range(3):
                w_copy(n, i).start()

    begin(0)
    begin(1)
    for n, (lo, size) in enumerate(steps):
        begin(n + 2)
        if lo % width == 0:
            p = lo // width
            x_copy(p).wait()
            for j in range(0, width, 512):
                part = raw[p, :, :, j : j + 512].reshape(rows * n_steps, 512)
                xbuf[:, lo + j : lo + j + 512] = dot(perm_ref[...], part).astype(BF16)
        for i in range(3):
            w_copy(n, i).wait()
        x = xbuf[:, lo : lo + size]
        for i in range(3):
            got = dot(x, bufs[i][lo : lo + size, :])
            if lo:
                outs[i][...] += got
            else:
                outs[i][...] = accs[i][...] + got if has_acc else got


def qkv(xs, perm, offsets, weights, acc):
    rows, steps, width = xs[0].shape
    m = rows * steps
    n_x = len(xs)
    has_acc = acc is not None
    outs = [jax.ShapeDtypeStruct((m, w.shape[1]), F32) for w in weights]
    cols = sum(w.shape[1] for w in weights)
    extra = list(acc) if has_acc else []
    depth = n_x * width
    plan, at = [], 0
    for size in FIRST_STEPS:
        plan.append((at, size))
        at += size
    while at < depth:
        plan.append((at, min(STEP, width - at % width)))
        at += plan[-1][1]
    return pl.pallas_call(
        functools.partial(qkv_kernel, tuple(offsets), has_acc, plan),
        out_shape=outs,
        in_specs=[VM] + [HBM] * (n_x + 3) + [VM] * len(extra),
        out_specs=[VM] * 3,
        scratch_shapes=[pltpu.VMEM((n_x, rows, steps, width), BF16), pltpu.VMEM((m, depth), BF16)]
        + [pltpu.VMEM((depth, w.shape[1]), BF16) for w in weights]
        + [pltpu.SemaphoreType.DMA((n_x,)), pltpu.SemaphoreType.DMA((len(plan), 3))],
        compiler_params=params(60.5),
        cost_estimate=QKV_COST,
        name="qkv",
    )(perm, *xs, *weights, *extra)


def panel_loads(srcs, dst, sem):
    size = dst.shape[1] // PARTS
    loads = []
    for i, src in enumerate(srcs):
        at = [pl.ds(p * size, size) for p in range(PARTS)]
        loads.append([pltpu.make_async_copy(src.at[a], dst.at[i, a], sem.at[i, p]) for p, a in enumerate(at)])
        for c in loads[-1]:
            c.start()
    return loads


def slot_mask(tiles, n_tok, cols, rank):
    tiles = tiles.astype(F32)
    rep = n_tok // (2 * CAP)
    slots = jnp.concatenate([tiles[:CAP]] * rep + [tiles[CAP:]] * rep, axis=0)
    slots = jnp.concatenate([slots] * (cols // 128), axis=1)
    return slots == lax.div(iota((n_tok, cols), 1), rank).astype(F32)


def mid_kernel(n_tok, rank, down_ref, oth_ref, *refs):
    ins, out_ref, x_ref, d_ref, sem = refs[:-4], refs[-4], refs[-3], refs[-2], refs[-1]
    _, cols, width = d_ref.shape
    loads = panel_loads((down_ref, oth_ref), d_ref, sem)
    for k, r in enumerate(ins):
        rows = slice(k * n_tok, (k + 1) * n_tok)
        for c in range(width // 128):
            for half in range(2):
                at = (c * 2 + half) * n_tok
                x_ref[half, rows, c * 128 : (c + 1) * 128] = r[at : at + n_tok, :]
    prod = 0.0
    for half in range(2):
        for c in loads[half]:
            c.wait()
        prod = prod + dot_t(d_ref[half], x_ref[half])
    prod = jnp.transpose(prod)
    for k, r in enumerate(ins):
        mask = slot_mask(r[r.shape[0] - 2 * CAP :, :], n_tok, cols, rank)
        part = jnp.where(mask, prod[k * n_tok : (k + 1) * n_tok], 0.0)
        tot = part[:, :128]
        for c in range(128, cols, 128):
            tot = tot + part[:, c : c + 128]
        out_ref[k * n_tok : (k + 1) * n_tok, :] = tot + pltpu.roll(tot, rank, 1)


def mid(recv, down, other, n_tok, rank):
    n = len(recv)
    cols, width = down.shape
    return pl.pallas_call(
        functools.partial(mid_kernel, n_tok, rank),
        out_shape=jax.ShapeDtypeStruct((n * n_tok, 128), F32),
        in_specs=[HBM] * 2 + [VM] * n,
        out_specs=VM,
        scratch_shapes=[
            pltpu.VMEM((2, n * n_tok, width), BF16),
            pltpu.VMEM((2, cols, width), BF16),
            pltpu.SemaphoreType.DMA((2, PARTS)),
        ],
        compiler_params=params(24),
        cost_estimate=COST,
        name="mid",
    )(down, other, *recv)


def up_kernel(n_tok, rank, n_recv, up_ref, oth_ref, a_ref, b_ref, *refs):
    ins, outs, u_ref, sem = refs[:n_recv], refs[n_recv : 2 * n_recv], refs[-2], refs[-1]
    _, cols, width = u_ref.shape
    loads = panel_loads((up_ref, oth_ref), u_ref, sem)
    total = (a_ref[...] + b_ref[...]).astype(BF16).astype(F32)
    spread = []
    for k in range(n_recv):
        both = jnp.concatenate([total[k * n_tok : (k + 1) * n_tok]] * (cols // 128), axis=1)
        mask = slot_mask(ins[k][...], n_tok, cols, rank)
        spread.append(jnp.where(mask, both, 0.0).astype(BF16))
    rows = jnp.concatenate(spread, axis=0)
    for half in range(2):
        for c in loads[half]:
            c.wait()
        for j in range(0, width, 512):
            got = dot(rows, u_ref[half, :, j : j + 512]).astype(BF16)
            for k in range(n_recv):
                outs[k][half * n_tok : (half + 1) * n_tok, j : j + 512] = got[k * n_tok : (k + 1) * n_tok]


def up(a, b, recv, up_rows, other, n_tok, rank):
    n = len(recv)
    cols, width = up_rows.shape
    last = recv[0].shape[0] // (2 * CAP) - 1
    tail = pl.BlockSpec((2 * CAP, 128), lambda i: (last, 0))

    def whole(x):
        return pl.BlockSpec(x.shape, lambda i: (0, 0))

    out = jax.ShapeDtypeStruct((2 * n_tok, width), BF16)
    return pl.pallas_call(
        functools.partial(up_kernel, n_tok, rank, n),
        out_shape=[out] * n,
        grid=(1,),
        in_specs=[HBM] * 2 + [whole(a), whole(b)] + [tail] * n,
        out_specs=[whole(out)] * n,
        scratch_shapes=[pltpu.VMEM((2, cols, width), BF16), pltpu.SemaphoreType.DMA((2, PARTS))],
        compiler_params=params(20),
        cost_estimate=COST,
        name="up",
    )(up_rows, other, a, b, *recv)


def make_attn_kernel(plan, steps, group, has_prev):
    nb = len(plan)
    halves = CAP // SUB
    n_tok = steps * CAP
    n_sub = steps * SUB
    n_q = group * n_sub

    def kernel(*refs):
        core_ref, rows_ref, q_hbm, k_hbm, v_hbm, tab_hbm, ck_ref, cv_ref = refs[:8]
        lora_refs = refs[8 : 8 + nb]
        at = 8 + nb + int(has_prev)
        out_ref, kbuf, vbuf, obuf, q_ref, k_ref, v_ref, tab_ref, loras, sem, osem = refs[at:]
        kv_local = k_ref.shape[1] // HD
        span = ck_ref.shape[1]
        scale = 1.0 / math.sqrt(HD)
        core = core_ref[0]
        blocks = [2 * j + (1 - core if other else core) for j, other in plan]

        def copies(b):
            at, to = pl.ds(pl.multiple_of(blocks[b] * n_tok, n_tok), n_tok), pl.ds(b * n_tok, n_tok)
            got = [
                pltpu.make_async_copy(src.at[at], dst.at[to], sem.at[b, n])
                for n, (src, dst) in enumerate(
                    ((q_hbm, q_ref), (k_hbm, k_ref), (v_hbm, v_ref), (tab_hbm, tab_ref))
                )
            ]
            part = pl.ds(n_tok if plan[b][1] else 0, n_tok)
            got.append(pltpu.make_async_copy(lora_refs[b].at[part], loras.at[b], sem.at[b, 4]))
            return got

        def begin(b):
            for i in range(CAP):
                r = rows_ref[0, blocks[b] * CAP + i]
                pltpu.make_async_copy(ck_ref.at[r], kbuf.at[b, i], sem.at[b, 5]).start()
                pltpu.make_async_copy(cv_ref.at[r], vbuf.at[b, i], sem.at[b, 6]).start()
            for c in copies(b):
                c.start()

        for b in range(min(AHEAD, nb)):
            begin(b)

        qi, ki = iota((n_sub, n_sub), 0), iota((n_sub, n_sub), 1)
        new_ok = (lax.rem(qi, SUB) == lax.rem(ki, SUB)) & (lax.div(qi, SUB) >= lax.div(ki, SUB))
        new_bias = jnp.concatenate([jnp.where(new_ok, 0.0, NEG)] * group, axis=0)
        col, sub = iota((CAP, SUB * span), 1), iota((CAP, SUB * span), 0)
        own = lax.div(col, span) == lax.rem(sub, SUB)
        at_pos = lax.rem(col, span).astype(F32)
        y, x = iota((n_tok, n_tok), 0), iota((n_tok, n_tok), 1)
        x_row, x_step = token_place(x, steps)
        turn = one_hot((lax.div(y, steps) == x_row) & (lax.rem(y, steps) == x_step))

        wide = group * HD
        for start in range(0, nb, TOGETHER):
            these = range(start, min(start + TOGETHER, nb))
            for b in these:
                if b + AHEAD < nb:
                    begin(b + AHEAD)
            for b in these:
                for c in copies(b):
                    c.wait()
                pltpu.make_async_copy(ck_ref.at[pl.ds(0, CAP)], kbuf.at[b], sem.at[b, 5]).wait()
                pltpu.make_async_copy(cv_ref.at[pl.ds(0, CAP)], vbuf.at[b], sem.at[b, 6]).wait()
            work = [(b, h, t) for b in these for h in range(kv_local) for t in range(halves)]
            biases, qs, kns, vns = {}, {}, {}, {}
            for b in these:
                rows = slice(b * n_tok, (b + 1) * n_tok)
                cos, sin = tab_ref[rows, :HD], tab_ref[rows, HD : 2 * HD]

                def rope(v):
                    return v * cos + pltpu.roll(v, HD // 2, 1) * sin

                for t in range(halves):
                    at = b * n_tok + t * n_sub
                    lens = tab_ref[at : at + CAP, 2 * HD :][:, :1]
                    bias = jnp.where(own & (at_pos < lens), 0.0, NEG)
                    biases[b, t] = jnp.concatenate([bias] * (n_q // CAP), axis=0)
                for h in range(kv_local):
                    hs = slice(h * HD, (h + 1) * HD)
                    heads = []
                    for g in range(group):
                        cs = slice((h * group + g) * HD, (h * group + g + 1) * HD)
                        heads.append(rope(q_ref[rows, cs] + loras[b, :, cs].astype(F32)).astype(BF16))
                    kn = rope(k_ref[rows, hs]).astype(BF16)
                    vn = v_ref[rows, hs].astype(BF16)
                    for t in range(halves):
                        ts = slice(t * n_sub, (t + 1) * n_sub)
                        qs[b, h, t] = jnp.concatenate([v[ts] for v in heads], axis=0)
                        kns[b, h, t], vns[b, h, t] = kn[ts], vn[ts]
            s1, s2 = {}, {}
            for w in work:
                b, h, t = w
                kc = kbuf[b, t * SUB : (t + 1) * SUB, :, h * HD : (h + 1) * HD].reshape(SUB * span, HD)
                s1[w] = dot_t(qs[w], kc) * scale + biases[b, t]
                s2[w] = dot_t(qs[w], kns[w]) * scale + new_bias
            p1, p2 = {}, {}
            for w in work:
                top = jnp.maximum(jnp.max(s1[w], axis=1, keepdims=True), jnp.max(s2[w], axis=1, keepdims=True))
                e1 = jnp.exp(s1[w] - top)
                e2 = jnp.exp(s2[w] - top)
                den = jnp.sum(e1, axis=1, keepdims=True) + jnp.sum(e2, axis=1, keepdims=True)
                inv = 1.0 / den
                p1[w], p2[w] = (e1 * inv).astype(BF16), (e2 * inv).astype(BF16)
            parts = {}
            for w in work:
                b, h, t = w
                vc = vbuf[b, t * SUB : (t + 1) * SUB, :, h * HD : (h + 1) * HD].reshape(SUB * span, HD)
                o = dot(p1[w], vc) + dot(p2[w], vns[w])
                o = o.astype(BF16)
                parts[w] = jnp.concatenate([o[g * n_sub : (g + 1) * n_sub] for g in range(group)], axis=1)
            for b in these:
                for h in range(kv_local):
                    both = jnp.concatenate([parts[b, h, t] for t in range(halves)], axis=0)
                    mixed = dot(turn, both).astype(BF16)
                    obuf[b, :, :, h * wide : (h + 1) * wide] = mixed.reshape(CAP, steps, wide)
                for i in range(CAP):
                    r = rows_ref[0, blocks[b] * CAP + i]
                    pltpu.make_async_copy(obuf.at[b, i], out_ref.at[r], osem).start()
        for b in range(nb):
            pltpu.make_async_copy(obuf.at[b], out_ref.at[pl.ds(0, CAP)], osem).wait()

    return kernel


def attention(plan, steps, core, rows, q, k, v, table, ck, cv, loras, prev):
    n_rows = ck.shape[0]
    nb = len(plan)
    n = nb * CAP * steps
    group = q.shape[1] // k.shape[1]
    buf = (nb, CAP) + ck.shape[1:]
    extra = [] if prev is None else [prev]
    return pl.pallas_call(
        make_attn_kernel(plan, steps, group, bool(extra)),
        out_shape=jax.ShapeDtypeStruct((n_rows, steps, q.shape[1]), BF16),
        in_specs=[SM, SM] + [HBM] * (6 + nb + len(extra)),
        out_specs=HBM,
        scratch_shapes=[
            pltpu.VMEM(buf, BF16),
            pltpu.VMEM(buf, BF16),
            pltpu.VMEM((nb, CAP, steps, q.shape[1]), BF16),
            pltpu.VMEM((n, q.shape[1]), F32),
            pltpu.VMEM((n, k.shape[1]), F32),
            pltpu.VMEM((n, v.shape[1]), F32),
            pltpu.VMEM((n, table.shape[1]), F32),
            pltpu.VMEM((nb, CAP * steps, q.shape[1]), BF16),
            pltpu.SemaphoreType.DMA((nb, 7)),
            pltpu.SemaphoreType.DMA,
        ],
        input_output_aliases={8 + nb: 0} if extra else {},
        compiler_params=params(62),
        cost_estimate=TINY,
        name="attn",
    )(core, rows, q, k, v, table, ck, cv, *loras, *extra)


def swap(x, n, bit):
    return lax.ppermute(x, "tp", [(i, i ^ bit) for i in range(n)])


def after(x, *deps):
    return lax.optimization_barrier((x, *deps))[0]


def body(
    tokens,
    adapter_id,
    pool_slot,
    lengths,
    w_query,
    w_key,
    w_value,
    pooled_down_weights,
    pool_up,
    cache_key,
    cache_value,
):
    n_grp = lax.axis_size("grp")
    n_tp = lax.axis_size("tp")
    row_count, steps, width = tokens.shape
    adp_rows, _, rank = pooled_down_weights.shape
    n_tok = steps * CAP
    n_blocks = row_count // CAP
    n_pairs = n_grp // 2
    seq = [*range(n_pairs // 2, n_pairs), *reversed(range(n_pairs // 2))]
    me = lax.axis_index("tp")
    core = lax.rem(me, 2)

    def cross(x, j):
        perm = [
            (g * n_tp + t, (g ^ (2 * j + t % 2)) * n_tp + t)
            for g in range(n_grp)
            for t in range(n_tp)
        ]
        return lax.ppermute(x, ("grp", "tp"), perm)

    other_tokens = swap(tokens, n_tp, 1)
    perm, send, slot, lens, rows = route(adp_rows, seq, steps, adapter_id, lengths, pool_slot)
    sends = pack(n_pairs, send, slot, tokens, other_tokens)
    recv = {j: cross(sends[j], j) for j in seq}

    first = recv[0]
    up_rows = after(pool_up, sends[0]).reshape(adp_rows * rank, pool_up.shape[2])
    up_other = swap(up_rows, n_tp, 1)
    down = jnp.swapaxes(after(pooled_down_weights, sends[0]), 1, 2).reshape(adp_rows * rank, width)
    down_other = swap(down, n_tp, 1)

    weights = (w_query, w_key, w_value)

    ready = after(perm, up_other, down_other)
    acc = qkv([tokens, other_tokens], ready, [0, 1], weights, None)
    pieces = {0: after(tokens, sends[0])}
    bit = n_tp // 2
    while bit > 1:
        pieces.update({off ^ bit: swap(p, n_tp, bit) for off, p in list(pieces.items())})
        bit //= 2
    far = [o for o in sorted(pieces) if o]

    half = HD // 2
    inv_freq = jnp.exp(jnp.arange(half, dtype=F32) * (-2.0 * math.log(ROPE_BASE) / HD))
    inv_freq = jnp.concatenate([inv_freq, inv_freq])
    step_of = jnp.tile(jnp.repeat(jnp.arange(steps, dtype=F32), SUB), row_count // SUB)
    lens = after(lens, first)
    angles = (lens + step_of[:, None]) * inv_freq
    sign = jnp.where(jnp.arange(HD) < half, -1.0, 1.0).astype(F32)
    table = jnp.concatenate([jnp.cos(angles), jnp.sin(angles) * sign, lens], axis=1)

    got = [recv[j] for j in seq]
    got, acc, table = lax.optimization_barrier((got, acc, table))
    part = mid(got, down, down_other, n_tok, rank)
    bit = 2
    while bit < n_tp // 2:
        part = part + swap(part, n_tp, bit)
        bit *= 2
    sent = up(part, swap(part, n_tp, bit), got, up_rows, up_other, n_tok, rank)
    back = {j: cross(x, j) for j, x in zip(seq, sent)}
    late = {}
    for o in far:
        x = after(pieces[o], sent[0])
        late[o] = x
        late[o ^ 1] = swap(x, n_tp, 1)
    offsets = sorted(late)
    ready = after(perm, back[0])
    q, k, v = qkv([late[o] for o in offsets], ready, offsets, weights, acc)

    def attend(plan, loras, core_id, prev):
        return attention(
            plan, steps, core_id, rows, q, k, v, table, cache_key, cache_value, loras, prev
        )

    if n_grp == n_blocks:
        core_id = core.astype(I32).reshape(1)
        own = {j: after(back[j], q) for j in seq}
        other = {j: swap(own[j], n_tp, 1) for j in seq}
        plan = [(j, o) for j in seq for o in (False, True)]
        placed = [(seq.index(j), o) for j, o in plan]
        return attend(placed, [(other if o else own)[j] for j, o in plan], core_id, None)

    pairs = [(back[j], swap(back[j], n_tp, 1)) for j in seq]
    mine_all = jnp.stack([a[:n_tok] for a, _ in pairs])
    other_all = jnp.stack([a[n_tok:] for _, a in pairs])
    even = jnp.where(core == 0, mine_all, other_all)
    odd = jnp.where(core == 0, other_all, mine_all)
    full = jnp.stack([even, odd], axis=1).reshape(n_grp, n_tok, even.shape[2])
    span = jnp.arange(pool_slot.shape[0], dtype=I32)
    pos = jnp.sum(jnp.where(adapter_id[:, None] == span[None, :], pool_slot[None, :], 0), axis=1)
    key = lax.bitwise_xor(lax.div(pos, adp_rows), lax.axis_index("grp"))
    order = jnp.array([2 * j + c for j in seq for c in (0, 1)], I32)
    used = jnp.any(key[:, None] == order[None, :], axis=0)
    at = jnp.cumsum(used.astype(I32)) - 1
    pick = (at[None, :] == jnp.arange(n_blocks)[:, None]) & used[None, :]
    chosen = full[jnp.sum(jnp.where(pick, jnp.arange(n_grp)[None, :], 0), axis=1)]
    twice = jnp.concatenate([chosen, chosen], axis=1)
    plan = [(b // 2, b % 2 == 1) for b in range(n_blocks)]
    return attend(plan, [twice[b] for b in range(n_blocks)], jnp.zeros((1,), I32), None)


def solution(mesh):
    in_specs = (
        P("grp", None, "tp"),
        P("grp"),
        P(),
        P("grp"),
        P(None, "tp"),
        P(None, "tp"),
        P(None, "tp"),
        P("grp", "tp", None),
        P("grp", None, "tp"),
        P("grp", None, "tp"),
        P("grp", None, "tp"),
    )
    out_specs = P("grp", None, "tp")
    return jax.shard_map(body, mesh=mesh, in_specs=in_specs, out_specs=out_specs, check_vma=False)
```

```python
import functools
import math

import jax
import jax.numpy as jnp
from jax import lax
from jax.experimental import pallas as pl
from jax.experimental.pallas import tpu as pltpu
from jax.sharding import PartitionSpec as P

HD = 128
CAP = 8
SUB = 4
ROPE_BASE = 500000.0
NEG = -1e30
MIB = 1024 * 1024
F32 = jnp.float32
BF16 = jnp.bfloat16
I32 = jnp.int32
FIRST_STEPS = (256, 256)
STEP = 512
PARTS = 4
AHEAD = 6
TOGETHER = 2

TINY = pl.CostEstimate(flops=1, bytes_accessed=1, transcendentals=0)
QKV_COST = pl.CostEstimate(flops=10**11, bytes_accessed=3 * 10**8, transcendentals=0)
COST = pl.CostEstimate(flops=10**10, bytes_accessed=3 * 10**7, transcendentals=0)
VM = pl.BlockSpec(memory_space=pltpu.VMEM)
SM = pl.BlockSpec(memory_space=pltpu.SMEM)
HBM = pl.BlockSpec(memory_space=pltpu.HBM)


def params(mib):
    return pltpu.CompilerParams(vmem_limit_bytes=int(mib * MIB))


def dot(a, b):
    return jnp.dot(a, b, preferred_element_type=F32)


def dot_t(a, b):
    return lax.dot_general(a, b, (((1,), (1,)), ((), ())), preferred_element_type=F32)


def iota(shape, dim):
    return lax.broadcasted_iota(I32, shape, dim)


def one_hot(cond):
    return jnp.where(cond, 1.0, 0.0).astype(BF16)


def token_place(p, steps):
    n_sub = SUB * steps
    half = lax.rem(lax.div(p, n_sub), CAP // SUB)
    return half * SUB + lax.rem(p, SUB), lax.rem(lax.div(p, SUB), steps)


def route_kernel(adp_rows, seq, steps, ids_ref, lens_ref, slots_ref, *outs):
    perm_ref, send_ref, slot_ref, len_ref, row_ref = outs
    rows = ids_ref.shape[1]
    pool = slots_ref.shape[1]
    toks = rows * steps
    me = lax.axis_index("grp")
    core = lax.rem(lax.axis_index("tp"), 2)
    sub, lane = iota((rows, rows), 0), iota((rows, rows), 1)
    eye = sub == lane

    def to_col(row):
        return jnp.sum(jnp.where(eye, row, 0.0), axis=1, keepdims=True)

    def to_row(col):
        return jnp.sum(jnp.where(eye, col, 0.0), axis=0, keepdims=True)

    ids_col = to_col(ids_ref[...].astype(F32))
    lens_col = to_col(lens_ref[...].astype(F32))
    span = iota((rows, pool), 1).astype(F32)
    pos = jnp.sum(jnp.where(ids_col == span, slots_ref[...].astype(F32), 0.0), axis=1, keepdims=True)
    pos = pos.astype(I32)
    owner = lax.div(pos, adp_rows)
    slot = (pos - owner * adp_rows).astype(F32)
    key = lax.bitwise_xor(owner, me)
    pair = lax.div(key, 2)
    place = jnp.zeros_like(pair)
    for at, j in enumerate(seq):
        place = jnp.where(pair == j, at, place)
    place = (place * 2 + lax.rem(key, 2)).astype(F32)
    key = key.astype(F32)
    place_row = to_row(place)
    same = place_row == place
    before = same & (lane < sub)
    rank = jnp.sum(jnp.where(before, 1.0, 0.0), axis=1, keepdims=True)
    dest = jnp.sum(jnp.where((place_row < place) | before, 1.0, 0.0), axis=1, keepdims=True)
    dest_row, key_row, rank_row = to_row(dest), to_row(key), to_row(rank)

    def wide(col):
        return jnp.broadcast_to(col, (rows, 128)).astype(BF16)

    row_perm = one_hot(sub.astype(F32) == dest_row)
    ids = jnp.broadcast_to(lane[:1].astype(F32), (8, rows)).astype(BF16)
    row_ref[...] = dot_t(ids, row_perm)[:1].astype(I32)
    row_of, _ = token_place(iota((toks, rows), 0), steps)
    row_of = (row_of + lax.div(iota((toks, rows), 0), CAP * steps) * CAP).astype(F32)
    len_ref[...] = dot(one_hot(row_of == dest_row), wide(lens_col))
    n_pairs = len(seq)
    y = iota((n_pairs * 2 * CAP, rows), 0)
    y_key = (lax.div(y, 2 * CAP) * 2 + core).astype(F32)
    y_rank = (lax.rem(lax.div(y, CAP), 2) * SUB + lax.rem(y, SUB)).astype(F32)
    slot_ref[...] = dot(one_hot((y_key == key_row) & (y_rank == rank_row)), wide(slot)).astype(BF16)

    spread = one_hot(lax.div(iota((rows, toks), 1), steps) == iota((rows, toks), 0))
    info = jnp.concatenate([dest_row, key_row, rank_row] + [dest_row] * 5, axis=0).astype(BF16)
    info = dot(info, spread)
    dest_tok, key_tok, rank_tok = info[0:1], info[1:2], info[2:3]
    p, step_tok = iota((toks, toks), 0), lax.rem(iota((toks, toks), 1), steps)
    p_row, p_step = token_place(p, steps)
    p_row = (p_row + lax.div(p, CAP * steps) * CAP).astype(F32)
    perm = one_hot((p_row == dest_tok) & (p_step == step_tok))
    perm_ref[...] = perm
    n_send = n_pairs * CAP * steps
    p, step_tok = iota((n_send, toks), 0), lax.rem(iota((n_send, toks), 1), steps)
    p_row, p_step = token_place(p, steps)
    p_key = (lax.div(p, CAP * steps) * 2 + core).astype(F32)
    send_ref[...] = one_hot((p_key == key_tok) & (p_row.astype(F32) == rank_tok) & (p_step == step_tok))


def route(adp_rows, seq, steps, adapter_id, lengths, pool_slot):
    rows = adapter_id.shape[0]
    toks = rows * steps
    out = [
        jax.ShapeDtypeStruct((toks, toks), BF16),
        jax.ShapeDtypeStruct((len(seq) * CAP * steps, toks), BF16),
        jax.ShapeDtypeStruct((len(seq) * 2 * CAP, 128), BF16),
        jax.ShapeDtypeStruct((toks, 128), F32),
        jax.ShapeDtypeStruct((1, rows), I32),
    ]
    return pl.pallas_call(
        functools.partial(route_kernel, adp_rows, seq, steps),
        out_shape=out,
        in_specs=[VM] * 3,
        out_specs=[VM] * len(out),
        compiler_params=params(62),
        name="route",
    )(adapter_id[None, :], lengths[None, :], pool_slot[None, :])


def pack_kernel(n_tok, send_ref, slot_ref, tok_ref, oth_ref, *sends):
    rows, steps, width = tok_ref.shape
    for j in range(0, width, 512):
        for half, ref in enumerate((tok_ref, oth_ref)):
            part = ref[:, :, j : j + 512].reshape(rows * steps, 512)
            got = dot(send_ref[...], part).astype(BF16)
            for k, out in enumerate(sends):
                for c in range(4):
                    at = ((j // 128 + c) * 2 + half) * n_tok
                    out[at : at + n_tok, :] = got[k * n_tok : (k + 1) * n_tok, c * 128 : (c + 1) * 128]
    for k, out in enumerate(sends):
        out[width // 128 * 2 * n_tok :, :] = slot_ref[k * 2 * CAP : (k + 1) * 2 * CAP, :]


def pack(n_pairs, send, slot, tokens, other):
    _, steps, width = tokens.shape
    n_tok = steps * CAP
    out = [jax.ShapeDtypeStruct((width // 128 * 2 * n_tok + 2 * CAP, 128), BF16)] * n_pairs
    return pl.pallas_call(
        functools.partial(pack_kernel, n_tok),
        out_shape=out,
        in_specs=[VM] * 4,
        out_specs=[VM] * len(out),
        compiler_params=params(62),
        name="pack",
    )(send, slot, tokens, other)


def qkv_kernel(offsets, has_acc, steps, perm_ref, *refs):
    n_x = len(offsets)
    me = lax.axis_index("tp")
    xs, ws = refs[:n_x], refs[n_x : n_x + 3]
    at = n_x + 3
    accs = refs[at : at + 3] if has_acc else (None,) * 3
    at += 3 if has_acc else 0
    outs, raw, xbuf = refs[at : at + 3], refs[at + 3], refs[at + 4]
    bufs, xsem, wsem = refs[at + 5 : at + 8], refs[at + 8], refs[at + 9]
    rows, n_steps, width = xs[0].shape

    def x_copy(p):
        return pltpu.make_async_copy(xs[p], raw.at[p], xsem.at[p])

    def w_copy(n, i):
        lo, size = steps[n]
        shard = lax.bitwise_xor(me, offsets[lo // width])
        row = pl.multiple_of(shard * width + lo % width, 256)
        return pltpu.make_async_copy(ws[i].at[pl.ds(row, size)], bufs[i].at[lo : lo + size], wsem.at[n, i])

    def begin(n):
        if n < len(steps):
            if steps[n][0] % width == 0:
                x_copy(steps[n][0] // width).start()
            for i in range(3):
                w_copy(n, i).start()

    begin(0)
    begin(1)
    for n, (lo, size) in enumerate(steps):
        begin(n + 2)
        if lo % width == 0:
            p = lo // width
            x_copy(p).wait()
            for j in range(0, width, 512):
                part = raw[p, :, :, j : j + 512].reshape(rows * n_steps, 512)
                xbuf[:, lo + j : lo + j + 512] = dot(perm_ref[...], part).astype(BF16)
        for i in range(3):
            w_copy(n, i).wait()
        x = xbuf[:, lo : lo + size]
        for i in range(3):
            got = dot(x, bufs[i][lo : lo + size, :])
            if lo:
                outs[i][...] += got
            else:
                outs[i][...] = accs[i][...] + got if has_acc else got


def qkv(xs, perm, offsets, weights, acc):
    rows, steps, width = xs[0].shape
    m = rows * steps
    n_x = len(xs)
    has_acc = acc is not None
    outs = [jax.ShapeDtypeStruct((m, w.shape[1]), F32) for w in weights]
    cols = sum(w.shape[1] for w in weights)
    extra = list(acc) if has_acc else []
    depth = n_x * width
    plan, at = [], 0
    for size in FIRST_STEPS:
        plan.append((at, size))
        at += size
    while at < depth:
        plan.append((at, min(STEP, width - at % width)))
        at += plan[-1][1]
    return pl.pallas_call(
        functools.partial(qkv_kernel, tuple(offsets), has_acc, plan),
        out_shape=outs,
        in_specs=[VM] + [HBM] * (n_x + 3) + [VM] * len(extra),
        out_specs=[VM] * 3,
        scratch_shapes=[pltpu.VMEM((n_x, rows, steps, width), BF16), pltpu.VMEM((m, depth), BF16)]
        + [pltpu.VMEM((depth, w.shape[1]), BF16) for w in weights]
        + [pltpu.SemaphoreType.DMA((n_x,)), pltpu.SemaphoreType.DMA((len(plan), 3))],
        compiler_params=params(60.5),
        cost_estimate=QKV_COST,
        name="qkv",
    )(perm, *xs, *weights, *extra)


def panel_loads(srcs, dst, sem):
    size = dst.shape[1] // PARTS
    loads = []
    for i, src in enumerate(srcs):
        at = [pl.ds(p * size, size) for p in range(PARTS)]
        loads.append([pltpu.make_async_copy(src.at[a], dst.at[i, a], sem.at[i, p]) for p, a in enumerate(at)])
        for c in loads[-1]:
            c.start()
    return loads


def slot_mask(tiles, n_tok, cols, rank):
    tiles = tiles.astype(F32)
    rep = n_tok // (2 * CAP)
    slots = jnp.concatenate([tiles[:CAP]] * rep + [tiles[CAP:]] * rep, axis=0)
    slots = jnp.concatenate([slots] * (cols // 128), axis=1)
    return slots == lax.div(iota((n_tok, cols), 1), rank).astype(F32)


def mid_kernel(n_tok, rank, down_ref, oth_ref, *refs):
    ins, out_ref, x_ref, d_ref, sem = refs[:-4], refs[-4], refs[-3], refs[-2], refs[-1]
    _, cols, width = d_ref.shape
    loads = panel_loads((down_ref, oth_ref), d_ref, sem)
    for k, r in enumerate(ins):
        rows = slice(k * n_tok, (k + 1) * n_tok)
        for c in range(width // 128):
            for half in range(2):
                at = (c * 2 + half) * n_tok
                x_ref[half, rows, c * 128 : (c + 1) * 128] = r[at : at + n_tok, :]
    prod = 0.0
    for half in range(2):
        for c in loads[half]:
            c.wait()
        prod = prod + dot_t(d_ref[half], x_ref[half])
    prod = jnp.transpose(prod)
    for k, r in enumerate(ins):
        mask = slot_mask(r[r.shape[0] - 2 * CAP :, :], n_tok, cols, rank)
        part = jnp.where(mask, prod[k * n_tok : (k + 1) * n_tok], 0.0)
        tot = part[:, :128]
        for c in range(128, cols, 128):
            tot = tot + part[:, c : c + 128]
        out_ref[k * n_tok : (k + 1) * n_tok, :] = tot + pltpu.roll(tot, rank, 1)


def mid(recv, down, other, n_tok, rank):
    n = len(recv)
    cols, width = down.shape
    return pl.pallas_call(
        functools.partial(mid_kernel, n_tok, rank),
        out_shape=jax.ShapeDtypeStruct((n * n_tok, 128), F32),
        in_specs=[HBM] * 2 + [VM] * n,
        out_specs=VM,
        scratch_shapes=[
            pltpu.VMEM((2, n * n_tok, width), BF16),
            pltpu.VMEM((2, cols, width), BF16),
            pltpu.SemaphoreType.DMA((2, PARTS)),
        ],
        compiler_params=params(24),
        cost_estimate=COST,
        name="mid",
    )(down, other, *recv)


def up_kernel(n_tok, rank, n_recv, up_ref, oth_ref, a_ref, b_ref, *refs):
    ins, outs, u_ref, sem = refs[:n_recv], refs[n_recv : 2 * n_recv], refs[-2], refs[-1]
    _, cols, width = u_ref.shape
    loads = panel_loads((up_ref, oth_ref), u_ref, sem)
    total = (a_ref[...] + b_ref[...]).astype(BF16).astype(F32)
    spread = []
    for k in range(n_recv):
        both = jnp.concatenate([total[k * n_tok : (k + 1) * n_tok]] * (cols // 128), axis=1)
        mask = slot_mask(ins[k][...], n_tok, cols, rank)
        spread.append(jnp.where(mask, both, 0.0).astype(BF16))
    rows = jnp.concatenate(spread, axis=0)
    for half in range(2):
        for c in loads[half]:
            c.wait()
        for j in range(0, width, 512):
            got = dot(rows, u_ref[half, :, j : j + 512]).astype(BF16)
            for k in range(n_recv):
                outs[k][half * n_tok : (half + 1) * n_tok, j : j + 512] = got[k * n_tok : (k + 1) * n_tok]


def up(a, b, recv, up_rows, other, n_tok, rank):
    n = len(recv)
    cols, width = up_rows.shape
    last = recv[0].shape[0] // (2 * CAP) - 1
    tail = pl.BlockSpec((2 * CAP, 128), lambda i: (last, 0))

    def whole(x):
        return pl.BlockSpec(x.shape, lambda i: (0, 0))

    out = jax.ShapeDtypeStruct((2 * n_tok, width), BF16)
    return pl.pallas_call(
        functools.partial(up_kernel, n_tok, rank, n),
        out_shape=[out] * n,
        grid=(1,),
        in_specs=[HBM] * 2 + [whole(a), whole(b)] + [tail] * n,
        out_specs=[whole(out)] * n,
        scratch_shapes=[pltpu.VMEM((2, cols, width), BF16), pltpu.SemaphoreType.DMA((2, PARTS))],
        compiler_params=params(20),
        cost_estimate=COST,
        name="up",
    )(up_rows, other, a, b, *recv)


def make_attn_kernel(plan, steps, group, has_prev):
    nb = len(plan)
    halves = CAP // SUB
    n_tok = steps * CAP
    n_sub = steps * SUB
    n_q = group * n_sub

    def kernel(*refs):
        core_ref, rows_ref, q_hbm, k_hbm, v_hbm, tab_hbm, ck_ref, cv_ref = refs[:8]
        lora_refs = refs[8 : 8 + nb]
        at = 8 + nb + int(has_prev)
        out_ref, kbuf, vbuf, obuf, q_ref, k_ref, v_ref, tab_ref, loras, sem, osem = refs[at:]
        kv_local = k_ref.shape[1] // HD
        span = ck_ref.shape[1]
        scale = 1.0 / math.sqrt(HD)
        core = core_ref[0]
        blocks = [2 * j + (1 - core if other else core) for j, other in plan]

        def copies(b):
            at, to = pl.ds(pl.multiple_of(blocks[b] * n_tok, n_tok), n_tok), pl.ds(b * n_tok, n_tok)
            got = [
                pltpu.make_async_copy(src.at[at], dst.at[to], sem.at[b, n])
                for n, (src, dst) in enumerate(
                    ((q_hbm, q_ref), (k_hbm, k_ref), (v_hbm, v_ref), (tab_hbm, tab_ref))
                )
            ]
            part = pl.ds(n_tok if plan[b][1] else 0, n_tok)
            got.append(pltpu.make_async_copy(lora_refs[b].at[part], loras.at[b], sem.at[b, 4]))
            return got

        def begin(b):
            for i in range(CAP):
                r = rows_ref[0, blocks[b] * CAP + i]
                pltpu.make_async_copy(ck_ref.at[r], kbuf.at[b, i], sem.at[b, 5]).start()
                pltpu.make_async_copy(cv_ref.at[r], vbuf.at[b, i], sem.at[b, 6]).start()
            for c in copies(b):
                c.start()

        for b in range(min(AHEAD, nb)):
            begin(b)

        qi, ki = iota((n_sub, n_sub), 0), iota((n_sub, n_sub), 1)
        new_ok = (lax.rem(qi, SUB) == lax.rem(ki, SUB)) & (lax.div(qi, SUB) >= lax.div(ki, SUB))
        new_bias = jnp.concatenate([jnp.where(new_ok, 0.0, NEG)] * group, axis=0)
        col, sub = iota((CAP, SUB * span), 1), iota((CAP, SUB * span), 0)
        own = lax.div(col, span) == lax.rem(sub, SUB)
        at_pos = lax.rem(col, span).astype(F32)
        y, x = iota((n_tok, n_tok), 0), iota((n_tok, n_tok), 1)
        x_row, x_step = token_place(x, steps)
        turn = one_hot((lax.div(y, steps) == x_row) & (lax.rem(y, steps) == x_step))

        wide = group * HD
        for start in range(0, nb, TOGETHER):
            these = range(start, min(start + TOGETHER, nb))
            for b in these:
                if b + AHEAD < nb:
                    begin(b + AHEAD)
            for b in these:
                for c in copies(b):
                    c.wait()
                pltpu.make_async_copy(ck_ref.at[pl.ds(0, CAP)], kbuf.at[b], sem.at[b, 5]).wait()
                pltpu.make_async_copy(cv_ref.at[pl.ds(0, CAP)], vbuf.at[b], sem.at[b, 6]).wait()
            work = [(b, h, t) for b in these for h in range(kv_local) for t in range(halves)]
            biases, qs, kns, vns = {}, {}, {}, {}
            for b in these:
                rows = slice(b * n_tok, (b + 1) * n_tok)
                cos, sin = tab_ref[rows, :HD], tab_ref[rows, HD : 2 * HD]

                def rope(v):
                    return v * cos + pltpu.roll(v, HD // 2, 1) * sin

                for t in range(halves):
                    at = b * n_tok + t * n_sub
                    lens = tab_ref[at : at + CAP, 2 * HD :][:, :1]
                    bias = jnp.where(own & (at_pos < lens), 0.0, NEG)
                    biases[b, t] = jnp.concatenate([bias] * (n_q // CAP), axis=0)
                for h in range(kv_local):
                    hs = slice(h * HD, (h + 1) * HD)
                    heads = []
                    for g in range(group):
                        cs = slice((h * group + g) * HD, (h * group + g + 1) * HD)
                        heads.append(rope(q_ref[rows, cs] + loras[b, :, cs].astype(F32)).astype(BF16))
                    kn = rope(k_ref[rows, hs]).astype(BF16)
                    vn = v_ref[rows, hs].astype(BF16)
                    for t in range(halves):
                        ts = slice(t * n_sub, (t + 1) * n_sub)
                        qs[b, h, t] = jnp.concatenate([v[ts] for v in heads], axis=0)
                        kns[b, h, t], vns[b, h, t] = kn[ts], vn[ts]
            s1, s2 = {}, {}
            for w in work:
                b, h, t = w
                kc = kbuf[b, t * SUB : (t + 1) * SUB, :, h * HD : (h + 1) * HD].reshape(SUB * span, HD)
                s1[w] = dot_t(qs[w], kc) * scale + biases[b, t]
                s2[w] = dot_t(qs[w], kns[w]) * scale + new_bias
            p1, p2 = {}, {}
            for w in work:
                top = jnp.maximum(jnp.max(s1[w], axis=1, keepdims=True), jnp.max(s2[w], axis=1, keepdims=True))
                e1 = jnp.exp(s1[w] - top)
                e2 = jnp.exp(s2[w] - top)
                den = jnp.sum(e1, axis=1, keepdims=True) + jnp.sum(e2, axis=1, keepdims=True)
                inv = 1.0 / den
                p1[w], p2[w] = (e1 * inv).astype(BF16), (e2 * inv).astype(BF16)
            parts = {}
            for w in work:
                b, h, t = w
                vc = vbuf[b, t * SUB : (t + 1) * SUB, :, h * HD : (h + 1) * HD].reshape(SUB * span, HD)
                o = dot(p1[w], vc) + dot(p2[w], vns[w])
                o = o.astype(BF16)
                parts[w] = jnp.concatenate([o[g * n_sub : (g + 1) * n_sub] for g in range(group)], axis=1)
            for b in these:
                for h in range(kv_local):
                    both = jnp.concatenate([parts[b, h, t] for t in range(halves)], axis=0)
                    mixed = dot(turn, both).astype(BF16)
                    obuf[b, :, :, h * wide : (h + 1) * wide] = mixed.reshape(CAP, steps, wide)
                for i in range(CAP):
                    r = rows_ref[0, blocks[b] * CAP + i]
                    pltpu.make_async_copy(obuf.at[b, i], out_ref.at[r], osem).start()
        for b in range(nb):
            pltpu.make_async_copy(obuf.at[b], out_ref.at[pl.ds(0, CAP)], osem).wait()

    return kernel


def attention(plan, steps, core, rows, q, k, v, table, ck, cv, loras, prev):
    n_rows = ck.shape[0]
    nb = len(plan)
    n = nb * CAP * steps
    group = q.shape[1] // k.shape[1]
    buf = (nb, CAP) + ck.shape[1:]
    extra = [] if prev is None else [prev]
    return pl.pallas_call(
        make_attn_kernel(plan, steps, group, bool(extra)),
        out_shape=jax.ShapeDtypeStruct((n_rows, steps, q.shape[1]), BF16),
        in_specs=[SM, SM] + [HBM] * (6 + nb + len(extra)),
        out_specs=HBM,
        scratch_shapes=[
            pltpu.VMEM(buf, BF16),
            pltpu.VMEM(buf, BF16),
            pltpu.VMEM((nb, CAP, steps, q.shape[1]), BF16),
            pltpu.VMEM((n, q.shape[1]), F32),
            pltpu.VMEM((n, k.shape[1]), F32),
            pltpu.VMEM((n, v.shape[1]), F32),
            pltpu.VMEM((n, table.shape[1]), F32),
            pltpu.VMEM((nb, CAP * steps, q.shape[1]), BF16),
            pltpu.SemaphoreType.DMA((nb, 7)),
            pltpu.SemaphoreType.DMA,
        ],
        input_output_aliases={8 + nb: 0} if extra else {},
        compiler_params=params(62),
        cost_estimate=TINY,
        name="attn",
    )(core, rows, q, k, v, table, ck, cv, *loras, *extra)


def swap(x, n, bit):
    return lax.ppermute(x, "tp", [(i, i ^ bit) for i in range(n)])


def after(x, *deps):
    return lax.optimization_barrier((x, *deps))[0]


def body(
    tokens,
    adapter_id,
    pool_slot,
    lengths,
    w_query,
    w_key,
    w_value,
    pooled_down_weights,
    pool_up,
    cache_key,
    cache_value,
):
    n_grp = lax.axis_size("grp")
    n_tp = lax.axis_size("tp")
    row_count, steps, width = tokens.shape
    adp_rows, _, rank = pooled_down_weights.shape
    n_tok = steps * CAP
    n_blocks = row_count // CAP
    n_pairs = n_grp // 2
    seq = [*range(n_pairs // 2, n_pairs), *reversed(range(n_pairs // 2))]
    me = lax.axis_index("tp")
    core = lax.rem(me, 2)

    def cross(x, j):
        perm = [
            (g * n_tp + t, (g ^ (2 * j + t % 2)) * n_tp + t)
            for g in range(n_grp)
            for t in range(n_tp)
        ]
        return lax.ppermute(x, ("grp", "tp"), perm)

    other_tokens = swap(tokens, n_tp, 1)
    perm, send, slot, lens, rows = route(adp_rows, seq, steps, adapter_id, lengths, pool_slot)
    sends = pack(n_pairs, send, slot, tokens, other_tokens)
    recv = {j: cross(sends[j], j) for j in seq}

    first = recv[0]
    up_rows = after(pool_up, sends[0]).reshape(adp_rows * rank, pool_up.shape[2])
    up_other = swap(up_rows, n_tp, 1)
    down = jnp.swapaxes(after(pooled_down_weights, sends[0]), 1, 2).reshape(adp_rows * rank, width)
    down_other = swap(down, n_tp, 1)

    weights = (w_query, w_key, w_value)

    ready = after(perm, up_other, down_other)
    acc = qkv([tokens, other_tokens], ready, [0, 1], weights, None)
    pieces = {0: after(tokens, sends[0])}
    bit = n_tp // 2
    while bit > 1:
        pieces.update({off ^ bit: swap(p, n_tp, bit) for off, p in list(pieces.items())})
        bit //= 2
    far = [o for o in sorted(pieces) if o]

    half = HD // 2
    inv_freq = jnp.exp(jnp.arange(half, dtype=F32) * (-2.0 * math.log(ROPE_BASE) / HD))
    inv_freq = jnp.concatenate([inv_freq, inv_freq])
    step_of = jnp.tile(jnp.repeat(jnp.arange(steps, dtype=F32), SUB), row_count // SUB)
    lens = after(lens, first)
    angles = (lens + step_of[:, None]) * inv_freq
    sign = jnp.where(jnp.arange(HD) < half, -1.0, 1.0).astype(F32)
    table = jnp.concatenate([jnp.cos(angles), jnp.sin(angles) * sign, lens], axis=1)

    got = [recv[j] for j in seq]
    got, acc, table = lax.optimization_barrier((got, acc, table))
    part = mid(got, down, down_other, n_tok, rank)
    bit = 2
    while bit < n_tp // 2:
        part = part + swap(part, n_tp, bit)
        bit *= 2
    sent = up(part, swap(part, n_tp, bit), got, up_rows, up_other, n_tok, rank)
    back = {j: cross(x, j) for j, x in zip(seq, sent)}
    late = {}
    for o in far:
        x = after(pieces[o], sent[0])
        late[o] = x
        late[o ^ 1] = swap(x, n_tp, 1)
    offsets = sorted(late)
    ready = after(perm, back[0])
    q, k, v = qkv([late[o] for o in offsets], ready, offsets, weights, acc)

    def attend(plan, loras, core_id, prev):
        return attention(
            plan, steps, core_id, rows, q, k, v, table, cache_key, cache_value, loras, prev
        )

    if n_grp == n_blocks:
        core_id = core.astype(I32).reshape(1)
        own = {j: after(back[j], q) for j in seq}
        other = {j: swap(own[j], n_tp, 1) for j in seq}
        plan = [(j, o) for j in seq for o in (False, True)]
        placed = [(seq.index(j), o) for j, o in plan]
        return attend(placed, [(other if o else own)[j] for j, o in plan], core_id, None)

    pairs = [(back[j], swap(back[j], n_tp, 1)) for j in seq]
    mine_all = jnp.stack([a[:n_tok] for a, _ in pairs])
    other_all = jnp.stack([a[n_tok:] for _, a in pairs])
    even = jnp.where(core == 0, mine_all, other_all)
    odd = jnp.where(core == 0, other_all, mine_all)
    full = jnp.stack([even, odd], axis=1).reshape(n_grp, n_tok, even.shape[2])
    span = jnp.arange(pool_slot.shape[0], dtype=I32)
    pos = jnp.sum(jnp.where(adapter_id[:, None] == span[None, :], pool_slot[None, :], 0), axis=1)
    key = lax.bitwise_xor(lax.div(pos, adp_rows), lax.axis_index("grp"))
    order = jnp.array([2 * j + c for j in seq for c in (0, 1)], I32)
    used = jnp.any(key[:, None] == order[None, :], axis=0)
    at = jnp.cumsum(used.astype(I32)) - 1
    pick = (at[None, :] == jnp.arange(n_blocks)[:, None]) & used[None, :]
    chosen = full[jnp.sum(jnp.where(pick, jnp.arange(n_grp)[None, :], 0), axis=1)]
    twice = jnp.concatenate([chosen, chosen], axis=1)
    plan = [(b // 2, b % 2 == 1) for b in range(n_blocks)]
    return attend(plan, [twice[b] for b in range(n_blocks)], jnp.zeros((1,), I32), None)


def solution(mesh):
    in_specs = (
        P("grp", None, "tp"),
        P("grp"),
        P(),
        P("grp"),
        P(None, "tp"),
        P(None, "tp"),
        P(None, "tp"),
        P("grp", "tp", None),
        P("grp", None, "tp"),
        P("grp", None, "tp"),
        P("grp", None, "tp"),
    )
    out_specs = P("grp", None, "tp")
    return jax.shard_map(body, mesh=mesh, in_specs=in_specs, out_specs=out_specs, check_vma=False)
```
